128 devices in a mesh: slab: 32 (over z, y, core), col: 4 (over x).
Axes of the slice: x: 4, y: 4, z: 4, core: 2. Of those that a mesh axis runs over, the one named last changes fastest.
Arguments:
- cell_rhs: float32 [3, 128, 64, 8, 256], P(None, None, 'slab', 'col'), may hold values from -6 to 6
- well_rhs: float32 [256, 3, 128], P(('slab', 'col')), may hold values from -6 to 6
- cell_colors: int32 [64, 8, 256], P('slab', 'col'), may hold values from 0 to 3, as said below
- incoming: float32 [6, 3, 3, 64, 8, 256], P(None, None, None, 'slab', 'col'), may hold values from -1.2 to 1.2
- pivot_inv: float32 [3, 3, 64, 8, 256], P(None, None, 'slab', 'col'), may hold values from -1 to 2
- perf_cell: int32 [8192], P(('slab', 'col')), may hold values from 0 to 1023
- perf_well: int32 [8192], P(('slab', 'col')), may hold values from 0 to 255
- perf_out: float32 [8192, 3, 3], P(('slab', 'col')), may hold values from -0.6 to 0.6
- perf_in: float32 [8192, 3, 3], P(('slab', 'col')), may hold values from -1.2 to 1.2
- well_pivot_inv: float32 [256, 3, 3], P(('slab', 'col')), may hold values from -1 to 2
Outputs:
- cell_adjoint: float32 [3, 128, 64, 8, 256], P(None, None, 'slab', 'col')
- well_adjoint: float32 [256, 3, 128], P(('slab', 'col'))
The draws below stay inside these ranges and needn't reach their ends.
Inputs may be any that keep to these rules, and one draw needn't show every extreme that they name: `cell_colors`: the parity of a cell's color equals the parity of its x + y + z. `perf_cell`: index of the cell within the 2 x 2 x 256 block of the device that holds the perforation. `perf_well`: well w is owned by the device holding entry w of the well arrays.
All inputs are finite; a program needn't handle non-finite values.
Results may differ from the reference program's by a relative error of at most 0.00011.
Values sent between devices are 32-bit elements; how exact they have to be, the bound alone decides.
No kernel may reach another device: no remote copies, remote signals or barrier semaphores. Data moves between devices by JAX's collectives and lax.ppermute only.
A program may use at most 128 MiB of HBM per device.

```python
import math
import jax
import jax.numpy as jnp
import numpy as np
from jax import lax

RHS = 128
CX = 2
CY = 2
CZ = 256
PERF_DEV = 64
NX = 64
NY = 8
NZ = 256
PERFS = 8192
WELLS = 256
N_COL = 4


def combine_blocks(diagonal, spread, shape_full, first_dim):
    identity = (lax.broadcasted_iota(jnp.int32, shape_full, first_dim) == lax.broadcasted_iota(jnp.int32, shape_full, first_dim + 1)).astype(jnp.float32)
    return identity * diagonal + (1.0 - identity) * spread


def draw_cell_colors(key, part):
    key = jax.random.fold_in(key, 11)
    shape_grid = (NX, NY, NZ)
    parity = (lax.broadcasted_iota(jnp.int32, shape_grid, 0) + lax.broadcasted_iota(jnp.int32, shape_grid, 1) + lax.broadcasted_iota(jnp.int32, shape_grid, 2)) % 2
    return parity + 2 * jax.random.randint(key, shape_grid, 0, 2, dtype=jnp.int32)


def draw_pivot_inv(key, part):
    key = jax.random.fold_in(key, 23)
    first_key, second_key = jax.random.split(key)
    shape_full = (3, 3, NX, NY, NZ)
    diagonal = jnp.exp(jax.random.uniform(first_key, shape_full, jnp.float32, math.log(0.5), math.log(2.0)))
    spread = jnp.clip(0.25 * jax.random.normal(second_key, shape_full, jnp.float32), -1.0, 1.0)
    return combine_blocks(diagonal, spread, shape_full, 0)


def draw_well_pivot_inv(key, part):
    key = jax.random.fold_in(key, 37)
    first_key, second_key = jax.random.split(key)
    shape_full = (WELLS, 3, 3)
    diagonal = jnp.exp(jax.random.uniform(first_key, shape_full, jnp.float32, math.log(0.5), math.log(2.0)))
    spread = jnp.clip(0.25 * jax.random.normal(second_key, shape_full, jnp.float32), -1.0, 1.0)
    return combine_blocks(diagonal, spread, shape_full, 1)


def place_ends(drawn, key, low, largest):
    spot = [jax.random.randint(jax.random.fold_in(key, axis), (), 0, length) for axis, length in enumerate(drawn.shape)]
    widest = drawn.shape.index(max(drawn.shape))
    beside = spot[:widest] + [(spot[widest] + 1) % drawn.shape[widest]] + spot[widest + 1:]
    return drawn.at[tuple(spot)].set(low).at[tuple(beside)].set(largest)


def steps_of(rng, shape, pieces, smallest, top_value):
    loudness, own = 1.0, jax.random.fold_in(rng, 6)
    for axis_at, blocks in pieces:
        heights = jnp.exp(jax.random.uniform(jax.random.fold_in(own, axis_at), (blocks,), jnp.float32, smallest / len(pieces), top_value / len(pieces)))
        loudness = loudness * jnp.repeat(heights, shape[axis_at] // blocks).reshape([-1 if axis == axis_at else 1 for axis in range(len(shape))])
    return loudness


def cumulative_ranks(amount, lean):
    loads = [(1 << 20) // math.isqrt(grade ** lean) + 1 for grade in range(1, amount + 1)]
    scale = 1 + sum(loads) // (1 << 30)
    return np.cumsum(np.array([max(1, weight // scale) for weight in loads]))


def ranked(rng, extent, number_of, slope):
    listing = cumulative_ranks(number_of, slope)
    ticket = jax.random.randint(jax.random.fold_in(rng, 1), extent, 0, int(listing[number_of - 1]))
    standing = jnp.searchsorted(jnp.asarray(listing, jnp.int32), ticket, side="right")
    return jax.random.permutation(jax.random.fold_in(rng, 2), number_of)[standing].astype(jnp.int32)


def noise(key, extent, scale, limit, pieces=(), kind=jnp.bfloat16):
    level = steps_of(key, extent, pieces, -0.22, 0.18) if pieces else 1.0
    array = jax.random.normal(key, extent, jnp.float32) * scale * level
    return jnp.minimum(jnp.maximum(array, -limit), limit).astype(kind)


def setup_inputs(seed: int = 0) -> dict:
    keys = jax.random.split(jax.random.key(seed), 11)
    cell_rhs = noise(keys[0], (3, RHS, NX, NY, NZ), 1.0, 6.0, ((2, 32), (3, 4)), jnp.float32)
    well_rhs = noise(keys[1], (WELLS, 3, RHS), 1.0, 6.0, ((0, 128),), jnp.float32)
    cell_colors = draw_cell_colors(jax.random.fold_in(keys[10], 71), 0)
    incoming = noise(keys[3], (6, 3, 3, NX, NY, NZ), 0.2, 1.2, ((3, 32), (4, 4)), jnp.float32)
    pivot_inv = draw_pivot_inv(jax.random.fold_in(keys[10], 71), 0)
    perf_cell = place_ends(jax.random.randint(keys[5], (PERFS,), 0, CX * CY * CZ), jax.random.fold_in(keys[5], 1), 0, (CX * CY * CZ) - 1).astype(jnp.int32)
    perf_well = place_ends(ranked(keys[6], (PERFS,), WELLS, 1), jax.random.fold_in(keys[6], 3), 0, WELLS - 1).astype(jnp.int32)
    perf_out = noise(keys[7], (PERFS, 3, 3), 0.1, 0.6, ((0, 128),), jnp.float32)
    perf_in = noise(keys[8], (PERFS, 3, 3), 0.2, 1.2, ((0, 128),), jnp.float32)
    well_pivot_inv = draw_well_pivot_inv(jax.random.fold_in(keys[10], 71), 0)
    return dict(cell_rhs=cell_rhs, well_rhs=well_rhs, cell_colors=cell_colors, incoming=incoming, pivot_inv=pivot_inv, perf_cell=perf_cell, perf_well=perf_well, perf_out=perf_out, perf_in=perf_in, well_pivot_inv=well_pivot_inv)


def apply_blocks(blocks, vector):
    return blocks[0][:, None] * vector[0][None] + blocks[1][:, None] * vector[1][None] + blocks[2][:, None] * vector[2][None]


def well_apply(blocks, vector):
    return blocks[:, 0, :, None] * vector[:, 0, None, :] + blocks[:, 1, :, None] * vector[:, 1, None, :] + blocks[:, 2, :, None] * vector[:, 2, None, :]


def z_lower(values):
    widths = [(0, 0)] * (values.ndim - 1) + [(1, 0)]
    return jnp.pad(values, widths)[..., :-1]


def z_upper(values):
    widths = [(0, 0)] * (values.ndim - 1) + [(0, 1)]
    return jnp.pad(values, widths)[..., 1:]


def face_sum(incoming, padded):
    size_x = padded.shape[2] - 2
    size_y = padded.shape[3] - 2
    center = padded[:, :, 1:size_x + 1, 1:size_y + 1]
    summed = apply_blocks(incoming[0], padded[:, :, 0:size_x, 1:size_y + 1])
    summed = summed + apply_blocks(incoming[1], padded[:, :, 2:size_x + 2, 1:size_y + 1])
    summed = summed + apply_blocks(incoming[2], padded[:, :, 1:size_x + 1, 0:size_y])
    summed = summed + apply_blocks(incoming[3], padded[:, :, 1:size_x + 1, 2:size_y + 2])
    summed = summed + apply_blocks(incoming[4], z_lower(center))
    summed = summed + apply_blocks(incoming[5], z_upper(center))
    return summed


def grid_sum(incoming, values):
    padded = jnp.pad(values, ((0, 0), (0, 0), (1, 1), (1, 1), (0, 0)))
    return face_sum(incoming, padded)


def reference(cell_rhs, well_rhs, cell_colors, incoming, pivot_inv, perf_cell, perf_well, perf_out, perf_in, well_pivot_inv):
    perf_total = perf_cell.shape[0]
    device = jnp.arange(perf_total, dtype=jnp.int32) // PERF_DEV
    slab_index = device // N_COL
    col_index = device % N_COL
    local_x = perf_cell // (CY * CZ)
    local_y = (perf_cell // CZ) % CY
    local_z = perf_cell % CZ
    global_cell = (((slab_index * CX + local_x) * NY + col_index * CY + local_y) * NZ + local_z).astype(jnp.int32)
    block_cols = 16
    rhs_blocks = cell_rhs.reshape(3, RHS // block_cols, block_cols, NX, NY, NZ).transpose(1, 0, 2, 3, 4, 5)
    well_blocks = well_rhs.reshape(WELLS, 3, RHS // block_cols, block_cols).transpose(2, 0, 1, 3)

    def solve(operands):
        rhs_part, well_part = operands
        forward = jnp.zeros_like(rhs_part)
        for color_index in range(4):
            if color_index == 0:
                source = rhs_part
            else:
                source = rhs_part - grid_sum(incoming, forward)
            forward = jnp.where((cell_colors == color_index)[None, None], apply_blocks(pivot_inv, source), forward)
        column_count = rhs_part.shape[1]
        flat_cells = forward.reshape(3, column_count, NX * NY * NZ)
        at_perfs = jnp.transpose(flat_cells[:, :, global_cell], (2, 0, 1))
        partial_value = well_apply(perf_out, at_perfs)
        summed_wells = jax.ops.segment_sum(partial_value, perf_well, num_segments=WELLS)
        well_adjoint = well_apply(well_pivot_inv, well_part - summed_wells)
        perf_fixes = well_apply(perf_in, well_adjoint[perf_well])
        cell_fix = jnp.zeros((NX * NY * NZ, 3, column_count), jnp.float32).at[global_cell].add(perf_fixes)
        corrected = forward - jnp.transpose(cell_fix, (1, 2, 0)).reshape(forward.shape)
        backward = jnp.zeros_like(corrected)
        for color_index in (3, 2, 1, 0):
            if color_index == 3:
                source = corrected
            else:
                source = corrected - grid_sum(incoming, backward)
            backward = jnp.where((cell_colors == color_index)[None, None], source, backward)
        return backward, well_adjoint

    cells_out, wells_out = lax.map(solve, (rhs_blocks, well_blocks))
    cell_adjoint = cells_out.transpose(1, 0, 2, 3, 4, 5).reshape(3, RHS, NX, NY, NZ)
    well_adjoint = wells_out.transpose(1, 2, 0, 3).reshape(WELLS, 3, RHS)
    return cell_adjoint, well_adjoint
```

```python
import jax
import jax.numpy as jnp
from jax import lax
from jax.experimental import pallas as pl
from jax.experimental.pallas import tpu as pltpu
from jax.sharding import PartitionSpec as P

RHS = 128
LANES = 128
ROWS = 32
SLICE = 8
FACE_RX, FACE_LX, FACE_RY, FACE_LY, FACE_ZU, FACE_ZS = range(6)
SHAPE4 = jax.ShapeDtypeStruct((4, 3, RHS, LANES), jnp.float32)
SHAPE2 = jax.ShapeDtypeStruct((2, 3, RHS, LANES), jnp.float32)
COEF = jax.ShapeDtypeStruct((8, 54, LANES), jnp.float32)


def call(body, outs, args, scratch=(), flops=1_000_000, name=None):
    return pl.pallas_call(
        body,
        out_shape=outs,
        in_specs=[pl.BlockSpec(memory_space=pltpu.VMEM)] * len(args),
        out_specs=jax.tree.map(lambda _: pl.BlockSpec(memory_space=pltpu.VMEM), outs),
        scratch_shapes=list(scratch),
        compiler_params=pltpu.CompilerParams(vmem_limit_bytes=32 * 1024 * 1024),
        cost_estimate=pl.CostEstimate(flops=flops, bytes_accessed=3_000_000, transcendentals=0),
        name=name,
    )(*args)


def spots():
    return lax.rem(lax.axis_index("slab"), 2), lax.rem(lax.axis_index("col"), 2)


def line_xy(tx, ty):
    sp, cp = spots()
    x = sp if tx else 1 - sp
    y = cp if ty else 1 - cp
    return x, y


def xor(a, b):
    return a + b - 2 * a * b


def lane_iota(rows):
    return lax.broadcasted_iota(jnp.int32, (rows, LANES), 1)


def pick(values, index):
    return jnp.take_along_axis(values, index, axis=1)


def split_z(low, high, odd):
    lane = lane_iota(low.shape[0])
    index = (2 * lane + odd) & (LANES - 1)
    return jnp.where(lane < LANES // 2, pick(low, index), pick(high, index))


def join_z(even, odd, half):
    lane = lane_iota(even.shape[0])
    index = half * (LANES // 2) + (lane >> 1)
    return jnp.where((lane & 1) == 0, pick(even, index), pick(odd, index))


def line_rows(ref, start, count):
    return ref[pl.ds(start, count, stride=SLICE), :]


def tile_split(tile):
    lane = lane_iota(SLICE)
    part = (lax.broadcasted_iota(jnp.int32, (SLICE, LANES), 0) >> 1) & 1
    even = pick(tile, (2 * lane) & (LANES - 1))
    odd = pick(tile, (2 * lane + 1) & (LANES - 1))
    low = lane < LANES // 2
    of_even = jnp.where(low, even, pltpu.roll(even, SLICE - 2, 0))
    of_odd = jnp.where(low, pltpu.roll(odd, 2, 0), odd)
    return jnp.where(part == 0, of_even, of_odd)


def pivoted(rhs_ref, piv, cls, tx, ty, rows):
    x, y = line_xy(tx, ty)
    odd = xor(xor(x, y), cls)
    planes = []
    for a in range(3):
        base = (a * RHS + rows) * SLICE + x * 4 + y
        planes.append(
            split_z(line_rows(rhs_ref, base, ROWS), line_rows(rhs_ref, base + 2, ROWS), odd)
        )
    return [
        piv[0 * 3 + b] * planes[0] + piv[1 * 3 + b] * planes[1] + piv[2 * 3 + b] * planes[2]
        for b in range(3)
    ]


def class_rows(ref, cls, tx, ty, count):
    x, y = line_xy(tx, ty)
    odd = xor(xor(x, y), cls)
    return ref[pl.ds(x * 4 + odd * 2 + y, count, stride=SLICE), :]


def chunks(body):
    def step(i, carry):
        body(pl.multiple_of(i * ROWS, ROWS))
        return carry

    lax.fori_loop(0, RHS // ROWS, step, 0)


def lines():
    return [(tx, ty) for tx in range(2) for ty in range(2)]


def store_sends(outs, tx, ty, b, rows, value):
    sxa, sxb, sya, syb = outs
    (sxb if tx else sxa)[ty, b, pl.ds(rows, ROWS), :] = value
    (syb if ty else sya)[tx, b, pl.ds(rows, ROWS), :] = value


def first_kernel(rhs_ref, piv_ref, colors_ref, q_ref, sxa, sxb, sya, syb, tiles, color_tile):
    for row in range(9):
        tiles[row * 8 : row * 8 + 8, :] = tile_split(piv_ref[row * 8 : row * 8 + 8, :])
    color_tile[...] = tile_split(colors_ref[...])
    for tx, ty in lines():
        piv_rows = class_rows(tiles, 0, tx, ty, 9)
        piv = [piv_rows[i : i + 1] for i in range(9)]
        mask = class_rows(color_tile, 0, tx, ty, 1) == 0

        def body(rows, tx=tx, ty=ty, piv=piv, mask=mask):
            for b, value in enumerate(pivoted(rhs_ref, piv, 0, tx, ty, rows)):
                q_ref[tx * 2 + ty, b, pl.ds(rows, ROWS), :] = value
                store_sends((sxa, sxb, sya, syb), tx, ty, b, rows, jnp.where(mask, value, 0.0))

        chunks(body)


def add_local(acc, coef, d, tx, ty, rows, sxa, sxb, cls):
    x, y = line_xy(tx, ty)
    odd = xor(xor(x, y), cls)
    shift = 1 + odd * (LANES - 2)
    own, across = (sxb, sxa) if tx else (sxa, sxb)
    part = pl.ds(rows, ROWS)
    for a in range(3):
        center = own[ty, a, part, :]
        for face, value in (
            (FACE_LX, across[ty, a, part, :]),
            (FACE_LY, own[1 - ty, a, part, :]),
            (FACE_ZU, center),
            (FACE_ZS, pltpu.roll(center, shift, 1)),
        ):
            for b in range(3):
                row = face * 9 + a * 3 + b
                acc[b] = acc[b] - coef[d, row : row + 1, :] * value
    return acc


def add_remote(acc, coef, d, tx, ty, rows, halos):
    rxa, rxb, rya, ryb = halos
    part = pl.ds(rows, ROWS)
    for a in range(3):
        for face, value in (
            (FACE_RX, (rxb if tx else rxa)[ty, a, part, :]),
            (FACE_RY, (ryb if ty else rya)[tx, a, part, :]),
        ):
            for b in range(3):
                row = face * 9 + a * 3 + b
                acc[b] = acc[b] - coef[d, row : row + 1, :] * value
    return acc


def second_kernel(
    rhs_ref, piv_ref, colors_ref, inc_ref, sxa, sxb,
    part_ref, fwd_ref, bwd_ref, cls_colors_ref, tiles, color_tile, raw, folded,
):
    for row in range(9):
        tiles[row * 8 : row * 8 + 8, :] = tile_split(piv_ref[row * 8 : row * 8 + 8, :])
    color_tile[...] = tile_split(colors_ref[...])
    spot = lax.broadcasted_iota(jnp.int32, (SLICE, LANES), 0)
    lane = lane_iota(SLICE)
    x_low = (spot >> 2) == 0
    y_low = (spot & 1) == 0
    z_even = ((spot >> 1) & 1) == 0
    edge = (z_even & (lane == 0)) | (jnp.logical_not(z_even) & (lane == LANES - 1))

    def source(face, entry):
        row = (face * 9 + entry) * 8
        return tile_split(inc_ref[row : row + 8, :])

    piv = [tiles[i * 8 : i * 8 + 8, :] for i in range(9)]
    for group, (first, second, low) in enumerate(((0, 1, x_low), (2, 3, y_low), (5, 4, z_even))):
        one = [None] * 9
        two = [None] * 9
        for entry in range(9):
            p, q = source(first, entry), source(second, entry)
            one[entry] = jnp.where(low, p, q)
            two[entry] = jnp.where(low, q, p)
            if group == 2:
                two[entry] = jnp.where(edge, 0.0, two[entry])
        for which, block in ((0, one), (1, two)):
            face = group * 2 + which
            for a in range(3):
                for b in range(3):
                    row = (face * 9 + a * 3 + b) * 8
                    raw[row : row + 8, :] = block[a * 3 + b]
                    folded[row : row + 8, :] = (
                        block[a * 3] * piv[b]
                        + block[a * 3 + 1] * piv[3 + b]
                        + block[a * 3 + 2] * piv[6 + b]
                    )
    for cls in range(2):
        for tx, ty in lines():
            d = cls * 4 + tx * 2 + ty
            fwd_ref[d] = class_rows(folded, cls, tx, ty, 54)
            bwd_ref[d] = class_rows(raw, cls, tx, ty, 54)
            cls_colors_ref[d : d + 1, :] = class_rows(color_tile, cls, tx, ty, 1)
    for tx, ty in lines():
        d = 4 + tx * 2 + ty
        piv_rows = class_rows(tiles, 1, tx, ty, 9)
        piv1 = [piv_rows[i : i + 1] for i in range(9)]

        def body(rows, tx=tx, ty=ty, piv1=piv1, d=d):
            acc = pivoted(rhs_ref, piv1, 1, tx, ty, rows)
            acc = add_local(acc, fwd_ref, d, tx, ty, rows, sxa, sxb, 1)
            for b in range(3):
                part_ref[tx * 2 + ty, b, pl.ds(rows, ROWS), :] = acc[b]

        chunks(body)


def local_kernel(cls, base_ref, coef_ref, sxa, sxb, part_ref):
    for tx, ty in lines():
        n = tx * 2 + ty

        def body(rows, tx=tx, ty=ty, n=n):
            acc = [base_ref[n, b, pl.ds(rows, ROWS), :] for b in range(3)]
            acc = add_local(acc, coef_ref, cls * 4 + n, tx, ty, rows, sxa, sxb, cls)
            for b in range(3):
                part_ref[n, b, pl.ds(rows, ROWS), :] = acc[b]

        chunks(body)


def remote_kernel(
    cls, color, part_ref, coef_ref, colors_ref, rxa, rxb, rya, ryb, full_ref, sxa, sxb, sya, syb
):
    for tx, ty in lines():
        n = tx * 2 + ty
        d = cls * 4 + n

        def body(rows, tx=tx, ty=ty, n=n, d=d):
            acc = [part_ref[n, b, pl.ds(rows, ROWS), :] for b in range(3)]
            acc = add_remote(acc, coef_ref, d, tx, ty, rows, (rxa, rxb, rya, ryb))
            mask = colors_ref[d : d + 1, :] == color
            for b in range(3):
                full_ref[n, b, pl.ds(rows, ROWS), :] = acc[b]
                store_sends((sxa, sxb, sya, syb), tx, ty, b, rows, jnp.where(mask, acc[b], 0.0))

        chunks(body)


def perf_place(perf_cell):
    sp, cp = spots()
    x = perf_cell >> 9
    y = (perf_cell >> 8) & 1
    z = perf_cell & 255
    cls = (x + y + z) & 1
    tx = (x + 1 - sp) & 1
    ty = (y + 1 - cp) & 1
    return (cls * 4 + tx * 2 + ty) * LANES + (z >> 1)


def hot(index, start, count):
    rows = lax.broadcasted_iota(jnp.int32, (count, index.shape[1]), 0) + start
    return jnp.where(rows == index, 1.0, 0.0).astype(jnp.bfloat16)


def thirds(values):
    one = values.astype(jnp.bfloat16)
    rest = values - one.astype(jnp.float32)
    two = rest.astype(jnp.bfloat16)
    three = (rest - two.astype(jnp.float32)).astype(jnp.bfloat16)
    return one, two, three


def exact_dot(values, ones, dims):
    out = None
    for part in thirds(values):
        term = lax.dot_general(part, ones, (dims, ((), ())), preferred_element_type=jnp.float32)
        out = term if out is None else out + term
    return out


def wells_kernel(
    part_ref, t_ref, q_ref, u_ref, coef_ref, colors_ref, rxa, rxb, rya, ryb,
    perf_cell_ref, perf_well_ref, perf_out_ref, even_ref, odd_ref, sums_ref, at_ref,
):
    for tx, ty in lines():
        n = tx * 2 + ty
        d = 4 + n

        def body(rows, tx=tx, ty=ty, n=n, d=d):
            part = pl.ds(rows, ROWS)
            acc = [part_ref[n, b, part, :] for b in range(3)]
            acc = add_remote(acc, coef_ref, d, tx, ty, rows, (rxa, rxb, rya, ryb))
            is_one = colors_ref[d : d + 1, :] == 1
            is_two = colors_ref[n : n + 1, :] == 2
            for b in range(3):
                odd_ref[n, b, part, :] = jnp.where(is_one, t_ref[n, b, part, :], acc[b])
                even_ref[n, b, part, :] = jnp.where(is_two, u_ref[n, b, part, :], q_ref[n, b, part, :])

        chunks(body)
    place = perf_place(perf_cell_ref[...])
    at_perfs = None
    for cls, ref in ((0, even_ref), (1, odd_ref)):
        for n in range(4):
            planes = ref[n].reshape(3 * RHS, LANES)
            term = exact_dot(planes, hot(place, (cls * 4 + n) * LANES, LANES), ((1,), (0,)))
            at_perfs = term if at_perfs is None else at_perfs + term
    for b in range(3):
        at_ref[b * RHS : (b + 1) * RHS, :] = sum(
            perf_out_ref[a * 3 + b : a * 3 + b + 1, :] * at_perfs[a * RHS : (a + 1) * RHS]
            for a in range(3)
        )
    wells = hot(perf_well_ref[...], 0, sums_ref.shape[0])
    out = None
    for part in thirds(at_ref[...]):
        term = lax.dot_general(
            wells, part, (((1,), (1,)), ((), ())), preferred_element_type=jnp.float32
        )
        out = term if out is None else out + term
    sums_ref[...] = out


def fix_kernel(
    wells_ref, even_ref, odd_ref, colors_ref, perf_cell_ref, perf_well_ref, perf_in_ref,
    even_out, odd_out, sxa, sxb, sya, syb, at_ref,
):
    wells = wells_ref[...].T
    at_perfs = exact_dot(wells, hot(perf_well_ref[...], 0, wells.shape[1]), ((1,), (0,)))
    for b in range(3):
        at_ref[b * RHS : (b + 1) * RHS, :] = sum(
            perf_in_ref[a * 3 + b : a * 3 + b + 1, :] * at_perfs[a * RHS : (a + 1) * RHS]
            for a in range(3)
        )
    place = perf_place(perf_cell_ref[...])
    fixes = thirds(at_ref[...])
    for cls, ref, out in ((1, odd_ref, odd_out), (0, even_ref, even_out)):
        for tx, ty in lines():
            n = tx * 2 + ty
            d = cls * 4 + n
            ones = hot(place, d * LANES, LANES)
            fix = sum(
                lax.dot_general(
                    part, ones, (((1,), (1,)), ((), ())), preferred_element_type=jnp.float32
                )
                for part in fixes
            )
            for b in range(3):
                value = ref[n, b] - fix[b * RHS : (b + 1) * RHS]
                out[n, b] = value
                if cls == 1:
                    sent = jnp.where(colors_ref[d : d + 1, :] == 3, value, 0.0)
                    (sxb if tx else sxa)[ty, b] = sent
                    (syb if ty else sya)[tx, b] = sent


def last_kernel(
    part_ref, u_ref, odd_three, odd_v, coef_ref, colors_ref, rxa, rxb, rya, ryb, out_ref
):
    for tx, ty in lines():
        n = tx * 2 + ty
        x, y = line_xy(tx, ty)
        flip = xor(x, y)

        def body(rows, tx=tx, ty=ty, n=n, x=x, y=y, flip=flip):
            part = pl.ds(rows, ROWS)
            acc = [part_ref[n, b, part, :] for b in range(3)]
            acc = add_remote(acc, coef_ref, n, tx, ty, rows, (rxa, rxb, rya, ryb))
            is_two = colors_ref[n : n + 1, :] == 2
            is_one = colors_ref[4 + n : 5 + n, :] == 1
            for b in range(3):
                even = jnp.where(is_two, u_ref[n, b, part, :], acc[b])
                odd = jnp.where(is_one, odd_v[n, b, part, :], odd_three[n, b, part, :])
                z_even = jnp.where(flip == 1, odd, even)
                z_odd = jnp.where(flip == 1, even, odd)
                for half in range(2):
                    start = (b * RHS + rows) * SLICE + x * 4 + half * 2 + y
                    out_ref[pl.ds(start, ROWS, stride=SLICE), :] = join_z(z_even, z_odd, half)

        chunks(body)


def pairs(axis, second):
    count = lax.axis_size(axis)
    found = []
    for i in range(second, count - 1, 2):
        found += [(i, i + 1), (i + 1, i)]
    return found


def exchange(sends):
    sxa, sxb, sya, syb = sends
    ryb = lax.ppermute(syb, "col", pairs("col", 1))
    rya = lax.ppermute(sya, "col", pairs("col", 0))
    rxb = lax.ppermute(sxb, "slab", pairs("slab", 1))
    rxa = lax.ppermute(sxa, "slab", pairs("slab", 0))
    return rxa, rxb, rya, ryb


def well_apply(blocks, vector):
    return (
        blocks[:, 0, :, None] * vector[:, 0, None, :]
        + blocks[:, 1, :, None] * vector[:, 1, None, :]
        + blocks[:, 2, :, None] * vector[:, 2, None, :]
    )


def to_rows(array):
    lead = array.shape[:-3]
    split = array.reshape(lead + (2, 2, 2, LANES))
    return jnp.swapaxes(split, -3, -2).reshape(-1, LANES)


def from_rows(rows):
    split = rows.reshape(3, RHS, 2, 2, 2, LANES)
    return jnp.swapaxes(split, -3, -2).reshape(3, RHS, 2, 2, 2 * LANES)


def per_device(
    cell_rhs, well_rhs, cell_colors, incoming, pivot_inv,
    perf_cell, perf_well, perf_out, perf_in, well_pivot_inv,
):
    rhs = to_rows(cell_rhs)
    colors_in = to_rows(cell_colors)
    inc = to_rows(incoming)
    piv = to_rows(pivot_inv)
    perfs = perf_cell.shape[0]
    place = perf_cell.reshape(1, perfs)
    well = perf_well.reshape(1, perfs)
    out_blocks = jnp.transpose(perf_out, (1, 2, 0)).reshape(9, perfs)
    in_blocks = jnp.transpose(perf_in, (1, 2, 0)).reshape(9, perfs)
    sends = [SHAPE2] * 4
    tile_scratch = [pltpu.VMEM((72, LANES), jnp.float32), pltpu.VMEM((8, LANES), jnp.int32)]

    q_even, *s0 = call(first_kernel, [SHAPE4] + sends, (rhs, piv, colors_in), tile_scratch, name="even_rhs")
    halo = exchange(s0)
    part, fwd, bwd, colors = call(
        second_kernel,
        [SHAPE4, COEF, COEF, jax.ShapeDtypeStruct((8, LANES), jnp.int32)],
        (rhs, piv, colors_in, inc, s0[0], s0[1]),
        tile_scratch + [pltpu.VMEM((54 * 8, LANES), jnp.float32)] * 2,
        name="blocks_and_local",
    )

    def local(cls, base, coef, s, name):
        def body(*refs):
            local_kernel(cls, *refs)

        return call(body, SHAPE4, (base, coef, s[0], s[1]), name=name)

    def remote(cls, color, part, coef, halo, name):
        def body(*refs):
            remote_kernel(cls, color, *refs)

        full, *s = call(body, [SHAPE4] + sends, (part, coef, colors) + tuple(halo), name=name)
        return full, s

    t_odd, s1 = remote(1, 1, part, fwd, halo, "forward_one")
    halo = exchange(s1)
    part = local(0, q_even, fwd, s1, "forward_two_local")
    u_even, s2 = remote(0, 2, part, fwd, halo, "forward_two")
    halo = exchange(s2)
    part = local(1, t_odd, fwd, s2, "forward_three_local")
    own_count = well_pivot_inv.shape[0]
    well_count = lax.axis_size(("slab", "col")) * own_count
    devices = well_count // own_count
    even, odd, sums = call(
        wells_kernel,
        [SHAPE4, SHAPE4, jax.ShapeDtypeStruct((well_count, 3 * RHS), jnp.float32)],
        (part, t_odd, q_even, u_even, fwd, colors) + tuple(halo) + (place, well, out_blocks),
        [pltpu.VMEM((3 * RHS, perfs), jnp.float32)],
        name="forward_three_wells",
    )
    axes = ("slab", "col")
    parts = lax.all_to_all(
        sums.reshape(devices, own_count * 3, RHS), axes, 0, 0, tiled=True
    )
    own_sum = jnp.sum(parts, axis=0).reshape(own_count, 3, RHS)
    well_adjoint = well_apply(well_pivot_inv, well_rhs - own_sum)
    spread = jnp.broadcast_to(well_adjoint.reshape(1, own_count * 3, RHS), (devices, own_count * 3, RHS))
    all_wells = lax.all_to_all(spread, axes, 0, 0, tiled=True).reshape(well_count, 3 * RHS)
    x_even, x_odd, *s3 = call(
        fix_kernel,
        [SHAPE4, SHAPE4] + sends,
        (all_wells, even, odd, colors, place, well, in_blocks),
        [pltpu.VMEM((3 * RHS, perfs), jnp.float32)],
        name="well_fix",
    )
    halo = exchange(s3)
    part = local(0, x_even, bwd, s3, "backward_two_local")
    u_even, s4 = remote(0, 2, part, bwd, halo, "backward_two")
    halo = exchange(s4)
    part = local(1, x_odd, bwd, s4, "backward_one_local")
    v_odd, s5 = remote(1, 1, part, bwd, halo, "backward_one")
    halo = exchange(s5)
    part = local(0, u_even, bwd, s5, "backward_zero_local")
    rows = call(
        last_kernel,
        jax.ShapeDtypeStruct((3 * RHS * SLICE, LANES), jnp.float32),
        (part, u_even, x_odd, v_odd, bwd, colors) + tuple(halo),
        name="backward_zero",
    )
    return from_rows(rows), well_adjoint


def solution(mesh):
    placed = (
        P(None, None, "slab", "col", None),
        P(("slab", "col"), None, None),
        P("slab", "col", None),
        P(None, None, None, "slab", "col", None),
        P(None, None, "slab", "col", None),
        P(("slab", "col")),
        P(("slab", "col")),
        P(("slab", "col"), None, None),
        P(("slab", "col"), None, None),
        P(("slab", "col"), None, None),
    )
    return jax.shard_map(
        per_device,
        mesh=mesh,
        in_specs=placed,
        out_specs=(P(None, None, "slab", "col", None), P(("slab", "col"), None, None)),
        check_vma=False,
    )
```

```python
import jax
import jax.numpy as jnp
from jax import lax
from jax.experimental import pallas as pl
from jax.experimental.pallas import tpu as pltpu
from jax.sharding import PartitionSpec as P

RHS = 128
LANES = 128
ROWS = 32
SLICE = 8
FACE_RX, FACE_LX, FACE_RY, FACE_LY, FACE_ZU, FACE_ZS = range(6)
PERFS = 64
SENT = 6 * RHS
EXTRA = 16
WIDE = 4 * LANES


def f32(*shape):
    return jax.ShapeDtypeStruct(shape, jnp.float32)


PLANES = f32(4, 3, RHS, LANES)
FACE = f32(SENT, LANES)
FACE_PLUS = f32(SENT + EXTRA, LANES)
COEF = f32(8, 54, LANES)


def call(body, outs, args, scratch=(), name=None, hbm=(), hbm_out=False):
    spaces = [pltpu.HBM if i in hbm else pltpu.VMEM for i in range(len(args))]
    out_space = pltpu.HBM if hbm_out else pltpu.VMEM
    return pl.pallas_call(
        body,
        out_shape=outs,
        in_specs=[pl.BlockSpec(memory_space=space) for space in spaces],
        out_specs=jax.tree.map(lambda _: pl.BlockSpec(memory_space=out_space), outs),
        scratch_shapes=list(scratch),
        compiler_params=pltpu.CompilerParams(vmem_limit_bytes=16 * 1024 * 1024),
        cost_estimate=pl.CostEstimate(flops=1_000_000, bytes_accessed=2_000_000, transcendentals=0),
        name=name,
    )(*args)


def spots():
    return lax.rem(lax.axis_index("slab"), 2), lax.rem(lax.axis_index("col"), 2)


def line_xy(tx, ty):
    sp, cp = spots()
    x = sp if tx else 1 - sp
    y = cp if ty else 1 - cp
    return x, y


def xor(a, b):
    return a + b - 2 * a * b


def lane_iota(rows):
    return lax.broadcasted_iota(jnp.int32, (rows, LANES), 1)


def pick(values, index):
    return jnp.take_along_axis(values, index, axis=1)


def split_z(low, high, odd):
    lane = lane_iota(low.shape[0])
    index = (2 * lane + odd) & (LANES - 1)
    return jnp.where(lane < LANES // 2, pick(low, index), pick(high, index))


def join_z(even, odd, half):
    lane = lane_iota(even.shape[0])
    index = half * (LANES // 2) + (lane >> 1)
    return jnp.where((lane & 1) == 0, pick(even, index), pick(odd, index))


def line_rows(ref, start, count):
    return ref[pl.ds(start, count, stride=SLICE), :]


def tile_split(tile):
    lane = lane_iota(SLICE)
    part = (lax.broadcasted_iota(jnp.int32, (SLICE, LANES), 0) >> 1) & 1
    even = pick(tile, (2 * lane) & (LANES - 1))
    odd = pick(tile, (2 * lane + 1) & (LANES - 1))
    low = lane < LANES // 2
    of_even = jnp.where(low, even, pltpu.roll(even, SLICE - 2, 0))
    of_odd = jnp.where(low, pltpu.roll(odd, 2, 0), odd)
    return jnp.where(part == 0, of_even, of_odd)


def split_tiles(source, target, count):
    for row in range(count):
        target[row * 8 : row * 8 + 8, :] = tile_split(source[row * 8 : row * 8 + 8, :])


def pivoted(rhs_ref, piv, cls, tx, ty, rows):
    x, y = line_xy(tx, ty)
    odd = xor(xor(x, y), cls)
    planes = []
    for a in range(3):
        base = (a * RHS + rows) * SLICE + x * 4 + y
        planes.append(
            split_z(line_rows(rhs_ref, base, ROWS), line_rows(rhs_ref, base + 2, ROWS), odd)
        )
    return [
        piv[0 * 3 + b] * planes[0] + piv[1 * 3 + b] * planes[1] + piv[2 * 3 + b] * planes[2]
        for b in range(3)
    ]


def class_rows(ref, cls, tx, ty, count):
    x, y = line_xy(tx, ty)
    odd = xor(xor(x, y), cls)
    return ref[pl.ds(x * 4 + odd * 2 + y, count, stride=SLICE), :]


def chunks(body):
    def step(i, carry):
        body(pl.multiple_of(i * ROWS, ROWS))
        return carry

    lax.fori_loop(0, RHS // ROWS, step, 0)


def lines():
    return [(tx, ty) for tx in range(2) for ty in range(2)]


def at_face(t, b, rows, count=ROWS):
    return pl.ds((t * 3 + b) * RHS + rows, count)


def from_sy(sya, syb, rows):
    return lambda tx, ty, a: (syb if ty else sya)[at_face(tx, a, rows), :]


def from_halos(halos, rows):
    rya, ryb, rxb, rxa = halos
    return (
        lambda tx, ty, a: (rxb if tx else rxa)[at_face(ty, a, rows), :],
        lambda tx, ty, a: (ryb if ty else rya)[at_face(tx, a, rows), :],
    )


def take(acc, coef, d, face, a, value):
    for b in range(3):
        row = face * 9 + a * 3 + b
        acc[b] = acc[b] - coef[d, row : row + 1, :] * value


def add_local(acc, coef, cls, tx, ty, get):
    x, y = line_xy(tx, ty)
    odd = xor(xor(x, y), cls)
    shift = 1 + odd * (LANES - 2)
    d = cls * 4 + tx * 2 + ty
    for a in range(3):
        center = get(tx, ty, a)
        take(acc, coef, d, FACE_LX, a, get(1 - tx, ty, a))
        take(acc, coef, d, FACE_LY, a, get(tx, 1 - ty, a))
        take(acc, coef, d, FACE_ZU, a, center)
        take(acc, coef, d, FACE_ZS, a, pltpu.roll(center, shift, 1))
    return acc


def add_remote(acc, coef, cls, tx, ty, get_x, get_y):
    d = cls * 4 + tx * 2 + ty
    for a in range(3):
        take(acc, coef, d, FACE_RX, a, get_x(tx, ty, a))
        take(acc, coef, d, FACE_RY, a, get_y(tx, ty, a))
    return acc


def store_faces(faces, tx, ty, b, rows, value):
    sya, syb, sxb, sxa = faces
    (syb if ty else sya)[at_face(tx, b, rows), :] = value
    (sxb if tx else sxa)[at_face(ty, b, rows), :] = value


def first_kernel(
    rhs_hbm, piv_hbm, colors_hbm, q_ref, sya, syb, sxb, sxa,
    rhs_ref, piv_ref, colors_ref, tiles, color_tile, sems,
):
    steps = RHS // ROWS

    def rhs_copy(i, a):
        part = pl.ds((a * RHS + i * ROWS) * SLICE, ROWS * SLICE)
        return pltpu.make_async_copy(rhs_hbm.at[part], rhs_ref.at[part], sems.at[2 + i * 3 + a])

    piv_copy = pltpu.make_async_copy(piv_hbm, piv_ref, sems.at[0])
    color_copy = pltpu.make_async_copy(colors_hbm, colors_ref, sems.at[1])
    piv_copy.start()
    color_copy.start()
    for i in range(steps):
        for a in range(3):
            rhs_copy(i, a).start()
    piv_copy.wait()
    split_tiles(piv_ref, tiles, 9)
    color_copy.wait()
    color_tile[...] = tile_split(colors_ref[...])

    def step(i, carry):
        for a in range(3):
            rhs_copy(i, a).wait()
        rows = pl.multiple_of(i * ROWS, ROWS)
        for tx, ty in lines():
            piv_rows = class_rows(tiles, 0, tx, ty, 9)
            piv = [piv_rows[e : e + 1] for e in range(9)]
            mask = class_rows(color_tile, 0, tx, ty, 1) == 0
            for b, value in enumerate(pivoted(rhs_ref, piv, 0, tx, ty, rows)):
                q_ref[tx * 2 + ty, b, pl.ds(rows, ROWS), :] = value
                store_faces((sya, syb, sxb, sxa), tx, ty, b, rows, jnp.where(mask, value, 0.0))
        return carry

    lax.fori_loop(0, steps, step, 0)


def second_kernel(
    rhs_ref, piv_ref, colors_ref, inc_ref, sya, syb, well_piv_ref,
    part_ref, fwd_ref, bwd_ref, cls_colors_ref, well_rows_ref, tiles, color_tile, raw, folded,
):
    well_rows_ref[...] = jnp.zeros(well_rows_ref.shape, jnp.float32)
    for a in range(3):
        well_rows_ref[0:2, a * 3 : a * 3 + 3] = well_piv_ref[a]
    split_tiles(piv_ref, tiles, 9)
    color_tile[...] = tile_split(colors_ref[...])
    spot = lax.broadcasted_iota(jnp.int32, (SLICE, LANES), 0)
    lane = lane_iota(SLICE)
    x_low = (spot >> 2) == 0
    y_low = (spot & 1) == 0
    z_even = ((spot >> 1) & 1) == 0
    edge = (z_even & (lane == 0)) | (jnp.logical_not(z_even) & (lane == LANES - 1))

    slab, col = lax.axis_index("slab"), lax.axis_index("col")
    inside = [
        jnp.where(low, jnp.where(at == 0, 0.0, 1.0), jnp.where(at == last, 0.0, 1.0))
        for low, at, last in (
            (x_low, slab, lax.axis_size("slab") - 1),
            (y_low, col, lax.axis_size("col") - 1),
        )
    ]

    def source(face, entry):
        row = (face * 9 + entry) * 8
        return tile_split(inc_ref[row : row + 8, :])

    piv = [tiles[i * 8 : i * 8 + 8, :] for i in range(9)]
    for group, (first, second, low) in enumerate(((0, 1, x_low), (2, 3, y_low), (5, 4, z_even))):
        one = [None] * 9
        two = [None] * 9
        for entry in range(9):
            p, q = source(first, entry), source(second, entry)
            one[entry] = jnp.where(low, p, q)
            two[entry] = jnp.where(low, q, p)
            if group < 2:
                one[entry] = one[entry] * inside[group]
            else:
                two[entry] = jnp.where(edge, 0.0, two[entry])
        for which, block in ((0, one), (1, two)):
            face = group * 2 + which
            for a in range(3):
                for b in range(3):
                    row = (face * 9 + a * 3 + b) * 8
                    raw[row : row + 8, :] = block[a * 3 + b]
                    folded[row : row + 8, :] = (
                        block[a * 3] * piv[b]
                        + block[a * 3 + 1] * piv[3 + b]
                        + block[a * 3 + 2] * piv[6 + b]
                    )
    for cls in range(2):
        for tx, ty in lines():
            d = cls * 4 + tx * 2 + ty
            fwd_ref[d] = class_rows(folded, cls, tx, ty, 54)
            bwd_ref[d] = class_rows(raw, cls, tx, ty, 54)
            cls_colors_ref[d : d + 1, :] = class_rows(color_tile, cls, tx, ty, 1)
    for tx, ty in lines():
        piv_rows = class_rows(tiles, 1, tx, ty, 9)
        piv1 = [piv_rows[i : i + 1] for i in range(9)]

        def body(rows, tx=tx, ty=ty, piv1=piv1):
            acc = pivoted(rhs_ref, piv1, 1, tx, ty, rows)
            acc = add_local(acc, fwd_ref, 1, tx, ty, from_sy(sya, syb, rows))
            for b in range(3):
                part_ref[tx * 2 + ty, b, pl.ds(rows, ROWS), :] = acc[b]

        chunks(body)


def local_kernel(cls, base_ref, coef_ref, sya, syb, part_ref):
    for tx, ty in lines():
        n = tx * 2 + ty

        def body(rows, tx=tx, ty=ty, n=n):
            acc = [base_ref[n, b, pl.ds(rows, ROWS), :] for b in range(3)]
            acc = add_local(acc, coef_ref, cls, tx, ty, from_sy(sya, syb, rows))
            for b in range(3):
                part_ref[n, b, pl.ds(rows, ROWS), :] = acc[b]

        chunks(body)


def remote_kernel(cls, color, part_ref, coef_ref, colors_ref, rya, ryb, rxb, rxa, full_ref, *faces):
    for tx, ty in lines():
        n = tx * 2 + ty
        d = cls * 4 + n

        def body(rows, tx=tx, ty=ty, n=n, d=d):
            acc = [part_ref[n, b, pl.ds(rows, ROWS), :] for b in range(3)]
            acc = add_remote(acc, coef_ref, cls, tx, ty, *from_halos((rya, ryb, rxb, rxa), rows))
            mask = colors_ref[d : d + 1, :] == color
            for b in range(3):
                full_ref[n, b, pl.ds(rows, ROWS), :] = acc[b]
                store_faces(faces, tx, ty, b, rows, jnp.where(mask, acc[b], 0.0))

        chunks(body)


def perf_place(perf_cell):
    sp, cp = spots()
    x = perf_cell >> 9
    y = (perf_cell >> 8) & 1
    z = perf_cell & 255
    cls = (x + y + z) & 1
    tx = (x + 1 - sp) & 1
    ty = (y + 1 - cp) & 1
    return (cls * 4 + tx * 2 + ty) * LANES + (z >> 1)


def forward_one_kernel(
    part_ref, coef_ref, colors_ref, rya, ryb, rxb, rxa, perf_cell_ref, perf_well_ref, perf_in_ref,
    full_ref, sya, syb, sxb, sxa,
):
    faces = (sya, syb, sxb, sxa)
    remote_kernel(1, 1, part_ref, coef_ref, colors_ref, rya, ryb, rxb, rxa, full_ref, *faces)
    for target, start, step in ((sya, 4, 2), (syb, 5, 2), (sxb, 6, 1), (sxa, 4, 1)):
        target[SENT:, :] = jnp.zeros((EXTRA, LANES), jnp.float32)
        target[SENT : SENT + 1, 0:PERFS] = perf_place(perf_cell_ref[...]).astype(jnp.float32)
        target[SENT + 1 : SENT + 2, 0:PERFS] = perf_well_ref[...].astype(jnp.float32)
        for a in range(3):
            row = SENT + 2 + a * 3
            target[row : row + 3, 0:PERFS] = perf_in_ref[a]
        for t in range(2):
            d = start + t * step
            row = SENT + 11 + t
            target[row : row + 1, :] = colors_ref[d : d + 1, :].astype(jnp.float32)


def forward_two_kernel(
    part_ref, coef_ref, colors_ref, rya, ryb, rxb, rxa, full_ref, sya, syb, sxb, sxa, extra_ref
):
    faces = (sya, syb, sxb, sxa)
    remote_kernel(0, 2, part_ref, coef_ref, colors_ref, rya, ryb, rxb, rxa, full_ref, *faces)
    for i, ref in enumerate((rya, ryb, rxb, rxa)):
        extra_ref[i] = ref[SENT:, :]


def hot(index, count, start=0, step=LANES):
    rows = lax.broadcasted_iota(jnp.int32, (count, index.shape[1]), 0)
    rows = start + (rows >> 7) * step + (rows & (LANES - 1))
    return jnp.where(rows == index, 1.0, 0.0).astype(jnp.bfloat16)


def halves(values):
    high = values.astype(jnp.bfloat16)
    return high, (values - high.astype(jnp.float32)).astype(jnp.bfloat16)


def dot_ones(parts, ones, dims):
    return sum(
        lax.dot_general(part, ones, (dims, ((), ())), preferred_element_type=jnp.float32)
        for part in parts
    )


def well_bits():
    slab = lax.axis_index("slab")
    return slab & 1, slab >> 3


def forward_three_kernel(
    part_ref, t_ref, q_ref, u_ref, coef_ref, colors_ref, rya, ryb, rxb, rxa,
    perf_cell_ref, perf_well_ref, perf_out_ref, well_rhs_ref, well_piv_ref,
    even_ref, odd_ref, keep_ref, send_ref, sya, syb, at_ref,
):
    for tx, ty in lines():
        n = tx * 2 + ty
        d = 4 + n

        def body(rows, tx=tx, ty=ty, n=n, d=d):
            part = pl.ds(rows, ROWS)
            acc = [part_ref[n, b, part, :] for b in range(3)]
            acc = add_remote(acc, coef_ref, 1, tx, ty, *from_halos((rya, ryb, rxb, rxa), rows))
            is_one = colors_ref[d : d + 1, :] == 1
            is_two = colors_ref[n : n + 1, :] == 2
            for b in range(3):
                value = jnp.where(is_one, t_ref[n, b, part, :], acc[b])
                odd_ref[n, b, part, :] = value
                (syb if ty else sya)[at_face(tx, b, rows), :] = value
                even_ref[n, b, part, :] = jnp.where(is_two, u_ref[n, b, part, :], q_ref[n, b, part, :])

        chunks(body)
    place = perf_place(perf_cell_ref[...])
    at_perfs = None
    for cls, ref in ((0, even_ref), (1, odd_ref)):
        for tx in range(2):
            planes = [ref[tx * 2 + ty].reshape(3 * RHS, LANES) for ty in range(2)]
            ones = hot(place, 2 * LANES, (cls * 4 + tx * 2) * LANES)
            term = dot_ones(halves(jnp.concatenate(planes, axis=1)), ones, ((1,), (0,)))
            at_perfs = term if at_perfs is None else at_perfs + term
    for b in range(3):
        at_ref[b * RHS : (b + 1) * RHS, :] = sum(
            perf_out_ref[a, b : b + 1, :] * at_perfs[a * RHS : (a + 1) * RHS] for a in range(3)
        )
    core, _ = well_bits()
    device = lax.axis_index("slab") * lax.axis_size("col") + lax.axis_index("col")
    parts = halves(at_ref[...])
    count = keep_ref.shape[0]
    for ref, start in ((keep_ref, core * count), (send_ref, (1 - core) * count)):
        wells = hot(perf_well_ref[...], count, start)
        total = sum(
            lax.dot_general(wells, part, (((1,), (1,)), ((), ())), preferred_element_type=jnp.float32)
            for part in parts
        )
        spot = lax.broadcasted_iota(jnp.int32, (count, LANES), 0) + start
        is_own = [spot == device * 2 + j for j in range(2)]
        for b in range(3):
            own = sum(jnp.where(is_own[j], well_rhs_ref[b, j : j + 1, :], 0.0) for j in range(2))
            ref[:, b * LANES : (b + 1) * LANES] = own - total[:, b * LANES : (b + 1) * LANES]
        ref[:, 3 * LANES :] = sum(
            jnp.where(is_own[j], well_piv_ref[j : j + 1, :], 0.0) for j in range(2)
        )


def blocks_kernel(keep_ref, got_ref, *outs):
    _, z_spot = well_bits()
    count = outs[0].shape[0]
    for m, out in enumerate(outs):
        rows = pl.ds(pl.multiple_of((z_spot ^ m) * count, count), count)
        out[...] = keep_ref[rows, :] + got_ref[rows, :]


def sum_kernel(*refs):
    a, b, c, d = refs[:4]
    refs[-1][...] = (a[...] + b[...]) + (c[...] + d[...])


def y_sum_kernel(a, b, c, d, odd_ref, rya, ryb, out_ref, sxb, sxa):
    sum_kernel(a, b, c, d, out_ref)
    for tx, ty in lines():
        for b_ in range(3):
            (sxb if tx else sxa)[at_face(ty, b_, 0, RHS), :] = odd_ref[tx * 2 + ty, b_]


def stack_kernel(*refs):
    count = refs[0].shape[0]
    for i, ref in enumerate(refs[:4]):
        refs[-1][i * count : (i + 1) * count, :] = ref[...]


def solve_kernel(own_ref, one_ref, two_ref, three_ref, out_ref):
    total = (own_ref[...] + one_ref[...]) + (two_ref[...] + three_ref[...])
    for b in range(3):
        out_ref[:, b * LANES : (b + 1) * LANES] = sum(
            total[:, 3 * LANES + a * 3 + b : 3 * LANES + a * 3 + b + 1]
            * total[:, a * LANES : (a + 1) * LANES]
            for a in range(3)
        )


def backward_two_kernel(
    wells_ref, other_ref, even_ref, odd_ref, colors_ref, coef_ref, rya, ryb, rxb, rxa, extra_ref,
    perf_cell_ref, perf_well_ref, perf_in_ref,
    u_ref, x_odd_ref, sya, syb, sxb, sxa, own_wells_ref, at_ref, x_even_ref, three_ref, hya, hyb, hxb, hxa,
):
    core, z_spot = well_bits()

    def place_of_well(well):
        return (((well >> 7) ^ core) << 7) | ((((well >> 5) & 3) ^ z_spot) << 5) | (well & 31)

    device = lax.axis_index("slab") * lax.axis_size("col") + lax.axis_index("col")
    for j in range(2):
        spot = place_of_well(device * 2 + j)
        rows = lax.broadcasted_iota(jnp.int32, (LANES, LANES), 0)
        for b in range(3):
            lanes = slice(b * LANES, (b + 1) * LANES)
            found = jnp.where(rows == spot, wells_ref[:, lanes], 0.0)
            found = found + jnp.where(rows + LANES == spot, other_ref[:, lanes], 0.0)
            own_wells_ref[b, j : j + 1, :] = jnp.sum(found, axis=0, keepdims=True)
    wells = halves(jnp.concatenate([wells_ref[...].T, other_ref[...].T], axis=1))

    def fixes_of(well, blocks):
        at_perfs = dot_ones(wells, hot(place_of_well(well), 2 * LANES), ((1,), (0,)))
        for b in range(3):
            at_ref[b * RHS : (b + 1) * RHS, :] = sum(
                blocks[a][b : b + 1, :] * at_perfs[a * RHS : (a + 1) * RHS] for a in range(3)
            )
        return halves(at_ref[...])

    def spread(fixes, place, start, step):
        return dot_ones(fixes, hot(place, 2 * LANES, start * LANES, step * LANES), ((1,), (1,)))

    fixes = fixes_of(perf_well_ref[...], [perf_in_ref[a] for a in range(3)])
    place = perf_place(perf_cell_ref[...])
    for cls, ref, out in ((1, odd_ref, x_odd_ref), (0, even_ref, x_even_ref)):
        for tx in range(2):
            fix = spread(fixes, place, cls * 4 + tx * 2, 1)
            for ty in range(2):
                n = tx * 2 + ty
                d = cls * 4 + n
                for b in range(3):
                    value = ref[n, b] - fix[b * RHS : (b + 1) * RHS, ty * LANES : (ty + 1) * LANES]
                    out[n, b] = value
                    if cls == 1:
                        three_ref[n, b] = jnp.where(colors_ref[d : d + 1, :] == 3, value, 0.0)
    for i, (halo, out, start, step) in enumerate(
        ((rya, hya, 4, 2), (ryb, hyb, 5, 2), (rxb, hxb, 6, 1), (rxa, hxa, 4, 1))
    ):
        extra = extra_ref[i]
        near_place = extra[0:1, 0:PERFS].astype(jnp.int32)
        near_well = extra[1:2, 0:PERFS].astype(jnp.int32)
        blocks = [extra[2 + a * 3 : 5 + a * 3, 0:PERFS] for a in range(3)]
        fix = spread(fixes_of(near_well, blocks), near_place, start, step)
        for t in range(2):
            mask = extra[11 + t : 12 + t, :] == 3.0
            for b in range(3):
                value = halo[at_face(t, b, 0, RHS), :]
                value = value - fix[b * RHS : (b + 1) * RHS, t * LANES : (t + 1) * LANES]
                out[at_face(t, b, 0, RHS), :] = jnp.where(mask, value, 0.0)
    for tx, ty in lines():
        n = tx * 2 + ty

        def body(rows, tx=tx, ty=ty, n=n):
            acc = [x_even_ref[n, b, pl.ds(rows, ROWS), :] for b in range(3)]
            acc = add_local(
                acc, coef_ref, 0, tx, ty,
                lambda i, j, a: three_ref[i * 2 + j, a, pl.ds(rows, ROWS), :],
            )
            acc = add_remote(acc, coef_ref, 0, tx, ty, *from_halos((hya, hyb, hxb, hxa), rows))
            mask = colors_ref[n : n + 1, :] == 2
            for b in range(3):
                u_ref[n, b, pl.ds(rows, ROWS), :] = acc[b]
                store_faces((sya, syb, sxb, sxa), tx, ty, b, rows, jnp.where(mask, acc[b], 0.0))

        chunks(body)


def last_kernel(
    part_ref, u_ref, odd_three, odd_v, coef_ref, colors_ref, rya, ryb, rxb, rxa, out_hbm, out_ref, sems
):
    steps = RHS // ROWS

    def out_copy(i, b):
        part = pl.ds((b * RHS + i * ROWS) * SLICE, ROWS * SLICE)
        return pltpu.make_async_copy(out_ref.at[part], out_hbm.at[part], sems.at[i * 3 + b])

    def step(i, carry):
        rows = pl.multiple_of(i * ROWS, ROWS)
        part = pl.ds(rows, ROWS)
        for tx, ty in lines():
            n = tx * 2 + ty
            x, y = line_xy(tx, ty)
            flip = xor(x, y)
            acc = [part_ref[n, b, part, :] for b in range(3)]
            acc = add_remote(acc, coef_ref, 0, tx, ty, *from_halos((rya, ryb, rxb, rxa), rows))
            is_two = colors_ref[n : n + 1, :] == 2
            is_one = colors_ref[4 + n : 5 + n, :] == 1
            for b in range(3):
                even = jnp.where(is_two, u_ref[n, b, part, :], acc[b])
                odd = jnp.where(is_one, odd_v[n, b, part, :], odd_three[n, b, part, :])
                z_even = jnp.where(flip == 1, odd, even)
                z_odd = jnp.where(flip == 1, even, odd)
                for half in range(2):
                    start = (b * RHS + rows) * SLICE + x * 4 + half * 2 + y
                    out_ref[pl.ds(start, ROWS, stride=SLICE), :] = join_z(z_even, z_odd, half)
        for b in range(3):
            out_copy(i, b).start()
        return carry

    lax.fori_loop(0, steps, step, 0)
    for i in range(steps):
        for b in range(3):
            out_copy(i, b).wait()


def pairs(axis, second):
    count = lax.axis_size(axis)
    found = []
    for i in range(second, count, 2):
        found += [(i, (i + 1) % count), ((i + 1) % count, i)]
    return found


def swap(value, axis, mask):
    return lax.ppermute(value, axis, [(i, i ^ mask) for i in range(lax.axis_size(axis))])


def exchange(sya, syb, sxb, sxa):
    rya = lax.ppermute(sya, "col", pairs("col", 0))
    ryb = lax.ppermute(syb, "col", pairs("col", 1))
    rxb = lax.ppermute(sxb, "slab", pairs("slab", 1))
    rxa = lax.ppermute(sxa, "slab", pairs("slab", 0))
    return rya, ryb, rxb, rxa


def to_rows(array):
    lead = array.shape[:-3]
    split = array.reshape(lead + (2, 2, 2, LANES))
    return jnp.swapaxes(split, -3, -2).reshape(-1, LANES)


def from_rows(rows):
    split = rows.reshape(3, RHS, 2, 2, 2, LANES)
    return jnp.swapaxes(split, -3, -2).reshape(3, RHS, 2, 2, 2 * LANES)


def per_device(
    cell_rhs, well_rhs, cell_colors, incoming, pivot_inv,
    perf_cell, perf_well, perf_out, perf_in, well_pivot_inv,
):
    rhs = to_rows(cell_rhs)
    colors_in = to_rows(cell_colors)
    inc = to_rows(incoming)
    piv = to_rows(pivot_inv)
    place = perf_cell.reshape(1, PERFS)
    well = perf_well.reshape(1, PERFS)
    out_blocks = jnp.transpose(perf_out, (1, 2, 0))
    in_blocks = jnp.transpose(perf_in, (1, 2, 0))
    well_side = jnp.transpose(well_rhs, (1, 0, 2))
    wells = lax.axis_size("slab") * lax.axis_size("col") * well_rhs.shape[0]
    tiles = pltpu.VMEM((72, LANES), jnp.float32)
    color_tile = pltpu.VMEM((8, LANES), jnp.int32)
    whole = pltpu.VMEM((3 * RHS * SLICE, LANES), jnp.float32)
    steps = RHS // ROWS

    def local(cls, base, coef, s, name):
        def body(*refs):
            local_kernel(cls, *refs)

        return call(body, PLANES, (base, coef, *s[:2]), name=name)

    q_even, *s = call(
        first_kernel,
        [PLANES] + [FACE] * 4,
        [pltpu.with_memory_space_constraint(v, pltpu.HBM) for v in (rhs, piv, colors_in)],
        [whole, tiles, color_tile, tiles, color_tile, pltpu.SemaphoreType.DMA((2 + 3 * steps,))],
        name="even_rhs",
        hbm=(0, 1, 2),
    )
    halo = exchange(*s)
    part, fwd, bwd, colors, well_piv = call(
        second_kernel,
        [PLANES, COEF, COEF, jax.ShapeDtypeStruct((8, LANES), jnp.int32), f32(8, LANES)],
        (rhs, piv, colors_in, inc, *s[:2], jnp.transpose(well_pivot_inv, (1, 0, 2))),
        [tiles, color_tile] + [pltpu.VMEM((54 * 8, LANES), jnp.float32)] * 2,
        name="blocks_and_local",
    )
    t_odd, *s = call(
        forward_one_kernel,
        [PLANES] + [FACE_PLUS] * 4,
        (part, fwd, colors, *halo, place, well, in_blocks),
        name="forward_one",
    )
    part = local(0, q_even, fwd, s, "forward_two_local")
    halo = exchange(*s)
    u_even, *s, extra = call(
        forward_two_kernel,
        [PLANES] + [FACE] * 4 + [f32(4, EXTRA, LANES)],
        (part, fwd, colors, *halo),
        name="forward_two",
    )
    part = local(1, t_odd, fwd, s, "forward_three_local")
    halo = exchange(*s)
    even, odd, keep, send, *s = call(
        forward_three_kernel,
        [PLANES, PLANES, f32(wells // 2, WIDE), f32(wells // 2, WIDE), FACE, FACE],
        (part, t_odd, q_even, u_even, fwd, colors, *halo, place, well, out_blocks, well_side, well_piv),
        [pltpu.VMEM((3 * RHS, PERFS), jnp.float32)],
        name="forward_three_wells",
    )
    halo = [lax.ppermute(face, "col", pairs("col", i)) for i, face in enumerate(s)]
    part = f32(wells // 8, WIDE)
    blocks = call(blocks_kernel, [part] * 4, (keep, swap(send, "slab", 1)), name="core_sum")
    moved = [swap(blocks[m], "slab", 8 * m) for m in (1, 2, 3)]
    mine = call(sum_kernel, part, (blocks[0], *moved), name="z_sum")
    moved = [swap(mine, "slab", 2 * m) for m in (1, 2, 3)]
    mine, sxb, sxa = call(
        y_sum_kernel, [part, FACE, FACE], (mine, *moved, odd, *halo), name="y_sum", hbm=(5, 6)
    )
    halo.append(lax.ppermute(sxb, "slab", pairs("slab", 1)))
    halo.append(lax.ppermute(sxa, "slab", pairs("slab", 0)))
    solved = call(
        solve_kernel,
        f32(wells // 8, 3 * LANES),
        (mine, *[swap(mine, "col", m) for m in (1, 2, 3)]),
        name="solve_wells",
    )
    moved = [swap(solved, "slab", 8 * m) for m in (1, 2, 3)]
    near = call(stack_kernel, f32(wells // 2, 3 * LANES), (solved, *moved), name="stack")
    far = swap(near, "slab", 1)
    u_even, x_odd, *s, own_wells = call(
        backward_two_kernel,
        [PLANES, PLANES] + [FACE] * 4 + [f32(3, 2, RHS)],
        (near, far, even, odd, colors, bwd, *halo, extra, place, well, in_blocks),
        [pltpu.VMEM((3 * RHS, PERFS), jnp.float32)]
        + [pltpu.VMEM(PLANES.shape, jnp.float32)] * 2
        + [pltpu.VMEM(FACE.shape, jnp.float32)] * 4,
        name="well_fix_backward_two",
    )
    part = local(1, x_odd, bwd, s, "backward_one_local")
    halo = exchange(*s)

    def backward_one(*refs):
        remote_kernel(1, 1, *refs)

    v_odd, *s = call(
        backward_one, [PLANES] + [FACE] * 4, (part, bwd, colors, *halo), name="backward_one"
    )
    part = local(0, u_even, bwd, s, "backward_zero_local")
    halo = exchange(*s)
    rows = call(
        last_kernel,
        f32(3 * RHS * SLICE, LANES),
        (part, u_even, x_odd, v_odd, bwd, colors, *halo),
        [whole, pltpu.SemaphoreType.DMA((3 * steps,))],
        name="backward_zero",
        hbm_out=True,
    )
    return from_rows(rows), jnp.transpose(own_wells, (1, 0, 2))


def solution(mesh):
    placed = (
        P(None, None, "slab", "col", None),
        P(("slab", "col"), None, None),
        P("slab", "col", None),
        P(None, None, None, "slab", "col", None),
        P(None, None, "slab", "col", None),
        P(("slab", "col")),
        P(("slab", "col")),
        P(("slab", "col"), None, None),
        P(("slab", "col"), None, None),
        P(("slab", "col"), None, None),
    )
    return jax.shard_map(
        per_device,
        mesh=mesh,
        in_specs=placed,
        out_specs=(P(None, None, "slab", "col", None), P(("slab", "col"), None, None)),
        check_vma=False,
    )
```

```python
import jax
import jax.numpy as jnp
from jax import lax
from jax.experimental import pallas as pl
from jax.experimental.pallas import tpu as pltpu
from jax.sharding import PartitionSpec as P

RHS = 128
LANES = 128
ROWS = 64
SLICE = 8
FACE_RX, FACE_LX, FACE_RY, FACE_LY, FACE_ZU, FACE_ZS = range(6)
PERFS = 64
SENT = 6 * RHS
EXTRA = 16
WIDE = 4 * LANES


def f32(*shape):
    return jax.ShapeDtypeStruct(shape, jnp.float32)


PLANES = f32(4, 3, RHS, LANES)
FACE = f32(SENT, LANES)
FACE_PLUS = f32(SENT + EXTRA, LANES)
PAST = (16, 8, 0, 0)
FACES = [f32(SENT + past, LANES) for past in PAST]
FACES_PLUS = [f32(SENT + EXTRA + past, LANES) for past in PAST]
COEF = f32(8, 54, LANES)


def call(body, outs, args, scratch=(), name=None, hbm=(), hbm_out=False):
    spaces = [pltpu.HBM if i in hbm else pltpu.VMEM for i in range(len(args))]
    out_space = pltpu.HBM if hbm_out else pltpu.VMEM
    return pl.pallas_call(
        body,
        out_shape=outs,
        in_specs=[pl.BlockSpec(memory_space=space) for space in spaces],
        out_specs=jax.tree.map(lambda _: pl.BlockSpec(memory_space=out_space), outs),
        scratch_shapes=list(scratch),
        compiler_params=pltpu.CompilerParams(vmem_limit_bytes=16 * 1024 * 1024),
        cost_estimate=pl.CostEstimate(flops=1_000_000, bytes_accessed=2_000_000, transcendentals=0),
        name=name,
    )(*args)


def spots():
    return lax.rem(lax.axis_index("slab"), 2), lax.rem(lax.axis_index("col"), 2)


def line_xy(tx, ty):
    sp, cp = spots()
    x = sp if tx else 1 - sp
    y = cp if ty else 1 - cp
    return x, y


def xor(a, b):
    return a + b - 2 * a * b


def lane_iota(rows):
    return lax.broadcasted_iota(jnp.int32, (rows, LANES), 1)


def pick(values, index):
    return jnp.take_along_axis(values, index, axis=1)


def split_z(low, high, odd):
    lane = lane_iota(low.shape[0])
    index = (2 * lane + odd) & (LANES - 1)
    return jnp.where(lane < LANES // 2, pick(low, index), pick(high, index))


def join_z(even, odd, half):
    lane = lane_iota(even.shape[0])
    index = half * (LANES // 2) + (lane >> 1)
    return jnp.where((lane & 1) == 0, pick(even, index), pick(odd, index))


def line_rows(ref, start, count):
    return ref[pl.ds(start, count, stride=SLICE), :]


def tile_split(tile):
    lane = lane_iota(SLICE)
    part = (lax.broadcasted_iota(jnp.int32, (SLICE, LANES), 0) >> 1) & 1
    even = pick(tile, (2 * lane) & (LANES - 1))
    odd = pick(tile, (2 * lane + 1) & (LANES - 1))
    low = lane < LANES // 2
    of_even = jnp.where(low, even, pltpu.roll(even, SLICE - 2, 0))
    of_odd = jnp.where(low, pltpu.roll(odd, 2, 0), odd)
    return jnp.where(part == 0, of_even, of_odd)


def split_tiles(source, target, count):
    for row in range(count):
        target[row * 8 : row * 8 + 8, :] = tile_split(source[row * 8 : row * 8 + 8, :])


def pivoted(rhs_ref, piv, cls, tx, ty, rows):
    x, y = line_xy(tx, ty)
    odd = xor(xor(x, y), cls)
    planes = []
    for a in range(3):
        base = (a * RHS + rows) * SLICE + x * 4 + y
        planes.append(
            split_z(line_rows(rhs_ref, base, ROWS), line_rows(rhs_ref, base + 2, ROWS), odd)
        )
    return [
        piv[0 * 3 + b] * planes[0] + piv[1 * 3 + b] * planes[1] + piv[2 * 3 + b] * planes[2]
        for b in range(3)
    ]


def class_rows(ref, cls, tx, ty, count):
    x, y = line_xy(tx, ty)
    odd = xor(xor(x, y), cls)
    return ref[pl.ds(x * 4 + odd * 2 + y, count, stride=SLICE), :]


def chunks(body):
    def step(i, carry):
        body(pl.multiple_of(i * ROWS, ROWS))
        return carry

    lax.fori_loop(0, RHS // ROWS, step, 0)


def lines():
    return [(tx, ty) for tx in range(2) for ty in range(2)]


def at_face(t, b, rows, count=ROWS):
    return pl.ds((t * 3 + b) * RHS + rows, count)


def from_sy(sya, syb, rows):
    return lambda tx, ty, a: (syb if ty else sya)[at_face(tx, a, rows), :]


def from_halos(halos, rows):
    rya, ryb, rxb, rxa = halos
    return (
        lambda tx, ty, a: (rxb if tx else rxa)[at_face(ty, a, rows), :],
        lambda tx, ty, a: (ryb if ty else rya)[at_face(tx, a, rows), :],
    )


def take(acc, coef, d, face, a, value):
    for b in range(3):
        row = face * 9 + a * 3 + b
        acc[b] = acc[b] - coef[d, row : row + 1, :] * value


def add_local(acc, coef, cls, tx, ty, get):
    x, y = line_xy(tx, ty)
    odd = xor(xor(x, y), cls)
    index = (lane_iota(ROWS) + (LANES - 1) + 2 * odd) & (LANES - 1)
    d = cls * 4 + tx * 2 + ty
    for a in range(3):
        center = get(tx, ty, a)
        take(acc, coef, d, FACE_LX, a, get(1 - tx, ty, a))
        take(acc, coef, d, FACE_LY, a, get(tx, 1 - ty, a))
        take(acc, coef, d, FACE_ZU, a, center)
        take(acc, coef, d, FACE_ZS, a, pick(center, index))
    return acc


def add_remote(acc, coef, cls, tx, ty, get_x, get_y):
    d = cls * 4 + tx * 2 + ty
    for a in range(3):
        take(acc, coef, d, FACE_RX, a, get_x(tx, ty, a))
        take(acc, coef, d, FACE_RY, a, get_y(tx, ty, a))
    return acc


def store_faces(faces, tx, ty, b, rows, value):
    sya, syb, sxb, sxa = faces
    (syb if ty else sya)[at_face(tx, b, rows), :] = value
    (sxb if tx else sxa)[at_face(ty, b, rows), :] = value


def first_kernel(
    rhs_hbm, piv_hbm, colors_hbm, q_ref, sya, syb, sxb, sxa,
    rhs_ref, piv_ref, colors_ref, tiles, color_tile, sems,
):
    steps = RHS // ROWS

    def rhs_copy(i, a):
        part = pl.ds((a * RHS + i * ROWS) * SLICE, ROWS * SLICE)
        return pltpu.make_async_copy(rhs_hbm.at[part], rhs_ref.at[part], sems.at[2 + i * 3 + a])

    piv_copy = pltpu.make_async_copy(piv_hbm, piv_ref, sems.at[0])
    color_copy = pltpu.make_async_copy(colors_hbm, colors_ref, sems.at[1])
    piv_copy.start()
    color_copy.start()
    for i in range(steps):
        for a in range(3):
            rhs_copy(i, a).start()
    piv_copy.wait()
    split_tiles(piv_ref, tiles, 9)
    color_copy.wait()
    color_tile[...] = tile_split(colors_ref[...])

    def step(i, carry):
        for a in range(3):
            rhs_copy(i, a).wait()
        rows = pl.multiple_of(i * ROWS, ROWS)
        for tx, ty in lines():
            piv_rows = class_rows(tiles, 0, tx, ty, 9)
            piv = [piv_rows[e : e + 1] for e in range(9)]
            mask = class_rows(color_tile, 0, tx, ty, 1) == 0
            for b, value in enumerate(pivoted(rhs_ref, piv, 0, tx, ty, rows)):
                q_ref[tx * 2 + ty, b, pl.ds(rows, ROWS), :] = value
                store_faces((sya, syb, sxb, sxa), tx, ty, b, rows, jnp.where(mask, value, 0.0))
        return carry

    lax.fori_loop(0, steps, step, 0)


def second_kernel(
    rhs_ref, piv_ref, colors_ref, inc_ref, sya, syb, well_piv_ref,
    part_ref, fwd_ref, bwd_ref, cls_colors_ref, well_rows_ref, tiles, color_tile, raw, folded,
):
    well_rows_ref[...] = jnp.zeros(well_rows_ref.shape, jnp.float32)
    for a in range(3):
        well_rows_ref[0:2, a * 3 : a * 3 + 3] = well_piv_ref[a]
    split_tiles(piv_ref, tiles, 9)
    color_tile[...] = tile_split(colors_ref[...])
    spot = lax.broadcasted_iota(jnp.int32, (SLICE, LANES), 0)
    lane = lane_iota(SLICE)
    x_low = (spot >> 2) == 0
    y_low = (spot & 1) == 0
    z_even = ((spot >> 1) & 1) == 0
    edge = (z_even & (lane == 0)) | (jnp.logical_not(z_even) & (lane == LANES - 1))

    slab, col = lax.axis_index("slab"), lax.axis_index("col")
    inside = [
        jnp.where(low, jnp.where(at == 0, 0.0, 1.0), jnp.where(at == last, 0.0, 1.0))
        for low, at, last in (
            (x_low, slab, lax.axis_size("slab") - 1),
            (y_low, col, lax.axis_size("col") - 1),
        )
    ]

    def source(face, entry):
        row = (face * 9 + entry) * 8
        return tile_split(inc_ref[row : row + 8, :])

    piv = [tiles[i * 8 : i * 8 + 8, :] for i in range(9)]
    for group, (first, second, low) in enumerate(((0, 1, x_low), (2, 3, y_low), (5, 4, z_even))):
        one = [None] * 9
        two = [None] * 9
        for entry in range(9):
            p, q = source(first, entry), source(second, entry)
            one[entry] = jnp.where(low, p, q)
            two[entry] = jnp.where(low, q, p)
            if group < 2:
                one[entry] = one[entry] * inside[group]
            else:
                two[entry] = jnp.where(edge, 0.0, two[entry])
        for which, block in ((0, one), (1, two)):
            face = group * 2 + which
            for a in range(3):
                for b in range(3):
                    row = (face * 9 + a * 3 + b) * 8
                    raw[row : row + 8, :] = block[a * 3 + b]
                    folded[row : row + 8, :] = (
                        block[a * 3] * piv[b]
                        + block[a * 3 + 1] * piv[3 + b]
                        + block[a * 3 + 2] * piv[6 + b]
                    )
    for cls in range(2):
        for tx, ty in lines():
            d = cls * 4 + tx * 2 + ty
            fwd_ref[d] = class_rows(folded, cls, tx, ty, 54)
            bwd_ref[d] = class_rows(raw, cls, tx, ty, 54)
            cls_colors_ref[d : d + 1, :] = class_rows(color_tile, cls, tx, ty, 1)
    for tx, ty in lines():
        piv_rows = class_rows(tiles, 1, tx, ty, 9)
        piv1 = [piv_rows[i : i + 1] for i in range(9)]

        def body(rows, tx=tx, ty=ty, piv1=piv1):
            acc = pivoted(rhs_ref, piv1, 1, tx, ty, rows)
            acc = add_local(acc, fwd_ref, 1, tx, ty, from_sy(sya, syb, rows))
            for b in range(3):
                part_ref[tx * 2 + ty, b, pl.ds(rows, ROWS), :] = acc[b]

        chunks(body)


def local_kernel(cls, base_ref, coef_ref, sya, syb, part_ref):
    for tx, ty in lines():
        n = tx * 2 + ty

        def body(rows, tx=tx, ty=ty, n=n):
            acc = [base_ref[n, b, pl.ds(rows, ROWS), :] for b in range(3)]
            acc = add_local(acc, coef_ref, cls, tx, ty, from_sy(sya, syb, rows))
            for b in range(3):
                part_ref[n, b, pl.ds(rows, ROWS), :] = acc[b]

        chunks(body)


def remote_kernel(cls, color, part_ref, coef_ref, colors_ref, rya, ryb, rxb, rxa, full_ref, *faces):
    for tx, ty in lines():
        n = tx * 2 + ty
        d = cls * 4 + n

        def body(rows, tx=tx, ty=ty, n=n, d=d):
            acc = [part_ref[n, b, pl.ds(rows, ROWS), :] for b in range(3)]
            acc = add_remote(acc, coef_ref, cls, tx, ty, *from_halos((rya, ryb, rxb, rxa), rows))
            mask = colors_ref[d : d + 1, :] == color
            for b in range(3):
                full_ref[n, b, pl.ds(rows, ROWS), :] = acc[b]
                store_faces(faces, tx, ty, b, rows, jnp.where(mask, acc[b], 0.0))

        chunks(body)


def perf_place(perf_cell):
    sp, cp = spots()
    x = perf_cell >> 9
    y = (perf_cell >> 8) & 1
    z = perf_cell & 255
    cls = (x + y + z) & 1
    tx = (x + 1 - sp) & 1
    ty = (y + 1 - cp) & 1
    return (cls * 4 + tx * 2 + ty) * LANES + (z >> 1)


def forward_one_kernel(
    part_ref, coef_ref, colors_ref, rya, ryb, rxb, rxa, perf_cell_ref, perf_well_ref, perf_in_ref,
    full_ref, sya, syb, sxb, sxa, table_ref,
):
    faces = (sya, syb, sxb, sxa)
    table_ref[...] = jnp.zeros((EXTRA, LANES), jnp.float32)
    table_ref[0:1, 0:PERFS] = perf_place(perf_cell_ref[...]).astype(jnp.float32)
    table_ref[1:2, 0:PERFS] = perf_well_ref[...].astype(jnp.float32)
    for a in range(3):
        table_ref[2 + a * 3 : 5 + a * 3, 0:PERFS] = perf_in_ref[a]
    remote_kernel(1, 1, part_ref, coef_ref, colors_ref, rya, ryb, rxb, rxa, full_ref, *faces)
    for target, start, step in ((sya, 4, 2), (syb, 5, 2), (sxb, 6, 1), (sxa, 4, 1)):
        target[SENT : SENT + EXTRA, :] = table_ref[...]
        if target.shape[0] > SENT + EXTRA:
            target[SENT + EXTRA :, :] = jnp.zeros((target.shape[0] - SENT - EXTRA, LANES), jnp.float32)
        for t in range(2):
            d = start + t * step
            row = SENT + 11 + t
            target[row : row + 1, :] = colors_ref[d : d + 1, :].astype(jnp.float32)


def forward_two_kernel(
    part_ref, coef_ref, colors_ref, rya, ryb, rxb, rxa, table_ref,
    full_ref, sya, syb, sxb, sxa, tables_ref,
):
    faces = (sya, syb, sxb, sxa)
    remote_kernel(0, 2, part_ref, coef_ref, colors_ref, rya, ryb, rxb, rxa, full_ref, *faces)
    tables_ref[0] = table_ref[...]
    for i, ref in enumerate((rya, ryb, rxb, rxa)):
        tables_ref[i + 1] = ref[SENT : SENT + EXTRA, :]


def hot(index, count, start=0, step=LANES):
    rows = lax.broadcasted_iota(jnp.int32, (count, index.shape[1]), 0)
    rows = start + (rows >> 7) * step + (rows & (LANES - 1))
    return jnp.where(rows == index, 1.0, 0.0).astype(jnp.bfloat16)


def halves(values):
    high = values.astype(jnp.bfloat16)
    return high, (values - high.astype(jnp.float32)).astype(jnp.bfloat16)


def dot_ones(parts, ones, dims):
    return sum(
        lax.dot_general(part, ones, (dims, ((), ())), preferred_element_type=jnp.float32)
        for part in parts
    )


def well_bits():
    slab = lax.axis_index("slab")
    return slab & 1, slab >> 3


def forward_three_kernel(
    part_ref, t_ref, q_ref, u_ref, coef_ref, colors_ref, rya, ryb, rxb, rxa,
    perf_cell_ref, perf_well_ref, perf_out_ref, well_rhs_ref, well_piv_ref,
    even_ref, odd_ref, keep_ref, send_ref, sya, syb, at_ref,
):
    for tx, ty in lines():
        n = tx * 2 + ty
        d = 4 + n

        def body(rows, tx=tx, ty=ty, n=n, d=d):
            part = pl.ds(rows, ROWS)
            acc = [part_ref[n, b, part, :] for b in range(3)]
            acc = add_remote(acc, coef_ref, 1, tx, ty, *from_halos((rya, ryb, rxb, rxa), rows))
            is_one = colors_ref[d : d + 1, :] == 1
            is_two = colors_ref[n : n + 1, :] == 2
            for b in range(3):
                value = jnp.where(is_one, t_ref[n, b, part, :], acc[b])
                odd_ref[n, b, part, :] = value
                (syb if ty else sya)[at_face(tx, b, rows), :] = value
                even_ref[n, b, part, :] = jnp.where(is_two, u_ref[n, b, part, :], q_ref[n, b, part, :])

        chunks(body)
    place = perf_place(perf_cell_ref[...])
    at_perfs = None
    for cls, ref in ((0, even_ref), (1, odd_ref)):
        for tx in range(2):
            planes = [ref[tx * 2 + ty].reshape(3 * RHS, LANES) for ty in range(2)]
            ones = hot(place, 2 * LANES, (cls * 4 + tx * 2) * LANES)
            term = dot_ones(halves(jnp.concatenate(planes, axis=1)), ones, ((1,), (0,)))
            at_perfs = term if at_perfs is None else at_perfs + term
    for b in range(3):
        at_ref[b * RHS : (b + 1) * RHS, :] = sum(
            perf_out_ref[a, b : b + 1, :] * at_perfs[a * RHS : (a + 1) * RHS] for a in range(3)
        )
    core, _ = well_bits()
    device = lax.axis_index("slab") * lax.axis_size("col") + lax.axis_index("col")
    parts = halves(at_ref[...])
    count = keep_ref.shape[0]
    for ref, start in ((keep_ref, core * count), (send_ref, (1 - core) * count)):
        wells = hot(perf_well_ref[...], count, start)
        total = sum(
            lax.dot_general(wells, part, (((1,), (1,)), ((), ())), preferred_element_type=jnp.float32)
            for part in parts
        )
        spot = lax.broadcasted_iota(jnp.int32, (count, LANES), 0) + start
        is_own = [spot == device * 2 + j for j in range(2)]
        for b in range(3):
            own = sum(jnp.where(is_own[j], well_rhs_ref[b, j : j + 1, :], 0.0) for j in range(2))
            ref[:, b * LANES : (b + 1) * LANES] = own - total[:, b * LANES : (b + 1) * LANES]
        ref[:, 3 * LANES :] = sum(
            jnp.where(is_own[j], well_piv_ref[j : j + 1, :], 0.0) for j in range(2)
        )


def blocks_kernel(keep_ref, got_ref, *outs):
    _, z_spot = well_bits()
    count = outs[0].shape[0]
    for m, out in enumerate(outs):
        rows = pl.ds(pl.multiple_of((z_spot ^ m) * count, count), count)
        out[...] = keep_ref[rows, :] + got_ref[rows, :]


def sum_kernel(*refs):
    a, b, c, d = refs[:4]
    refs[-1][...] = (a[...] + b[...]) + (c[...] + d[...])


def y_sum_kernel(a, b, c, d, odd_ref, rya, ryb, out_ref, sxb, sxa):
    sum_kernel(a, b, c, d, out_ref)
    for tx, ty in lines():
        for b_ in range(3):
            (sxb if tx else sxa)[at_face(ty, b_, 0, RHS), :] = odd_ref[tx * 2 + ty, b_]


def stack_kernel(*refs):
    count = refs[0].shape[0]
    for i, ref in enumerate(refs[:4]):
        refs[-1][i * count : (i + 1) * count, :] = ref[...]


def solve_kernel(own_ref, one_ref, two_ref, three_ref, out_ref):
    total = (own_ref[...] + one_ref[...]) + (two_ref[...] + three_ref[...])
    for b in range(3):
        out_ref[:, b * LANES : (b + 1) * LANES] = sum(
            total[:, 3 * LANES + a * 3 + b : 3 * LANES + a * 3 + b + 1]
            * total[:, a * LANES : (a + 1) * LANES]
            for a in range(3)
        )


def backward_two_kernel(
    wells_ref, other_ref, even_ref, odd_ref, colors_ref, coef_ref, rya, ryb, rxb, rxa, tables_ref,
    u_ref, x_odd_ref, sya, syb, sxb, sxa, own_wells_ref, fix_ref, x_even_ref, three_ref, hya, hyb, hxb, hxa,
):
    core, z_spot = well_bits()

    def place_of_well(well):
        return (((well >> 7) ^ core) << 7) | ((((well >> 5) & 3) ^ z_spot) << 5) | (well & 31)

    device = lax.axis_index("slab") * lax.axis_size("col") + lax.axis_index("col")
    for j in range(2):
        spot = place_of_well(device * 2 + j)
        rows = lax.broadcasted_iota(jnp.int32, (LANES, LANES), 0)
        for b in range(3):
            lanes = slice(b * LANES, (b + 1) * LANES)
            found = jnp.where(rows == spot, wells_ref[:, lanes], 0.0)
            found = found + jnp.where(rows + LANES == spot, other_ref[:, lanes], 0.0)
            own_wells_ref[b, j : j + 1, :] = jnp.sum(found, axis=0, keepdims=True)
    wells = halves(jnp.concatenate([wells_ref[...].T, other_ref[...].T], axis=1))
    tables = [tables_ref[i] for i in range(5)]
    for first in (0, 2, 4):
        pair = tables[first : first + 2]
        well = jnp.concatenate([table[1:2] for table in pair], axis=1).astype(jnp.int32)
        at_perfs = dot_ones(wells, hot(place_of_well(well), 2 * LANES), ((1,), (0,)))
        for i, table in enumerate(pair):
            for b in range(3):
                fix = sum(
                    table[2 + a * 3 + b : 3 + a * 3 + b]
                    * at_perfs[a * RHS : (a + 1) * RHS, i * LANES : (i + 1) * LANES]
                    for a in range(3)
                )
                for part, value in enumerate(halves(fix)):
                    lanes = slice(part * LANES, (part + 1) * LANES)
                    fix_ref[first + i, b * RHS : (b + 1) * RHS, lanes] = value

    def spread(group, start, step):
        place = tables[group][0:1].astype(jnp.int32)
        ones = hot(place, 2 * LANES, start * LANES, step * LANES)
        return lax.dot_general(
            fix_ref[group], jnp.concatenate([ones, ones], axis=1),
            (((1,), (1,)), ((), ())), preferred_element_type=jnp.float32,
        )

    for cls, ref, out in ((1, odd_ref, x_odd_ref), (0, even_ref, x_even_ref)):
        for tx in range(2):
            fix = spread(0, cls * 4 + tx * 2, 1)
            for ty in range(2):
                n = tx * 2 + ty
                d = cls * 4 + n
                for b in range(3):
                    value = ref[n, b] - fix[b * RHS : (b + 1) * RHS, ty * LANES : (ty + 1) * LANES]
                    out[n, b] = value
                    if cls == 1:
                        three_ref[n, b] = jnp.where(colors_ref[d : d + 1, :] == 3, value, 0.0)
    for i, (halo, out, start, step) in enumerate(
        ((rya, hya, 4, 2), (ryb, hyb, 5, 2), (rxb, hxb, 6, 1), (rxa, hxa, 4, 1))
    ):
        fix = spread(i + 1, start, step)
        for t in range(2):
            mask = tables[i + 1][11 + t : 12 + t] == 3.0
            for b in range(3):
                value = halo[at_face(t, b, 0, RHS), :]
                value = value - fix[b * RHS : (b + 1) * RHS, t * LANES : (t + 1) * LANES]
                out[at_face(t, b, 0, RHS), :] = jnp.where(mask, value, 0.0)
    for tx, ty in lines():
        n = tx * 2 + ty

        def body(rows, tx=tx, ty=ty, n=n):
            acc = [x_even_ref[n, b, pl.ds(rows, ROWS), :] for b in range(3)]
            acc = add_local(
                acc, coef_ref, 0, tx, ty,
                lambda i, j, a: three_ref[i * 2 + j, a, pl.ds(rows, ROWS), :],
            )
            acc = add_remote(acc, coef_ref, 0, tx, ty, *from_halos((hya, hyb, hxb, hxa), rows))
            mask = colors_ref[n : n + 1, :] == 2
            for b in range(3):
                u_ref[n, b, pl.ds(rows, ROWS), :] = acc[b]
                store_faces((sya, syb, sxb, sxa), tx, ty, b, rows, jnp.where(mask, acc[b], 0.0))

        chunks(body)


def last_kernel(
    part_ref, u_ref, odd_three, odd_v, coef_ref, colors_ref, rya, ryb, rxb, rxa, out_hbm, out_ref, sems
):
    steps = RHS // ROWS

    def out_copy(i, b):
        part = pl.ds((b * RHS + i * ROWS) * SLICE, ROWS * SLICE)
        return pltpu.make_async_copy(out_ref.at[part], out_hbm.at[part], sems.at[i * 3 + b])

    def step(i, carry):
        rows = pl.multiple_of(i * ROWS, ROWS)
        part = pl.ds(rows, ROWS)
        for tx, ty in lines():
            n = tx * 2 + ty
            x, y = line_xy(tx, ty)
            flip = xor(x, y)
            acc = [part_ref[n, b, part, :] for b in range(3)]
            acc = add_remote(acc, coef_ref, 0, tx, ty, *from_halos((rya, ryb, rxb, rxa), rows))
            is_two = colors_ref[n : n + 1, :] == 2
            is_one = colors_ref[4 + n : 5 + n, :] == 1
            for b in range(3):
                even = jnp.where(is_two, u_ref[n, b, part, :], acc[b])
                odd = jnp.where(is_one, odd_v[n, b, part, :], odd_three[n, b, part, :])
                z_even = jnp.where(flip == 1, odd, even)
                z_odd = jnp.where(flip == 1, even, odd)
                for half in range(2):
                    start = (b * RHS + rows) * SLICE + x * 4 + half * 2 + y
                    out_ref[pl.ds(start, ROWS, stride=SLICE), :] = join_z(z_even, z_odd, half)
        for b in range(3):
            out_copy(i, b).start()
        return carry

    lax.fori_loop(0, steps, step, 0)
    for i in range(steps):
        for b in range(3):
            out_copy(i, b).wait()


def pairs(axis, second):
    count = lax.axis_size(axis)
    found = []
    for i in range(second, count, 2):
        found += [(i, (i + 1) % count), ((i + 1) % count, i)]
    return found


def swap(value, axis, mask):
    return lax.ppermute(value, axis, [(i, i ^ mask) for i in range(lax.axis_size(axis))])


def exchange(sya, syb, sxb, sxa):
    rya = lax.ppermute(sya, "col", pairs("col", 0))
    ryb = lax.ppermute(syb, "col", pairs("col", 1))
    rxb = lax.ppermute(sxb, "slab", pairs("slab", 1))
    rxa = lax.ppermute(sxa, "slab", pairs("slab", 0))
    return rya, ryb, rxb, rxa


def to_rows(array):
    lead = array.shape[:-3]
    split = array.reshape(lead + (2, 2, 2, LANES))
    return jnp.swapaxes(split, -3, -2).reshape(-1, LANES)


def from_rows(rows):
    split = rows.reshape(3, RHS, 2, 2, 2, LANES)
    return jnp.swapaxes(split, -3, -2).reshape(3, RHS, 2, 2, 2 * LANES)


def per_device(
    cell_rhs, well_rhs, cell_colors, incoming, pivot_inv,
    perf_cell, perf_well, perf_out, perf_in, well_pivot_inv,
):
    rhs = to_rows(cell_rhs)
    colors_in = to_rows(cell_colors)
    inc = to_rows(incoming)
    piv = to_rows(pivot_inv)
    place = perf_cell.reshape(1, PERFS)
    well = perf_well.reshape(1, PERFS)
    out_blocks = jnp.transpose(perf_out, (1, 2, 0))
    in_blocks = jnp.transpose(perf_in, (1, 2, 0))
    well_side = jnp.transpose(well_rhs, (1, 0, 2))
    wells = lax.axis_size("slab") * lax.axis_size("col") * well_rhs.shape[0]
    tiles = pltpu.VMEM((72, LANES), jnp.float32)
    color_tile = pltpu.VMEM((8, LANES), jnp.int32)
    whole = pltpu.VMEM((3 * RHS * SLICE, LANES), jnp.float32)
    steps = RHS // ROWS

    def local(cls, base, coef, s, name):
        def body(*refs):
            local_kernel(cls, *refs)

        return call(body, PLANES, (base, coef, *s[:2]), name=name)

    q_even, *s = call(
        first_kernel,
        [PLANES] + FACES,
        [pltpu.with_memory_space_constraint(v, pltpu.HBM) for v in (rhs, piv, colors_in)],
        [whole, tiles, color_tile, tiles, color_tile, pltpu.SemaphoreType.DMA((2 + 3 * steps,))],
        name="even_rhs",
        hbm=(0, 1, 2),
    )
    halo = exchange(*s)
    part, fwd, bwd, colors, well_piv = call(
        second_kernel,
        [PLANES, COEF, COEF, jax.ShapeDtypeStruct((8, LANES), jnp.int32), f32(8, LANES)],
        (rhs, piv, colors_in, inc, *s[:2], jnp.transpose(well_pivot_inv, (1, 0, 2))),
        [tiles, color_tile] + [pltpu.VMEM((54 * 8, LANES), jnp.float32)] * 2,
        name="blocks_and_local",
    )
    t_odd, *s, table = call(
        forward_one_kernel,
        [PLANES] + FACES_PLUS + [f32(EXTRA, LANES)],
        (part, fwd, colors, *halo, place, well, in_blocks),
        name="forward_one",
    )
    part = local(0, q_even, fwd, s, "forward_two_local")
    halo = exchange(*s)
    u_even, *s, tables = call(
        forward_two_kernel,
        [PLANES] + FACES + [f32(5, EXTRA, LANES)],
        (part, fwd, colors, *halo, table),
        name="forward_two",
    )
    part = local(1, t_odd, fwd, s, "forward_three_local")
    halo = exchange(*s)
    even, odd, keep, send, *s = call(
        forward_three_kernel,
        [PLANES, PLANES, f32(wells // 2, WIDE), f32(wells // 2, WIDE), FACE_PLUS, FACE_PLUS],
        (part, t_odd, q_even, u_even, fwd, colors, *halo, place, well, out_blocks, well_side, well_piv),
        [pltpu.VMEM((3 * RHS, PERFS), jnp.float32)],
        name="forward_three_wells",
    )
    halo = [lax.ppermute(face, "col", pairs("col", i)) for i, face in enumerate(s)]
    part = f32(wells // 8, WIDE)
    blocks = call(blocks_kernel, [part] * 4, (keep, swap(send, "slab", 1)), name="core_sum")
    moved = [swap(blocks[m], "slab", 8 * m) for m in (1, 2, 3)]
    mine = call(sum_kernel, part, (blocks[0], *moved), name="z_sum")
    moved = [swap(mine, "slab", 2 * m) for m in (1, 2, 3)]
    mine, sxb, sxa = call(
        y_sum_kernel, [part, FACE, FACE], (mine, *moved, odd, *halo), name="y_sum", hbm=(5, 6)
    )
    halo.append(lax.ppermute(sxb, "slab", pairs("slab", 1)))
    halo.append(lax.ppermute(sxa, "slab", pairs("slab", 0)))
    solved = call(
        solve_kernel,
        f32(wells // 8, 3 * LANES),
        (mine, *[swap(mine, "col", m) for m in (1, 2, 3)]),
        name="solve_wells",
    )
    moved = [swap(solved, "slab", 8 * m) for m in (1, 2, 3)]
    near = call(stack_kernel, f32(wells // 2, 3 * LANES), (solved, *moved), name="stack")
    far = swap(near, "slab", 1)
    u_even, x_odd, *s, own_wells = call(
        backward_two_kernel,
        [PLANES, PLANES] + FACES + [f32(3, 2, RHS)],
        (near, far, even, odd, colors, bwd, *halo, tables),
        [pltpu.VMEM((5, 3 * RHS, 2 * LANES), jnp.bfloat16)]
        + [pltpu.VMEM(PLANES.shape, jnp.float32)] * 2
        + [pltpu.VMEM(FACE.shape, jnp.float32)] * 4,
        name="well_fix_backward_two",
    )
    part = local(1, x_odd, bwd, s, "backward_one_local")
    halo = exchange(*s)

    def backward_one(*refs):
        remote_kernel(1, 1, *refs)

    v_odd, *s = call(
        backward_one, [PLANES] + FACES, (part, bwd, colors, *halo), name="backward_one"
    )
    part = local(0, u_even, bwd, s, "backward_zero_local")
    halo = exchange(*s)
    rows = call(
        last_kernel,
        f32(3 * RHS * SLICE, LANES),
        (part, u_even, x_odd, v_odd, bwd, colors, *halo),
        [whole, pltpu.SemaphoreType.DMA((3 * steps,))],
        name="backward_zero",
        hbm_out=True,
    )
    return from_rows(rows), jnp.transpose(own_wells, (1, 0, 2))


def solution(mesh):
    placed = (
        P(None, None, "slab", "col", None),
        P(("slab", "col"), None, None),
        P("slab", "col", None),
        P(None, None, None, "slab", "col", None),
        P(None, None, "slab", "col", None),
        P(("slab", "col")),
        P(("slab", "col")),
        P(("slab", "col"), None, None),
        P(("slab", "col"), None, None),
        P(("slab", "col"), None, None),
    )
    return jax.shard_map(
        per_device,
        mesh=mesh,
        in_specs=placed,
        out_specs=(P(None, None, "slab", "col", None), P(("slab", "col"), None, None)),
        check_vma=False,
    )
```

```python
import jax
import jax.numpy as jnp
from jax import lax
from jax.experimental import pallas as pl
from jax.experimental.pallas import tpu as pltpu
from jax.sharding import PartitionSpec as P

RHS = 128
LANES = 128
ROWS = 64
SLICE = 8
FACE_RX, FACE_LX, FACE_RY, FACE_LY, FACE_ZU, FACE_ZS = range(6)
PERFS = 64
SENT = 6 * RHS
EXTRA = 16
WIDE = 4 * LANES
BLOCK = 32


def f32(*shape):
    return jax.ShapeDtypeStruct(shape, jnp.float32)


PLANES = f32(4, 3, RHS, LANES)
FACE = f32(SENT, LANES)
FACE_PLUS = f32(SENT + EXTRA, LANES)
PAST = (16, 8, 0, 0)
FACES = [f32(SENT + past, LANES) for past in PAST]
FACES_PLUS = [f32(SENT + EXTRA + past, LANES) for past in PAST]
COEF = f32(8, 54, LANES)


def call(body, outs, args, scratch=(), name=None, hbm=(), hbm_out=False):
    spaces = [pltpu.HBM if i in hbm else pltpu.VMEM for i in range(len(args))]
    out_space = pltpu.HBM if hbm_out else pltpu.VMEM
    return pl.pallas_call(
        body,
        out_shape=outs,
        in_specs=[pl.BlockSpec(memory_space=space) for space in spaces],
        out_specs=jax.tree.map(lambda _: pl.BlockSpec(memory_space=out_space), outs),
        scratch_shapes=list(scratch),
        compiler_params=pltpu.CompilerParams(vmem_limit_bytes=16 * 1024 * 1024),
        cost_estimate=pl.CostEstimate(flops=1_000_000, bytes_accessed=2_000_000, transcendentals=0),
        name=name,
    )(*args)


def spots():
    return lax.rem(lax.axis_index("slab"), 2), lax.rem(lax.axis_index("col"), 2)


def line_xy(tx, ty):
    sp, cp = spots()
    x = sp if tx else 1 - sp
    y = cp if ty else 1 - cp
    return x, y


def xor(a, b):
    return a + b - 2 * a * b


def lane_iota(rows):
    return lax.broadcasted_iota(jnp.int32, (rows, LANES), 1)


def pick(values, index):
    return jnp.take_along_axis(values, index, axis=1)


def split_z(low, high, odd):
    lane = lane_iota(low.shape[0])
    index = (2 * lane + odd) & (LANES - 1)
    return jnp.where(lane < LANES // 2, pick(low, index), pick(high, index))


def join_z(even, odd, half):
    lane = lane_iota(even.shape[0])
    index = half * (LANES // 2) + (lane >> 1)
    return jnp.where((lane & 1) == 0, pick(even, index), pick(odd, index))


def line_rows(ref, start, count):
    return ref[pl.ds(start, count, stride=SLICE), :]


def tile_split(tile):
    lane = lane_iota(SLICE)
    part = (lax.broadcasted_iota(jnp.int32, (SLICE, LANES), 0) >> 1) & 1
    even = pick(tile, (2 * lane) & (LANES - 1))
    odd = pick(tile, (2 * lane + 1) & (LANES - 1))
    low = lane < LANES // 2
    of_even = jnp.where(low, even, pltpu.roll(even, SLICE - 2, 0))
    of_odd = jnp.where(low, pltpu.roll(odd, 2, 0), odd)
    return jnp.where(part == 0, of_even, of_odd)


def split_tiles(source, target, count):
    for row in range(count):
        target[row * 8 : row * 8 + 8, :] = tile_split(source[row * 8 : row * 8 + 8, :])


def pivoted(rhs_ref, piv, cls, tx, ty, rows):
    x, y = line_xy(tx, ty)
    odd = xor(xor(x, y), cls)
    planes = []
    for a in range(3):
        base = (a * RHS + rows) * SLICE + x * 4 + y
        planes.append(
            split_z(line_rows(rhs_ref, base, ROWS), line_rows(rhs_ref, base + 2, ROWS), odd)
        )
    return [
        piv[0 * 3 + b] * planes[0] + piv[1 * 3 + b] * planes[1] + piv[2 * 3 + b] * planes[2]
        for b in range(3)
    ]


def class_rows(ref, cls, tx, ty, count):
    x, y = line_xy(tx, ty)
    odd = xor(xor(x, y), cls)
    return ref[pl.ds(x * 4 + odd * 2 + y, count, stride=SLICE), :]


def chunks(body):
    def step(i, carry):
        body(pl.multiple_of(i * ROWS, ROWS))
        return carry

    lax.fori_loop(0, RHS // ROWS, step, 0)


def lines():
    return [(tx, ty) for tx in range(2) for ty in range(2)]


def at_face(t, b, rows, count=ROWS):
    return pl.ds((t * 3 + b) * RHS + rows, count)


def from_sy(sya, syb, rows):
    return lambda tx, ty, a: (syb if ty else sya)[at_face(tx, a, rows), :]


def from_halos(halos, rows):
    rya, ryb, rxb, rxa = halos
    return (
        lambda tx, ty, a: (rxb if tx else rxa)[at_face(ty, a, rows), :],
        lambda tx, ty, a: (ryb if ty else rya)[at_face(tx, a, rows), :],
    )


def take(acc, coef, d, face, a, value):
    for b in range(3):
        row = face * 9 + a * 3 + b
        acc[b] = acc[b] - coef[d, row : row + 1, :] * value


def add_local(acc, coef, cls, tx, ty, get):
    x, y = line_xy(tx, ty)
    odd = xor(xor(x, y), cls)
    index = (lane_iota(ROWS) + (LANES - 1) + 2 * odd) & (LANES - 1)
    d = cls * 4 + tx * 2 + ty
    for a in range(3):
        center = get(tx, ty, a)
        take(acc, coef, d, FACE_LX, a, get(1 - tx, ty, a))
        take(acc, coef, d, FACE_LY, a, get(tx, 1 - ty, a))
        take(acc, coef, d, FACE_ZU, a, center)
        take(acc, coef, d, FACE_ZS, a, pick(center, index))
    return acc


def add_remote(acc, coef, cls, tx, ty, get_x, get_y):
    d = cls * 4 + tx * 2 + ty
    for a in range(3):
        take(acc, coef, d, FACE_RX, a, get_x(tx, ty, a))
        take(acc, coef, d, FACE_RY, a, get_y(tx, ty, a))
    return acc


def store_faces(faces, tx, ty, b, rows, value):
    sya, syb, sxb, sxa = faces
    (syb if ty else sya)[at_face(tx, b, rows), :] = value
    (sxb if tx else sxa)[at_face(ty, b, rows), :] = value


def first_kernel(
    rhs_hbm, piv_hbm, colors_hbm, q_ref, sya, syb, sxb, sxa,
    rhs_ref, piv_ref, colors_ref, tiles, color_tile, sems,
):
    steps = RHS // ROWS

    def rhs_copy(i, a):
        part = pl.ds((a * RHS + i * ROWS) * SLICE, ROWS * SLICE)
        return pltpu.make_async_copy(rhs_hbm.at[part], rhs_ref.at[part], sems.at[2 + i * 3 + a])

    piv_copy = pltpu.make_async_copy(piv_hbm, piv_ref, sems.at[0])
    color_copy = pltpu.make_async_copy(colors_hbm, colors_ref, sems.at[1])
    piv_copy.start()
    color_copy.start()
    for i in range(steps):
        for a in range(3):
            rhs_copy(i, a).start()
    piv_copy.wait()
    split_tiles(piv_ref, tiles, 9)
    color_copy.wait()
    color_tile[...] = tile_split(colors_ref[...])

    def step(i, carry):
        for a in range(3):
            rhs_copy(i, a).wait()
        rows = pl.multiple_of(i * ROWS, ROWS)
        for tx, ty in lines():
            piv_rows = class_rows(tiles, 0, tx, ty, 9)
            piv = [piv_rows[e : e + 1] for e in range(9)]
            mask = class_rows(color_tile, 0, tx, ty, 1) == 0
            for b, value in enumerate(pivoted(rhs_ref, piv, 0, tx, ty, rows)):
                q_ref[tx * 2 + ty, b, pl.ds(rows, ROWS), :] = value
                store_faces((sya, syb, sxb, sxa), tx, ty, b, rows, jnp.where(mask, value, 0.0))
        return carry

    lax.fori_loop(0, steps, step, 0)


def second_kernel(
    rhs_ref, piv_ref, colors_ref, inc_ref, sya, syb, well_piv_ref,
    part_ref, fwd_ref, bwd_ref, cls_colors_ref, well_rows_ref, tiles, color_tile, raw, folded,
):
    well_rows_ref[...] = jnp.zeros(well_rows_ref.shape, jnp.float32)
    for a in range(3):
        well_rows_ref[0:2, a * 3 : a * 3 + 3] = well_piv_ref[a]
    split_tiles(piv_ref, tiles, 9)
    color_tile[...] = tile_split(colors_ref[...])
    spot = lax.broadcasted_iota(jnp.int32, (SLICE, LANES), 0)
    lane = lane_iota(SLICE)
    x_low = (spot >> 2) == 0
    y_low = (spot & 1) == 0
    z_even = ((spot >> 1) & 1) == 0
    edge = (z_even & (lane == 0)) | (jnp.logical_not(z_even) & (lane == LANES - 1))

    slab, col = lax.axis_index("slab"), lax.axis_index("col")
    inside = [
        jnp.where(low, jnp.where(at == 0, 0.0, 1.0), jnp.where(at == last, 0.0, 1.0))
        for low, at, last in (
            (x_low, slab, lax.axis_size("slab") - 1),
            (y_low, col, lax.axis_size("col") - 1),
        )
    ]

    def source(face, entry):
        row = (face * 9 + entry) * 8
        return tile_split(inc_ref[row : row + 8, :])

    piv = [tiles[i * 8 : i * 8 + 8, :] for i in range(9)]
    for group, (first, second, low) in enumerate(((0, 1, x_low), (2, 3, y_low), (5, 4, z_even))):
        one = [None] * 9
        two = [None] * 9
        for entry in range(9):
            p, q = source(first, entry), source(second, entry)
            one[entry] = jnp.where(low, p, q)
            two[entry] = jnp.where(low, q, p)
            if group < 2:
                one[entry] = one[entry] * inside[group]
            else:
                two[entry] = jnp.where(edge, 0.0, two[entry])
        for which, block in ((0, one), (1, two)):
            face = group * 2 + which
            for a in range(3):
                for b in range(3):
                    row = (face * 9 + a * 3 + b) * 8
                    raw[row : row + 8, :] = block[a * 3 + b]
                    folded[row : row + 8, :] = (
                        block[a * 3] * piv[b]
                        + block[a * 3 + 1] * piv[3 + b]
                        + block[a * 3 + 2] * piv[6 + b]
                    )
    for cls in range(2):
        for tx, ty in lines():
            d = cls * 4 + tx * 2 + ty
            fwd_ref[d] = class_rows(folded, cls, tx, ty, 54)
            bwd_ref[d] = class_rows(raw, cls, tx, ty, 54)
            cls_colors_ref[d : d + 1, :] = class_rows(color_tile, cls, tx, ty, 1)
    for tx, ty in lines():
        piv_rows = class_rows(tiles, 1, tx, ty, 9)
        piv1 = [piv_rows[i : i + 1] for i in range(9)]

        def body(rows, tx=tx, ty=ty, piv1=piv1):
            acc = pivoted(rhs_ref, piv1, 1, tx, ty, rows)
            acc = add_local(acc, fwd_ref, 1, tx, ty, from_sy(sya, syb, rows))
            for b in range(3):
                part_ref[tx * 2 + ty, b, pl.ds(rows, ROWS), :] = acc[b]

        chunks(body)


def local_kernel(cls, base_ref, coef_ref, sya, syb, part_ref):
    for tx, ty in lines():
        n = tx * 2 + ty

        def body(rows, tx=tx, ty=ty, n=n):
            acc = [base_ref[n, b, pl.ds(rows, ROWS), :] for b in range(3)]
            acc = add_local(acc, coef_ref, cls, tx, ty, from_sy(sya, syb, rows))
            for b in range(3):
                part_ref[n, b, pl.ds(rows, ROWS), :] = acc[b]

        chunks(body)


def remote_kernel(cls, color, part_ref, coef_ref, colors_ref, rya, ryb, rxb, rxa, full_ref, *faces):
    for tx, ty in lines():
        n = tx * 2 + ty
        d = cls * 4 + n

        def body(rows, tx=tx, ty=ty, n=n, d=d):
            acc = [part_ref[n, b, pl.ds(rows, ROWS), :] for b in range(3)]
            acc = add_remote(acc, coef_ref, cls, tx, ty, *from_halos((rya, ryb, rxb, rxa), rows))
            mask = colors_ref[d : d + 1, :] == color
            for b in range(3):
                full_ref[n, b, pl.ds(rows, ROWS), :] = acc[b]
                store_faces(faces, tx, ty, b, rows, jnp.where(mask, acc[b], 0.0))

        chunks(body)


def perf_place(perf_cell):
    sp, cp = spots()
    x = perf_cell >> 9
    y = (perf_cell >> 8) & 1
    z = perf_cell & 255
    cls = (x + y + z) & 1
    tx = (x + 1 - sp) & 1
    ty = (y + 1 - cp) & 1
    return (cls * 4 + tx * 2 + ty) * LANES + (z >> 1)


def forward_one_kernel(
    part_ref, coef_ref, colors_ref, rya, ryb, rxb, rxa, perf_cell_ref, perf_well_ref, perf_in_ref,
    full_ref, sya, syb, sxb, sxa, table_ref,
):
    faces = (sya, syb, sxb, sxa)
    table_ref[...] = jnp.zeros((EXTRA, LANES), jnp.float32)
    table_ref[0:1, 0:PERFS] = perf_place(perf_cell_ref[...]).astype(jnp.float32)
    table_ref[1:2, 0:PERFS] = perf_well_ref[...].astype(jnp.float32)
    for a in range(3):
        table_ref[2 + a * 3 : 5 + a * 3, 0:PERFS] = perf_in_ref[a]
    remote_kernel(1, 1, part_ref, coef_ref, colors_ref, rya, ryb, rxb, rxa, full_ref, *faces)
    for target, start, step in ((sya, 4, 2), (syb, 5, 2), (sxb, 6, 1), (sxa, 4, 1)):
        target[SENT : SENT + EXTRA, :] = table_ref[...]
        if target.shape[0] > SENT + EXTRA:
            target[SENT + EXTRA :, :] = jnp.zeros((target.shape[0] - SENT - EXTRA, LANES), jnp.float32)
        for t in range(2):
            d = start + t * step
            row = SENT + 11 + t
            target[row : row + 1, :] = colors_ref[d : d + 1, :].astype(jnp.float32)


def forward_two_kernel(
    part_ref, coef_ref, colors_ref, rya, ryb, rxb, rxa, table_ref,
    full_ref, sya, syb, sxb, sxa, tables_ref,
):
    faces = (sya, syb, sxb, sxa)
    remote_kernel(0, 2, part_ref, coef_ref, colors_ref, rya, ryb, rxb, rxa, full_ref, *faces)
    tables_ref[0] = table_ref[...]
    for i, ref in enumerate((rya, ryb, rxb, rxa)):
        tables_ref[i + 1] = ref[SENT : SENT + EXTRA, :]


def hot(index, count, start=0, step=LANES):
    rows = lax.broadcasted_iota(jnp.int32, (count, index.shape[1]), 0)
    rows = start + (rows >> 7) * step + (rows & (LANES - 1))
    return jnp.where(rows == index, 1.0, 0.0).astype(jnp.bfloat16)


def halves(values):
    high = values.astype(jnp.bfloat16)
    return high, (values - high.astype(jnp.float32)).astype(jnp.bfloat16)


def dot_ones(parts, ones, dims):
    return sum(
        lax.dot_general(part, ones, (dims, ((), ())), preferred_element_type=jnp.float32)
        for part in parts
    )


def well_bits():
    slab = lax.axis_index("slab")
    return slab & 1, slab >> 3, (slab >> 1) & 3


def core_wells(shape, core):
    rows = lax.broadcasted_iota(jnp.int32, shape, 0)
    return (rows >> 3) * 16 + core * 8 + (rows & 7)


def own_row(j):
    return well_bits()[2] * 8 + lax.axis_index("col") * 2 + j


def forward_three_kernel(
    part_ref, t_ref, q_ref, u_ref, coef_ref, colors_ref, rya, ryb, rxb, rxa,
    perf_cell_ref, perf_well_ref, perf_out_ref, well_rhs_ref,
    even_ref, odd_ref, keep_ref, send_ref, sya, syb, at_ref,
):
    for tx, ty in lines():
        n = tx * 2 + ty
        d = 4 + n

        def body(rows, tx=tx, ty=ty, n=n, d=d):
            part = pl.ds(rows, ROWS)
            acc = [part_ref[n, b, part, :] for b in range(3)]
            acc = add_remote(acc, coef_ref, 1, tx, ty, *from_halos((rya, ryb, rxb, rxa), rows))
            is_one = colors_ref[d : d + 1, :] == 1
            is_two = colors_ref[n : n + 1, :] == 2
            for b in range(3):
                value = jnp.where(is_one, t_ref[n, b, part, :], acc[b])
                odd_ref[n, b, part, :] = value
                (syb if ty else sya)[at_face(tx, b, rows), :] = value
                even_ref[n, b, part, :] = jnp.where(is_two, u_ref[n, b, part, :], q_ref[n, b, part, :])

        chunks(body)
    place = perf_place(perf_cell_ref[...])
    at_perfs = None
    for cls, ref in ((0, even_ref), (1, odd_ref)):
        for tx in range(2):
            planes = [ref[tx * 2 + ty].reshape(3 * RHS, LANES) for ty in range(2)]
            ones = hot(place, 2 * LANES, (cls * 4 + tx * 2) * LANES)
            term = dot_ones(halves(jnp.concatenate(planes, axis=1)), ones, ((1,), (0,)))
            at_perfs = term if at_perfs is None else at_perfs + term
    for b in range(3):
        at_ref[b * RHS : (b + 1) * RHS, :] = sum(
            perf_out_ref[a, b : b + 1, :] * at_perfs[a * RHS : (a + 1) * RHS] for a in range(3)
        )
    core, _, _ = well_bits()
    device = lax.axis_index("slab") * lax.axis_size("col") + lax.axis_index("col")
    parts = halves(at_ref[...])
    count = keep_ref.shape[0]
    for ref, which in ((keep_ref, core), (send_ref, 1 - core)):
        wells = jnp.where(core_wells((count, PERFS), which) == perf_well_ref[...], 1.0, 0.0)
        total = sum(
            lax.dot_general(
                wells.astype(jnp.bfloat16), part, (((1,), (1,)), ((), ())),
                preferred_element_type=jnp.float32,
            )
            for part in parts
        )
        is_own = [core_wells((count, LANES), which) == device * 2 + j for j in range(2)]
        for b in range(3):
            own = sum(jnp.where(is_own[j], well_rhs_ref[b, j : j + 1, :], 0.0) for j in range(2))
            ref[:, b * LANES : (b + 1) * LANES] = own - total[:, b * LANES : (b + 1) * LANES]


def core_sum_kernel(keep_ref, got_ref, *outs):
    _, z_spot, _ = well_bits()
    count = outs[0].shape[0]
    for m, out in enumerate(outs):
        rows = pl.ds(pl.multiple_of((z_spot ^ m) * count, count), count)
        out[0:count, :] = keep_ref[rows, :] + got_ref[rows, :]
        if out.shape[0] > count:
            out[count:, :] = jnp.zeros((out.shape[0] - count, out.shape[1]), jnp.float32)


def sum_of(refs):
    a, b, c, d = (ref[0:BLOCK, :] for ref in refs)
    return (a + b) + (c + d)


def store_twice(value, out, far_out, lanes=slice(None)):
    out[:, lanes] = value
    far_out[0:BLOCK, lanes] = value


def z_sum_kernel(a, b, c, d, well_piv_ref, out_ref, far_ref):
    far_ref[BLOCK:, :] = jnp.zeros((SLICE, WIDE), jnp.float32)
    store_twice(sum_of((a, b, c, d)), out_ref, far_ref, slice(0, 3 * LANES))
    rows = lax.broadcasted_iota(jnp.int32, (BLOCK, LANES), 0)
    blocks = sum(jnp.where(rows == own_row(j), well_piv_ref[j : j + 1, :], 0.0) for j in range(2))
    store_twice(blocks, out_ref, far_ref, slice(3 * LANES, WIDE))


def y_sum_kernel(a, b, c, d, odd_ref, rya, ryb, out_ref, far_ref, sxb, sxa):
    far_ref[BLOCK:, :] = jnp.zeros((SLICE, WIDE), jnp.float32)
    store_twice(sum_of((a, b, c, d)), out_ref, far_ref)
    for tx, ty in lines():
        for e in range(3):
            (sxb if tx else sxa)[at_face(ty, e, 0, RHS), :] = odd_ref[tx * 2 + ty, e]


def stack_kernel(*refs):
    for i, ref in enumerate(refs[:4]):
        refs[-1][i * BLOCK : (i + 1) * BLOCK, :] = ref[0:BLOCK, :]


def solve_kernel(a, b, c, d, out_ref, far_ref, own_ref):
    total = sum_of((a, b, c, d))
    far_ref[BLOCK:, :] = jnp.zeros((SLICE, 3 * LANES), jnp.float32)
    rows = lax.broadcasted_iota(jnp.int32, (BLOCK, LANES), 0)
    for e in range(3):
        lanes = slice(e * LANES, (e + 1) * LANES)
        value = sum(
            total[:, 3 * LANES + i * 3 + e : 3 * LANES + i * 3 + e + 1]
            * total[:, i * LANES : (i + 1) * LANES]
            for i in range(3)
        )
        store_twice(value, out_ref, far_ref, lanes)
        for j in range(2):
            found = jnp.where(rows == own_row(j), value, 0.0)
            own_ref[e, j : j + 1, :] = jnp.sum(found, axis=0, keepdims=True)


def backward_two_kernel(
    wells_ref, other_ref, even_ref, odd_ref, colors_ref, coef_ref, rya, ryb, rxb, rxa, tables_ref,
    u_ref, x_odd_ref, sya, syb, sxb, sxa, fix_ref, x_even_ref, three_ref, hya, hyb, hxb, hxa,
):
    core, z_spot, _ = well_bits()

    def place_of_well(well):
        return (
            ((((well >> 3) & 1) ^ core) << 7)
            | ((((well >> 6) & 3) ^ z_spot) << 5)
            | (((well >> 4) & 3) << 3)
            | (well & 7)
        )

    wells = halves(jnp.concatenate([wells_ref[...].T, other_ref[...].T], axis=1))
    tables = [tables_ref[i] for i in range(5)]
    for first in (0, 2, 4):
        pair = tables[first : first + 2]
        well = jnp.concatenate([table[1:2] for table in pair], axis=1).astype(jnp.int32)
        at_perfs = dot_ones(wells, hot(place_of_well(well), 2 * LANES), ((1,), (0,)))
        for i, table in enumerate(pair):
            for b in range(3):
                fix = sum(
                    table[2 + a * 3 + b : 3 + a * 3 + b]
                    * at_perfs[a * RHS : (a + 1) * RHS, i * LANES : (i + 1) * LANES]
                    for a in range(3)
                )
                for part, value in enumerate(halves(fix)):
                    lanes = slice(part * LANES, (part + 1) * LANES)
                    fix_ref[first + i, b * RHS : (b + 1) * RHS, lanes] = value

    def spread(group, start, step):
        place = tables[group][0:1].astype(jnp.int32)
        ones = hot(place, 2 * LANES, start * LANES, step * LANES)
        return lax.dot_general(
            fix_ref[group], jnp.concatenate([ones, ones], axis=1),
            (((1,), (1,)), ((), ())), preferred_element_type=jnp.float32,
        )

    for cls, ref, out in ((1, odd_ref, x_odd_ref), (0, even_ref, x_even_ref)):
        for tx in range(2):
            fix = spread(0, cls * 4 + tx * 2, 1)
            for ty in range(2):
                n = tx * 2 + ty
                d = cls * 4 + n
                for b in range(3):
                    value = ref[n, b] - fix[b * RHS : (b + 1) * RHS, ty * LANES : (ty + 1) * LANES]
                    out[n, b] = value
                    if cls == 1:
                        three_ref[n, b] = jnp.where(colors_ref[d : d + 1, :] == 3, value, 0.0)
    for i, (halo, out, start, step) in enumerate(
        ((rya, hya, 4, 2), (ryb, hyb, 5, 2), (rxb, hxb, 6, 1), (rxa, hxa, 4, 1))
    ):
        fix = spread(i + 1, start, step)
        for t in range(2):
            mask = tables[i + 1][11 + t : 12 + t] == 3.0
            for b in range(3):
                value = halo[at_face(t, b, 0, RHS), :]
                value = value - fix[b * RHS : (b + 1) * RHS, t * LANES : (t + 1) * LANES]
                out[at_face(t, b, 0, RHS), :] = jnp.where(mask, value, 0.0)
    for tx, ty in lines():
        n = tx * 2 + ty

        def body(rows, tx=tx, ty=ty, n=n):
            acc = [x_even_ref[n, b, pl.ds(rows, ROWS), :] for b in range(3)]
            acc = add_local(
                acc, coef_ref, 0, tx, ty,
                lambda i, j, a: three_ref[i * 2 + j, a, pl.ds(rows, ROWS), :],
            )
            acc = add_remote(acc, coef_ref, 0, tx, ty, *from_halos((hya, hyb, hxb, hxa), rows))
            mask = colors_ref[n : n + 1, :] == 2
            for b in range(3):
                u_ref[n, b, pl.ds(rows, ROWS), :] = acc[b]
                store_faces((sya, syb, sxb, sxa), tx, ty, b, rows, jnp.where(mask, acc[b], 0.0))

        chunks(body)


def last_kernel(
    part_ref, u_ref, odd_three, odd_v, coef_ref, colors_ref, rya, ryb, rxb, rxa, out_hbm, out_ref, sems
):
    steps = RHS // ROWS

    def out_copy(i, b):
        part = pl.ds((b * RHS + i * ROWS) * SLICE, ROWS * SLICE)
        return pltpu.make_async_copy(out_ref.at[part], out_hbm.at[part], sems.at[i * 3 + b])

    def step(i, carry):
        rows = pl.multiple_of(i * ROWS, ROWS)
        part = pl.ds(rows, ROWS)
        for tx, ty in lines():
            n = tx * 2 + ty
            x, y = line_xy(tx, ty)
            flip = xor(x, y)
            acc = [part_ref[n, b, part, :] for b in range(3)]
            acc = add_remote(acc, coef_ref, 0, tx, ty, *from_halos((rya, ryb, rxb, rxa), rows))
            is_two = colors_ref[n : n + 1, :] == 2
            is_one = colors_ref[4 + n : 5 + n, :] == 1
            for b in range(3):
                even = jnp.where(is_two, u_ref[n, b, part, :], acc[b])
                odd = jnp.where(is_one, odd_v[n, b, part, :], odd_three[n, b, part, :])
                z_even = jnp.where(flip == 1, odd, even)
                z_odd = jnp.where(flip == 1, even, odd)
                for half in range(2):
                    start = (b * RHS + rows) * SLICE + x * 4 + half * 2 + y
                    out_ref[pl.ds(start, ROWS, stride=SLICE), :] = join_z(z_even, z_odd, half)
        for b in range(3):
            out_copy(i, b).start()
        return carry

    lax.fori_loop(0, steps, step, 0)
    for i in range(steps):
        for b in range(3):
            out_copy(i, b).wait()


def pairs(axis, second):
    count = lax.axis_size(axis)
    found = []
    for i in range(second, count, 2):
        found += [(i, (i + 1) % count), ((i + 1) % count, i)]
    return found


def swap(value, axis, mask):
    return lax.ppermute(value, axis, [(i, i ^ mask) for i in range(lax.axis_size(axis))])


def exchange(sya, syb, sxb, sxa):
    rya = lax.ppermute(sya, "col", pairs("col", 0))
    ryb = lax.ppermute(syb, "col", pairs("col", 1))
    rxb = lax.ppermute(sxb, "slab", pairs("slab", 1))
    rxa = lax.ppermute(sxa, "slab", pairs("slab", 0))
    return rya, ryb, rxb, rxa


def to_rows(array):
    lead = array.shape[:-3]
    split = array.reshape(lead + (2, 2, 2, LANES))
    return jnp.swapaxes(split, -3, -2).reshape(-1, LANES)


def from_rows(rows):
    split = rows.reshape(3, RHS, 2, 2, 2, LANES)
    return jnp.swapaxes(split, -3, -2).reshape(3, RHS, 2, 2, 2 * LANES)


def per_device(
    cell_rhs, well_rhs, cell_colors, incoming, pivot_inv,
    perf_cell, perf_well, perf_out, perf_in, well_pivot_inv,
):
    rhs = to_rows(cell_rhs)
    colors_in = to_rows(cell_colors)
    inc = to_rows(incoming)
    piv = to_rows(pivot_inv)
    place = perf_cell.reshape(1, PERFS)
    well = perf_well.reshape(1, PERFS)
    out_blocks = jnp.transpose(perf_out, (1, 2, 0))
    in_blocks = jnp.transpose(perf_in, (1, 2, 0))
    well_side = jnp.transpose(well_rhs, (1, 0, 2))
    tiles = pltpu.VMEM((72, LANES), jnp.float32)
    color_tile = pltpu.VMEM((8, LANES), jnp.int32)
    whole = pltpu.VMEM((3 * RHS * SLICE, LANES), jnp.float32)
    steps = RHS // ROWS

    def local(cls, base, coef, s, name):
        def body(*refs):
            local_kernel(cls, *refs)

        return call(body, PLANES, (base, coef, *s[:2]), name=name)

    q_even, *s = call(
        first_kernel,
        [PLANES] + FACES,
        [pltpu.with_memory_space_constraint(v, pltpu.HBM) for v in (rhs, piv, colors_in)],
        [whole, tiles, color_tile, tiles, color_tile, pltpu.SemaphoreType.DMA((2 + 3 * steps,))],
        name="even_rhs",
        hbm=(0, 1, 2),
    )
    halo = exchange(*s)
    part, fwd, bwd, colors, well_piv = call(
        second_kernel,
        [PLANES, COEF, COEF, jax.ShapeDtypeStruct((8, LANES), jnp.int32), f32(8, LANES)],
        (rhs, piv, colors_in, inc, *s[:2], jnp.transpose(well_pivot_inv, (1, 0, 2))),
        [tiles, color_tile] + [pltpu.VMEM((54 * 8, LANES), jnp.float32)] * 2,
        name="blocks_and_local",
    )
    t_odd, *s, table = call(
        forward_one_kernel,
        [PLANES] + FACES_PLUS + [f32(EXTRA, LANES)],
        (part, fwd, colors, *halo, place, well, in_blocks),
        name="forward_one",
    )
    part = local(0, q_even, fwd, s, "forward_two_local")
    halo = exchange(*s)
    u_even, *s, tables = call(
        forward_two_kernel,
        [PLANES] + FACES + [f32(5, EXTRA, LANES)],
        (part, fwd, colors, *halo, table),
        name="forward_two",
    )
    part = local(1, t_odd, fwd, s, "forward_three_local")
    halo = exchange(*s)
    even, odd, keep, send, *s = call(
        forward_three_kernel,
        [PLANES, PLANES, f32(4 * BLOCK, 3 * LANES), f32(4 * BLOCK, 3 * LANES), FACE_PLUS, FACE_PLUS],
        (part, t_odd, q_even, u_even, fwd, colors, *halo, place, well, out_blocks, well_side),
        [pltpu.VMEM((3 * RHS, PERFS), jnp.float32)],
        name="forward_three_wells",
    )
    halo = [lax.ppermute(face, "col", pairs("col", i)) for i, face in enumerate(s)]
    narrow = [f32(BLOCK + (SLICE if m == 2 else 0), 3 * LANES) for m in range(4)]
    wide = [f32(BLOCK, WIDE), f32(BLOCK + SLICE, WIDE)]

    def swaps(near, far, axis, unit):
        return [swap(far if m == 2 else near, axis, unit * m) for m in (1, 2, 3)]

    blocks = call(core_sum_kernel, narrow, (keep, swap(send, "slab", 1)), name="core_sum")
    moved = [swap(blocks[m], "slab", 8 * m) for m in (1, 2, 3)]
    mine, far = call(z_sum_kernel, wide, (blocks[0], *moved, well_piv), name="z_sum")
    mine, far, sxb, sxa = call(
        y_sum_kernel,
        wide + [FACE, FACE],
        (mine, *swaps(mine, far, "slab", 2), odd, *halo),
        name="y_sum",
        hbm=(5, 6),
    )
    halo.append(lax.ppermute(sxb, "slab", pairs("slab", 1)))
    halo.append(lax.ppermute(sxa, "slab", pairs("slab", 0)))
    mine, far, own_wells = call(
        solve_kernel,
        [narrow[0], narrow[2], f32(3, 2, RHS)],
        (mine, *swaps(mine, far, "col", 1)),
        name="solve_wells",
    )
    near = call(
        stack_kernel, f32(4 * BLOCK, 3 * LANES), (mine, *swaps(mine, far, "slab", 8)), name="stack"
    )
    far = swap(near, "slab", 1)
    u_even, x_odd, *s = call(
        backward_two_kernel,
        [PLANES, PLANES] + FACES,
        (near, far, even, odd, colors, bwd, *halo, tables),
        [pltpu.VMEM((5, 3 * RHS, 2 * LANES), jnp.bfloat16)]
        + [pltpu.VMEM(PLANES.shape, jnp.float32)] * 2
        + [pltpu.VMEM(FACE.shape, jnp.float32)] * 4,
        name="well_fix_backward_two",
    )
    part = local(1, x_odd, bwd, s, "backward_one_local")
    halo = exchange(*s)

    def backward_one(*refs):
        remote_kernel(1, 1, *refs)

    v_odd, *s = call(
        backward_one, [PLANES] + FACES, (part, bwd, colors, *halo), name="backward_one"
    )
    part = local(0, u_even, bwd, s, "backward_zero_local")
    halo = exchange(*s)
    rows = call(
        last_kernel,
        f32(3 * RHS * SLICE, LANES),
        (part, u_even, x_odd, v_odd, bwd, colors, *halo),
        [whole, pltpu.SemaphoreType.DMA((3 * steps,))],
        name="backward_zero",
        hbm_out=True,
    )
    return from_rows(rows), jnp.transpose(own_wells, (1, 0, 2))


def solution(mesh):
    placed = (
        P(None, None, "slab", "col", None),
        P(("slab", "col"), None, None),
        P("slab", "col", None),
        P(None, None, None, "slab", "col", None),
        P(None, None, "slab", "col", None),
        P(("slab", "col")),
        P(("slab", "col")),
        P(("slab", "col"), None, None),
        P(("slab", "col"), None, None),
        P(("slab", "col"), None, None),
    )
    return jax.shard_map(
        per_device,
        mesh=mesh,
        in_specs=placed,
        out_specs=(P(None, None, "slab", "col", None), P(("slab", "col"), None, None)),
        check_vma=False,
    )
```

```python
import jax
import jax.numpy as jnp
from jax import lax
from jax.experimental import pallas as pl
from jax.experimental.pallas import tpu as pltpu
from jax.sharding import PartitionSpec as P

RHS = 128
LANES = 128
ROWS = 64
SLICE = 8
FACE_RX, FACE_LX, FACE_RY, FACE_LY, FACE_ZU, FACE_ZS = range(6)
PERFS = 64
SENT = 6 * RHS
EXTRA = 16
WIDE = 4 * LANES
BLOCK = 32


def f32(*shape):
    return jax.ShapeDtypeStruct(shape, jnp.float32)


PLANES = f32(4, 3, RHS, LANES)
FACE = f32(SENT, LANES)
FACE_PLUS = f32(SENT + EXTRA, LANES)
PAST = (16, 8, 0, 0)
FACES = [f32(SENT + past, LANES) for past in PAST]
FACES_PLUS = [f32(SENT + EXTRA + past, LANES) for past in PAST]
COEF = f32(8, 54, LANES)


def call(body, outs, args, scratch=(), name=None, hbm=(), hbm_out=False):
    spaces = [pltpu.HBM if i in hbm else pltpu.VMEM for i in range(len(args))]
    out_space = pltpu.HBM if hbm_out else pltpu.VMEM
    return pl.pallas_call(
        body,
        out_shape=outs,
        in_specs=[pl.BlockSpec(memory_space=space) for space in spaces],
        out_specs=jax.tree.map(lambda _: pl.BlockSpec(memory_space=out_space), outs),
        scratch_shapes=list(scratch),
        compiler_params=pltpu.CompilerParams(vmem_limit_bytes=16 * 1024 * 1024),
        cost_estimate=pl.CostEstimate(flops=1_000_000, bytes_accessed=2_000_000, transcendentals=0),
        name=name,
    )(*args)


def spots():
    return lax.rem(lax.axis_index("slab"), 2), lax.rem(lax.axis_index("col"), 2)


def line_xy(tx, ty):
    sp, cp = spots()
    x = sp if tx else 1 - sp
    y = cp if ty else 1 - cp
    return x, y


def xor(a, b):
    return a + b - 2 * a * b


def lane_iota(rows):
    return lax.broadcasted_iota(jnp.int32, (rows, LANES), 1)


def pick(values, index):
    return jnp.take_along_axis(values, index, axis=1)


def split_z(low, high, odd):
    lane = lane_iota(low.shape[0])
    index = (2 * lane + odd) & (LANES - 1)
    return jnp.where(lane < LANES // 2, pick(low, index), pick(high, index))


def join_z(even, odd, half):
    lane = lane_iota(even.shape[0])
    index = half * (LANES // 2) + (lane >> 1)
    return jnp.where((lane & 1) == 0, pick(even, index), pick(odd, index))


def line_rows(ref, start, count):
    return ref[pl.ds(start, count, stride=SLICE), :]


def tile_split(tile):
    lane = lane_iota(SLICE)
    part = (lax.broadcasted_iota(jnp.int32, (SLICE, LANES), 0) >> 1) & 1
    even = pick(tile, (2 * lane) & (LANES - 1))
    odd = pick(tile, (2 * lane + 1) & (LANES - 1))
    low = lane < LANES // 2
    of_even = jnp.where(low, even, pltpu.roll(even, SLICE - 2, 0))
    of_odd = jnp.where(low, pltpu.roll(odd, 2, 0), odd)
    return jnp.where(part == 0, of_even, of_odd)


def split_tiles(source, target, count):
    for row in range(count):
        target[row * 8 : row * 8 + 8, :] = tile_split(source[row * 8 : row * 8 + 8, :])


def pivoted(rhs_ref, piv, cls, tx, ty, rows):
    x, y = line_xy(tx, ty)
    odd = xor(xor(x, y), cls)
    planes = []
    for a in range(3):
        base = (a * RHS + rows) * SLICE + x * 4 + y
        planes.append(
            split_z(line_rows(rhs_ref, base, ROWS), line_rows(rhs_ref, base + 2, ROWS), odd)
        )
    return [
        piv[0 * 3 + b] * planes[0] + piv[1 * 3 + b] * planes[1] + piv[2 * 3 + b] * planes[2]
        for b in range(3)
    ]


def class_rows(ref, cls, tx, ty, count):
    x, y = line_xy(tx, ty)
    odd = xor(xor(x, y), cls)
    return ref[pl.ds(x * 4 + odd * 2 + y, count, stride=SLICE), :]


def chunks(body):
    def step(i, carry):
        body(pl.multiple_of(i * ROWS, ROWS))
        return carry

    lax.fori_loop(0, RHS // ROWS, step, 0)


def lines():
    return [(tx, ty) for tx in range(2) for ty in range(2)]


def at_face(t, b, rows, count=ROWS):
    return pl.ds((t * 3 + b) * RHS + rows, count)


def from_sy(sya, syb, rows):
    return lambda tx, ty, a: (syb if ty else sya)[at_face(tx, a, rows), :]


def from_halos(halos, rows):
    rya, ryb, rxb, rxa = halos
    return (
        lambda tx, ty, a: (rxb if tx else rxa)[at_face(ty, a, rows), :],
        lambda tx, ty, a: (ryb if ty else rya)[at_face(tx, a, rows), :],
    )


def take(acc, coef, d, face, a, value):
    for b in range(3):
        row = face * 9 + a * 3 + b
        acc[b] = acc[b] - coef[d, row : row + 1, :] * value


def add_local(acc, coef, cls, tx, ty, get):
    x, y = line_xy(tx, ty)
    odd = xor(xor(x, y), cls)
    index = (lane_iota(ROWS) + (LANES - 1) + 2 * odd) & (LANES - 1)
    d = cls * 4 + tx * 2 + ty
    for a in range(3):
        center = get(tx, ty, a)
        take(acc, coef, d, FACE_LX, a, get(1 - tx, ty, a))
        take(acc, coef, d, FACE_LY, a, get(tx, 1 - ty, a))
        take(acc, coef, d, FACE_ZU, a, center)
        take(acc, coef, d, FACE_ZS, a, pick(center, index))
    return acc


def add_remote(acc, coef, cls, tx, ty, get_x, get_y):
    d = cls * 4 + tx * 2 + ty
    for a in range(3):
        take(acc, coef, d, FACE_RX, a, get_x(tx, ty, a))
        take(acc, coef, d, FACE_RY, a, get_y(tx, ty, a))
    return acc


def store_faces(faces, tx, ty, b, rows, value):
    sya, syb, sxb, sxa = faces
    (syb if ty else sya)[at_face(tx, b, rows), :] = value
    (sxb if tx else sxa)[at_face(ty, b, rows), :] = value


def first_kernel(
    rhs_hbm, piv_hbm, colors_hbm, q_ref, sya, syb, sxb, sxa,
    rhs_ref, piv_ref, colors_ref, tiles, color_tile, sems,
):
    steps = RHS // ROWS

    def rhs_copy(i, a):
        part = pl.ds((a * RHS + i * ROWS) * SLICE, ROWS * SLICE)
        return pltpu.make_async_copy(rhs_hbm.at[part], rhs_ref.at[part], sems.at[2 + i * 3 + a])

    piv_copy = pltpu.make_async_copy(piv_hbm, piv_ref, sems.at[0])
    color_copy = pltpu.make_async_copy(colors_hbm, colors_ref, sems.at[1])
    piv_copy.start()
    color_copy.start()
    for i in range(steps):
        for a in range(3):
            rhs_copy(i, a).start()
    piv_copy.wait()
    split_tiles(piv_ref, tiles, 9)
    color_copy.wait()
    color_tile[0:SLICE, :] = tile_split(colors_ref[...])

    def step(i, carry):
        for a in range(3):
            rhs_copy(i, a).wait()
        rows = pl.multiple_of(i * ROWS, ROWS)
        for tx, ty in lines():
            piv_rows = class_rows(tiles, 0, tx, ty, 9)
            piv = [piv_rows[e : e + 1] for e in range(9)]
            mask = class_rows(color_tile, 0, tx, ty, 1) == 0
            for b, value in enumerate(pivoted(rhs_ref, piv, 0, tx, ty, rows)):
                q_ref[tx * 2 + ty, b, pl.ds(rows, ROWS), :] = value
                store_faces((sya, syb, sxb, sxa), tx, ty, b, rows, jnp.where(mask, value, 0.0))
        return carry

    lax.fori_loop(0, steps, step, 0)


def second_kernel(
    rhs_ref, piv_ref, colors_ref, inc_ref, sya, syb, well_piv_ref,
    part_ref, fwd_ref, bwd_ref, cls_colors_ref, well_rows_ref, tiles, color_tile, raw, folded,
):
    well_rows_ref[...] = jnp.zeros(well_rows_ref.shape, jnp.float32)
    for a in range(3):
        well_rows_ref[0:2, a * 3 : a * 3 + 3] = well_piv_ref[a]
    split_tiles(piv_ref, tiles, 9)
    color_tile[0:SLICE, :] = tile_split(colors_ref[...])
    spot = lax.broadcasted_iota(jnp.int32, (SLICE, LANES), 0)
    lane = lane_iota(SLICE)
    x_low = (spot >> 2) == 0
    y_low = (spot & 1) == 0
    z_even = ((spot >> 1) & 1) == 0
    edge = (z_even & (lane == 0)) | (jnp.logical_not(z_even) & (lane == LANES - 1))

    slab, col = lax.axis_index("slab"), lax.axis_index("col")
    inside = [
        jnp.where(low, jnp.where(at == 0, 0.0, 1.0), jnp.where(at == last, 0.0, 1.0))
        for low, at, last in (
            (x_low, slab, lax.axis_size("slab") - 1),
            (y_low, col, lax.axis_size("col") - 1),
        )
    ]

    def source(face, entry):
        row = (face * 9 + entry) * 8
        return tile_split(inc_ref[row : row + 8, :])

    piv = [tiles[i * 8 : i * 8 + 8, :] for i in range(9)]
    for group, (first, second, low) in enumerate(((0, 1, x_low), (2, 3, y_low), (5, 4, z_even))):
        one = [None] * 9
        two = [None] * 9
        for entry in range(9):
            p, q = source(first, entry), source(second, entry)
            one[entry] = jnp.where(low, p, q)
            two[entry] = jnp.where(low, q, p)
            if group < 2:
                one[entry] = one[entry] * inside[group]
            else:
                two[entry] = jnp.where(edge, 0.0, two[entry])
        for which, block in ((0, one), (1, two)):
            face = group * 2 + which
            for a in range(3):
                for b in range(3):
                    row = (face * 9 + a * 3 + b) * 8
                    raw[row : row + 8, :] = block[a * 3 + b]
                    folded[row : row + 8, :] = (
                        block[a * 3] * piv[b]
                        + block[a * 3 + 1] * piv[3 + b]
                        + block[a * 3 + 2] * piv[6 + b]
                    )
    for cls in range(2):
        for tx, ty in lines():
            d = cls * 4 + tx * 2 + ty
            fwd_ref[d] = class_rows(folded, cls, tx, ty, 54)
            bwd_ref[d] = class_rows(raw, cls, tx, ty, 54)
            cls_colors_ref[d : d + 1, :] = class_rows(color_tile, cls, tx, ty, 1)
    for tx, ty in lines():
        piv_rows = class_rows(tiles, 1, tx, ty, 9)
        piv1 = [piv_rows[i : i + 1] for i in range(9)]

        def body(rows, tx=tx, ty=ty, piv1=piv1):
            acc = pivoted(rhs_ref, piv1, 1, tx, ty, rows)
            acc = add_local(acc, fwd_ref, 1, tx, ty, from_sy(sya, syb, rows))
            for b in range(3):
                part_ref[tx * 2 + ty, b, pl.ds(rows, ROWS), :] = acc[b]

        chunks(body)


def local_kernel(cls, base_ref, coef_ref, sya, syb, part_ref):
    for tx, ty in lines():
        n = tx * 2 + ty

        def body(rows, tx=tx, ty=ty, n=n):
            acc = [base_ref[n, b, pl.ds(rows, ROWS), :] for b in range(3)]
            acc = add_local(acc, coef_ref, cls, tx, ty, from_sy(sya, syb, rows))
            for b in range(3):
                part_ref[n, b, pl.ds(rows, ROWS), :] = acc[b]

        chunks(body)


def remote_kernel(cls, color, part_ref, coef_ref, colors_ref, rya, ryb, rxb, rxa, full_ref, *faces):
    for tx, ty in lines():
        n = tx * 2 + ty
        d = cls * 4 + n

        def body(rows, tx=tx, ty=ty, n=n, d=d):
            acc = [part_ref[n, b, pl.ds(rows, ROWS), :] for b in range(3)]
            acc = add_remote(acc, coef_ref, cls, tx, ty, *from_halos((rya, ryb, rxb, rxa), rows))
            mask = colors_ref[d : d + 1, :] == color
            for b in range(3):
                full_ref[n, b, pl.ds(rows, ROWS), :] = acc[b]
                store_faces(faces, tx, ty, b, rows, jnp.where(mask, acc[b], 0.0))

        chunks(body)


def perf_place(perf_cell):
    sp, cp = spots()
    x = perf_cell >> 9
    y = (perf_cell >> 8) & 1
    z = perf_cell & 255
    cls = (x + y + z) & 1
    tx = (x + 1 - sp) & 1
    ty = (y + 1 - cp) & 1
    return (cls * 4 + tx * 2 + ty) * LANES + (z >> 1)


def forward_one_kernel(
    part_ref, coef_ref, colors_ref, rya, ryb, rxb, rxa, perf_cell_ref, perf_well_ref, perf_in_ref,
    full_ref, sya, syb, sxb, sxa, table_ref,
):
    faces = (sya, syb, sxb, sxa)
    table_ref[...] = jnp.zeros((EXTRA, LANES), jnp.float32)
    table_ref[0:1, 0:PERFS] = perf_place(perf_cell_ref[...]).astype(jnp.float32)
    table_ref[1:2, 0:PERFS] = perf_well_ref[...].astype(jnp.float32)
    for a in range(3):
        table_ref[2 + a * 3 : 5 + a * 3, 0:PERFS] = perf_in_ref[a]
    remote_kernel(1, 1, part_ref, coef_ref, colors_ref, rya, ryb, rxb, rxa, full_ref, *faces)
    for target, start, step in ((sya, 4, 2), (syb, 5, 2), (sxb, 6, 1), (sxa, 4, 1)):
        target[SENT : SENT + EXTRA, :] = table_ref[...]
        if target.shape[0] > SENT + EXTRA:
            target[SENT + EXTRA :, :] = jnp.zeros((target.shape[0] - SENT - EXTRA, LANES), jnp.float32)
        for t in range(2):
            d = start + t * step
            row = SENT + 11 + t
            target[row : row + 1, :] = colors_ref[d : d + 1, :].astype(jnp.float32)


def forward_two_kernel(
    part_ref, coef_ref, colors_ref, rya, ryb, rxb, rxa, table_ref,
    full_ref, sya, syb, sxb, sxa, tables_ref,
):
    faces = (sya, syb, sxb, sxa)
    remote_kernel(0, 2, part_ref, coef_ref, colors_ref, rya, ryb, rxb, rxa, full_ref, *faces)
    tables_ref[0] = table_ref[...]
    for i, ref in enumerate((rya, ryb, rxb, rxa)):
        tables_ref[i + 1] = ref[SENT : SENT + EXTRA, :]


def hot(index, count, start=0, step=LANES):
    rows = lax.broadcasted_iota(jnp.int32, (count, index.shape[1]), 0)
    rows = start + (rows >> 7) * step + (rows & (LANES - 1))
    return jnp.where(rows == index, 1.0, 0.0).astype(jnp.bfloat16)


def halves(values):
    high = values.astype(jnp.bfloat16)
    return high, (values - high.astype(jnp.float32)).astype(jnp.bfloat16)


def dot_ones(parts, ones, dims):
    return sum(
        lax.dot_general(part, ones, (dims, ((), ())), preferred_element_type=jnp.float32)
        for part in parts
    )


def well_bits():
    slab = lax.axis_index("slab")
    return slab & 1, slab >> 3, (slab >> 1) & 3


def core_wells(shape, core):
    rows = lax.broadcasted_iota(jnp.int32, shape, 0)
    return (rows >> 3) * 16 + core * 8 + (rows & 7)


def own_row(j):
    return well_bits()[2] * 8 + lax.axis_index("col") * 2 + j


def planes_at_perfs(ref, cls, place):
    total = None
    for tx in range(2):
        planes = [ref[tx * 2 + ty].reshape(3 * RHS, LANES) for ty in range(2)]
        ones = hot(place, 2 * LANES, (cls * 4 + tx * 2) * LANES)
        term = dot_ones(halves(jnp.concatenate(planes, axis=1)), ones, ((1,), (0,)))
        total = term if total is None else total + term
    return total


def forward_three_local_kernel(
    base_ref, coef_ref, sya, syb, q_ref, u_ref, colors_ref, perf_cell_ref, part_ref, even_ref, at_ref
):
    local_kernel(1, base_ref, coef_ref, sya, syb, part_ref)
    for n in range(4):
        is_two = colors_ref[n : n + 1, :] == 2
        for b in range(3):
            even_ref[n, b] = jnp.where(is_two, u_ref[n, b], q_ref[n, b])
    at_ref[...] = planes_at_perfs(even_ref, 0, perf_place(perf_cell_ref[...]))


def forward_three_kernel(
    part_ref, t_ref, coef_ref, colors_ref, rya, ryb, rxb, rxa,
    perf_cell_ref, perf_well_ref, perf_out_ref, well_rhs_ref, at_even_ref,
    odd_ref, keep_ref, send_ref, at_ref,
):
    for tx, ty in lines():
        n = tx * 2 + ty
        d = 4 + n

        def body(rows, tx=tx, ty=ty, n=n, d=d):
            part = pl.ds(rows, ROWS)
            acc = [part_ref[n, b, part, :] for b in range(3)]
            acc = add_remote(acc, coef_ref, 1, tx, ty, *from_halos((rya, ryb, rxb, rxa), rows))
            is_one = colors_ref[d : d + 1, :] == 1
            for b in range(3):
                value = jnp.where(is_one, t_ref[n, b, part, :], acc[b])
                odd_ref[n, b, part, :] = value

        chunks(body)
    at_perfs = at_even_ref[...] + planes_at_perfs(odd_ref, 1, perf_place(perf_cell_ref[...]))
    for b in range(3):
        at_ref[b * RHS : (b + 1) * RHS, :] = sum(
            perf_out_ref[a, b : b + 1, :] * at_perfs[a * RHS : (a + 1) * RHS] for a in range(3)
        )
    core, _, _ = well_bits()
    device = lax.axis_index("slab") * lax.axis_size("col") + lax.axis_index("col")
    parts = halves(at_ref[...])
    count = keep_ref.shape[0]
    for ref, which in ((keep_ref, core), (send_ref, 1 - core)):
        wells = jnp.where(core_wells((count, PERFS), which) == perf_well_ref[...], 1.0, 0.0)
        total = sum(
            lax.dot_general(
                wells.astype(jnp.bfloat16), part, (((1,), (1,)), ((), ())),
                preferred_element_type=jnp.float32,
            )
            for part in parts
        )
        is_own = [core_wells((count, LANES), which) == device * 2 + j for j in range(2)]
        for b in range(3):
            own = sum(jnp.where(is_own[j], well_rhs_ref[b, j : j + 1, :], 0.0) for j in range(2))
            ref[:, b * LANES : (b + 1) * LANES] = own - total[:, b * LANES : (b + 1) * LANES]


def core_sum_kernel(keep_ref, got_ref, odd_ref, *outs):
    *outs, sya, syb = outs
    for tx, ty in lines():
        for e in range(3):
            (syb if ty else sya)[at_face(tx, e, 0, RHS), :] = odd_ref[tx * 2 + ty, e]
    for face in (sya, syb):
        face[SENT:, :] = jnp.zeros((EXTRA, LANES), jnp.float32)
    _, z_spot, _ = well_bits()
    count = outs[0].shape[0]
    for m, out in enumerate(outs):
        rows = pl.ds(pl.multiple_of((z_spot ^ m) * count, count), count)
        out[0:count, :] = keep_ref[rows, :] + got_ref[rows, :]
        if out.shape[0] > count:
            out[count:, :] = jnp.zeros((out.shape[0] - count, out.shape[1]), jnp.float32)


def sum_of(refs):
    a, b, c, d = (ref[0:BLOCK, :] for ref in refs)
    return (a + b) + (c + d)


def store_twice(value, out, far_out, lanes=slice(None)):
    out[:, lanes] = value
    far_out[0:BLOCK, lanes] = value


def z_sum_kernel(a, b, c, d, well_piv_ref, out_ref, far_ref):
    far_ref[BLOCK:, :] = jnp.zeros((SLICE, WIDE), jnp.float32)
    store_twice(sum_of((a, b, c, d)), out_ref, far_ref, slice(0, 3 * LANES))
    rows = lax.broadcasted_iota(jnp.int32, (BLOCK, LANES), 0)
    blocks = sum(jnp.where(rows == own_row(j), well_piv_ref[j : j + 1, :], 0.0) for j in range(2))
    store_twice(blocks, out_ref, far_ref, slice(3 * LANES, WIDE))


def y_sum_kernel(a, b, c, d, odd_ref, rya, ryb, out_ref, far_ref, sxb, sxa):
    far_ref[BLOCK:, :] = jnp.zeros((SLICE, WIDE), jnp.float32)
    store_twice(sum_of((a, b, c, d)), out_ref, far_ref)
    for tx, ty in lines():
        for e in range(3):
            (sxb if tx else sxa)[at_face(ty, e, 0, RHS), :] = odd_ref[tx * 2 + ty, e]


def stack_kernel(*refs):
    for i, ref in enumerate(refs[:4]):
        refs[-1][i * BLOCK : (i + 1) * BLOCK, :] = ref[0:BLOCK, :]


def solve_kernel(a, b, c, d, out_ref, far_ref, own_ref):
    total = sum_of((a, b, c, d))
    far_ref[BLOCK:, :] = jnp.zeros((SLICE, 3 * LANES), jnp.float32)
    rows = lax.broadcasted_iota(jnp.int32, (BLOCK, LANES), 0)
    for e in range(3):
        lanes = slice(e * LANES, (e + 1) * LANES)
        value = sum(
            total[:, 3 * LANES + i * 3 + e : 3 * LANES + i * 3 + e + 1]
            * total[:, i * LANES : (i + 1) * LANES]
            for i in range(3)
        )
        store_twice(value, out_ref, far_ref, lanes)
        for j in range(2):
            found = jnp.where(rows == own_row(j), value, 0.0)
            own_ref[e, j : j + 1, :] = jnp.sum(found, axis=0, keepdims=True)


def backward_two_kernel(
    wells_ref, other_ref, even_ref, odd_ref, colors_ref, coef_ref, rya, ryb, rxb, rxa, tables_ref,
    u_ref, x_odd_ref, sya, syb, sxb, sxa, fix_ref, x_even_ref, three_ref, hya, hyb, hxb, hxa,
):
    core, z_spot, _ = well_bits()

    def place_of_well(well):
        return (
            ((((well >> 3) & 1) ^ core) << 7)
            | ((((well >> 6) & 3) ^ z_spot) << 5)
            | (((well >> 4) & 3) << 3)
            | (well & 7)
        )

    wells = halves(jnp.concatenate([wells_ref[...].T, other_ref[...].T], axis=1))
    tables = [tables_ref[i] for i in range(5)]
    for first in (0, 2, 4):
        pair = tables[first : first + 2]
        well = jnp.concatenate([table[1:2] for table in pair], axis=1).astype(jnp.int32)
        at_perfs = dot_ones(wells, hot(place_of_well(well), 2 * LANES), ((1,), (0,)))
        for i, table in enumerate(pair):
            for b in range(3):
                fix = sum(
                    table[2 + a * 3 + b : 3 + a * 3 + b]
                    * at_perfs[a * RHS : (a + 1) * RHS, i * LANES : (i + 1) * LANES]
                    for a in range(3)
                )
                for part, value in enumerate(halves(fix)):
                    lanes = slice(part * LANES, (part + 1) * LANES)
                    fix_ref[first + i, b * RHS : (b + 1) * RHS, lanes] = value

    def spread(group, start, step):
        place = tables[group][0:1].astype(jnp.int32)
        ones = hot(place, 2 * LANES, start * LANES, step * LANES)
        return lax.dot_general(
            fix_ref[group], jnp.concatenate([ones, ones], axis=1),
            (((1,), (1,)), ((), ())), preferred_element_type=jnp.float32,
        )

    for cls, ref, out in ((1, odd_ref, x_odd_ref), (0, even_ref, x_even_ref)):
        for tx in range(2):
            fix = spread(0, cls * 4 + tx * 2, 1)
            for ty in range(2):
                n = tx * 2 + ty
                d = cls * 4 + n
                for b in range(3):
                    value = ref[n, b] - fix[b * RHS : (b + 1) * RHS, ty * LANES : (ty + 1) * LANES]
                    out[n, b] = value
                    if cls == 1:
                        three_ref[n, b] = jnp.where(colors_ref[d : d + 1, :] == 3, value, 0.0)
    for i, (halo, out, start, step) in enumerate(
        ((rya, hya, 4, 2), (ryb, hyb, 5, 2), (rxb, hxb, 6, 1), (rxa, hxa, 4, 1))
    ):
        fix = spread(i + 1, start, step)
        for t in range(2):
            mask = tables[i + 1][11 + t : 12 + t] == 3.0
            for b in range(3):
                value = halo[at_face(t, b, 0, RHS), :]
                value = value - fix[b * RHS : (b + 1) * RHS, t * LANES : (t + 1) * LANES]
                out[at_face(t, b, 0, RHS), :] = jnp.where(mask, value, 0.0)
    for tx, ty in lines():
        n = tx * 2 + ty

        def body(rows, tx=tx, ty=ty, n=n):
            acc = [x_even_ref[n, b, pl.ds(rows, ROWS), :] for b in range(3)]
            acc = add_local(
                acc, coef_ref, 0, tx, ty,
                lambda i, j, a: three_ref[i * 2 + j, a, pl.ds(rows, ROWS), :],
            )
            acc = add_remote(acc, coef_ref, 0, tx, ty, *from_halos((hya, hyb, hxb, hxa), rows))
            mask = colors_ref[n : n + 1, :] == 2
            for b in range(3):
                u_ref[n, b, pl.ds(rows, ROWS), :] = acc[b]
                store_faces((sya, syb, sxb, sxa), tx, ty, b, rows, jnp.where(mask, acc[b], 0.0))

        chunks(body)


def last_kernel(
    part_ref, u_ref, odd_three, odd_v, coef_ref, colors_ref, rya, ryb, rxb, rxa, out_hbm, out_ref, sems
):
    steps = RHS // ROWS

    def out_copy(i, b):
        part = pl.ds((b * RHS + i * ROWS) * SLICE, ROWS * SLICE)
        return pltpu.make_async_copy(out_ref.at[part], out_hbm.at[part], sems.at[i * 3 + b])

    def step(i, carry):
        rows = pl.multiple_of(i * ROWS, ROWS)
        part = pl.ds(rows, ROWS)
        for tx, ty in lines():
            n = tx * 2 + ty
            x, y = line_xy(tx, ty)
            flip = xor(x, y)
            acc = [part_ref[n, b, part, :] for b in range(3)]
            acc = add_remote(acc, coef_ref, 0, tx, ty, *from_halos((rya, ryb, rxb, rxa), rows))
            is_two = colors_ref[n : n + 1, :] == 2
            is_one = colors_ref[4 + n : 5 + n, :] == 1
            for b in range(3):
                even = jnp.where(is_two, u_ref[n, b, part, :], acc[b])
                odd = jnp.where(is_one, odd_v[n, b, part, :], odd_three[n, b, part, :])
                z_even = jnp.where(flip == 1, odd, even)
                z_odd = jnp.where(flip == 1, even, odd)
                for half in range(2):
                    start = (b * RHS + rows) * SLICE + x * 4 + half * 2 + y
                    out_ref[pl.ds(start, ROWS, stride=SLICE), :] = join_z(z_even, z_odd, half)
        for b in range(3):
            out_copy(i, b).start()
        return carry

    lax.fori_loop(0, steps, step, 0)
    for i in range(steps):
        for b in range(3):
            out_copy(i, b).wait()


def pairs(axis, second):
    count = lax.axis_size(axis)
    found = []
    for i in range(second, count, 2):
        found += [(i, (i + 1) % count), ((i + 1) % count, i)]
    return found


def swap(value, axis, mask):
    return lax.ppermute(value, axis, [(i, i ^ mask) for i in range(lax.axis_size(axis))])


def exchange(sya, syb, sxb, sxa):
    rya = lax.ppermute(sya, "col", pairs("col", 0))
    ryb = lax.ppermute(syb, "col", pairs("col", 1))
    rxb = lax.ppermute(sxb, "slab", pairs("slab", 1))
    rxa = lax.ppermute(sxa, "slab", pairs("slab", 0))
    return rya, ryb, rxb, rxa


def to_rows(array):
    lead = array.shape[:-3]
    split = array.reshape(lead + (2, 2, 2, LANES))
    return jnp.swapaxes(split, -3, -2).reshape(-1, LANES)


def from_rows(rows):
    split = rows.reshape(3, RHS, 2, 2, 2, LANES)
    return jnp.swapaxes(split, -3, -2).reshape(3, RHS, 2, 2, 2 * LANES)


def per_device(
    cell_rhs, well_rhs, cell_colors, incoming, pivot_inv,
    perf_cell, perf_well, perf_out, perf_in, well_pivot_inv,
):
    rhs = to_rows(cell_rhs)
    colors_in = to_rows(cell_colors)
    inc = to_rows(incoming)
    piv = to_rows(pivot_inv)
    place = perf_cell.reshape(1, PERFS)
    well = perf_well.reshape(1, PERFS)
    out_blocks = jnp.transpose(perf_out, (1, 2, 0))
    in_blocks = jnp.transpose(perf_in, (1, 2, 0))
    well_side = jnp.transpose(well_rhs, (1, 0, 2))
    tiles = pltpu.VMEM((17 * SLICE, LANES), jnp.float32)
    color_tile = pltpu.VMEM((9 * SLICE, LANES), jnp.int32)
    block_tiles = pltpu.VMEM((57 * SLICE, LANES), jnp.float32)
    piv_in = pltpu.VMEM((9 * SLICE, LANES), jnp.float32)
    color_in = pltpu.VMEM((SLICE, LANES), jnp.int32)
    whole = pltpu.VMEM((3 * RHS * SLICE, LANES), jnp.float32)
    steps = RHS // ROWS

    def local(cls, base, coef, s, name):
        def body(*refs):
            local_kernel(cls, *refs)

        return call(body, PLANES, (base, coef, *s[:2]), name=name)

    q_even, *s = call(
        first_kernel,
        [PLANES] + FACES,
        [pltpu.with_memory_space_constraint(v, pltpu.HBM) for v in (rhs, piv, colors_in)],
        [whole, piv_in, color_in, tiles, color_tile, pltpu.SemaphoreType.DMA((2 + 3 * steps,))],
        name="even_rhs",
        hbm=(0, 1, 2),
    )
    halo = exchange(*s)
    part, fwd, bwd, colors, well_piv = call(
        second_kernel,
        [PLANES, COEF, COEF, jax.ShapeDtypeStruct((8, LANES), jnp.int32), f32(8, LANES)],
        (rhs, piv, colors_in, inc, *s[:2], jnp.transpose(well_pivot_inv, (1, 0, 2))),
        [tiles, color_tile, block_tiles, block_tiles],
        name="blocks_and_local",
    )
    t_odd, *s, table = call(
        forward_one_kernel,
        [PLANES] + FACES_PLUS + [f32(EXTRA, LANES)],
        (part, fwd, colors, *halo, place, well, in_blocks),
        name="forward_one",
    )
    part = local(0, q_even, fwd, s, "forward_two_local")
    halo = exchange(*s)
    u_even, *s, tables = call(
        forward_two_kernel,
        [PLANES] + FACES + [f32(5, EXTRA, LANES)],
        (part, fwd, colors, *halo, table),
        name="forward_two",
    )
    part, even, at_even = call(
        forward_three_local_kernel,
        [PLANES, PLANES, f32(3 * RHS, PERFS)],
        (t_odd, fwd, *s[:2], q_even, u_even, colors, place),
        name="forward_three_local",
    )
    halo = exchange(*s)
    odd, keep, send = call(
        forward_three_kernel,
        [PLANES, f32(4 * BLOCK, 3 * LANES), f32(4 * BLOCK, 3 * LANES)],
        (part, t_odd, fwd, colors, *halo, place, well, out_blocks, well_side, at_even),
        [pltpu.VMEM((3 * RHS, PERFS), jnp.float32)],
        name="forward_three_wells",
    )
    narrow = [f32(BLOCK + (SLICE if m == 2 else 0), 3 * LANES) for m in range(4)]
    wide = [f32(BLOCK, WIDE), f32(BLOCK + SLICE, WIDE)]

    def swaps(near, far, axis, unit):
        return [swap(far if m == 2 else near, axis, unit * m) for m in (1, 2, 3)]

    *blocks, sya, syb = call(
        core_sum_kernel, narrow + [FACE_PLUS] * 2, (keep, swap(send, "slab", 1), odd), name="core_sum"
    )
    halo = [lax.ppermute(face, "col", pairs("col", i)) for i, face in enumerate((sya, syb))]
    moved = [swap(blocks[m], "slab", 8 * m) for m in (1, 2, 3)]
    mine, far = call(z_sum_kernel, wide, (blocks[0], *moved, well_piv), name="z_sum")
    mine, far, sxb, sxa = call(
        y_sum_kernel,
        wide + [FACE, FACE],
        (mine, *swaps(mine, far, "slab", 2), odd, *halo),
        name="y_sum",
        hbm=(5, 6),
    )
    halo.append(lax.ppermute(sxb, "slab", pairs("slab", 1)))
    halo.append(lax.ppermute(sxa, "slab", pairs("slab", 0)))
    mine, far, own_wells = call(
        solve_kernel,
        [narrow[0], narrow[2], f32(3, 2, RHS)],
        (mine, *swaps(mine, far, "col", 1)),
        name="solve_wells",
    )
    near = call(
        stack_kernel, f32(4 * BLOCK, 3 * LANES), (mine, *swaps(mine, far, "slab", 8)), name="stack"
    )
    far = swap(near, "slab", 1)
    u_even, x_odd, *s = call(
        backward_two_kernel,
        [PLANES, PLANES] + FACES,
        (near, far, even, odd, colors, bwd, *halo, tables),
        [pltpu.VMEM((5, 3 * RHS, 2 * LANES), jnp.bfloat16)]
        + [pltpu.VMEM(PLANES.shape, jnp.float32)] * 2
        + [pltpu.VMEM(FACE.shape, jnp.float32)] * 4,
        name="well_fix_backward_two",
    )
    part = local(1, x_odd, bwd, s, "backward_one_local")
    halo = exchange(*s)

    def backward_one(*refs):
        remote_kernel(1, 1, *refs)

    v_odd, *s = call(
        backward_one, [PLANES] + FACES, (part, bwd, colors, *halo), name="backward_one"
    )
    part = local(0, u_even, bwd, s, "backward_zero_local")
    halo = exchange(*s)
    rows = call(
        last_kernel,
        f32(3 * RHS * SLICE, LANES),
        (part, u_even, x_odd, v_odd, bwd, colors, *halo),
        [whole, pltpu.SemaphoreType.DMA((3 * steps,))],
        name="backward_zero",
        hbm_out=True,
    )
    return from_rows(rows), jnp.transpose(own_wells, (1, 0, 2))


def solution(mesh):
    placed = (
        P(None, None, "slab", "col", None),
        P(("slab", "col"), None, None),
        P("slab", "col", None),
        P(None, None, None, "slab", "col", None),
        P(None, None, "slab", "col", None),
        P(("slab", "col")),
        P(("slab", "col")),
        P(("slab", "col"), None, None),
        P(("slab", "col"), None, None),
        P(("slab", "col"), None, None),
    )
    return jax.shard_map(
        per_device,
        mesh=mesh,
        in_specs=placed,
        out_specs=(P(None, None, "slab", "col", None), P(("slab", "col"), None, None)),
        check_vma=False,
    )
```

```python
import jax
import jax.numpy as jnp
from jax import lax
from jax.experimental import pallas as pl
from jax.experimental.pallas import tpu as pltpu
from jax.sharding import PartitionSpec as P

RHS = 128
LANES = 128
ROWS = 64
SLICE = 8
FACE_RX, FACE_LX, FACE_RY, FACE_LY, FACE_ZU, FACE_ZS = range(6)
PERFS = 64
SENT = 6 * RHS
EXTRA = 16
WIDE = 4 * LANES
BLOCK = 32


def f32(*shape):
    return jax.ShapeDtypeStruct(shape, jnp.float32)


PLANES = f32(4, 3, RHS, LANES)
FACE = f32(SENT, LANES)
FACE_PLUS = f32(SENT + EXTRA, LANES)
PAST = (8, 16, 0, 0)
FACES = [f32(SENT + past, LANES) for past in PAST]
FACES_PLUS = [f32(SENT + EXTRA + past, LANES) for past in PAST]
COEF = f32(8, 54, LANES)


def call(body, outs, args, scratch=(), name=None, hbm=(), hbm_out=False):
    spaces = [pltpu.HBM if i in hbm else pltpu.VMEM for i in range(len(args))]
    out_space = pltpu.HBM if hbm_out else pltpu.VMEM
    return pl.pallas_call(
        body,
        out_shape=outs,
        in_specs=[pl.BlockSpec(memory_space=space) for space in spaces],
        out_specs=jax.tree.map(lambda _: pl.BlockSpec(memory_space=out_space), outs),
        scratch_shapes=list(scratch),
        compiler_params=pltpu.CompilerParams(vmem_limit_bytes=16 * 1024 * 1024),
        cost_estimate=pl.CostEstimate(flops=1_000_000, bytes_accessed=2_000_000, transcendentals=0),
        name=name,
    )(*args)


def spots():
    return lax.rem(lax.axis_index("slab"), 2), lax.rem(lax.axis_index("col"), 2)


def line_xy(tx, ty):
    sp, cp = spots()
    x = sp if tx else 1 - sp
    y = cp if ty else 1 - cp
    return x, y


def xor(a, b):
    return a + b - 2 * a * b


def lane_iota(rows):
    return lax.broadcasted_iota(jnp.int32, (rows, LANES), 1)


def pick(values, index):
    return jnp.take_along_axis(values, index, axis=1)


def split_z(low, high, odd):
    lane = lane_iota(low.shape[0])
    index = (2 * lane + odd) & (LANES - 1)
    return jnp.where(lane < LANES // 2, pick(low, index), pick(high, index))


def join_z(even, odd, half):
    lane = lane_iota(even.shape[0])
    index = half * (LANES // 2) + (lane >> 1)
    return jnp.where((lane & 1) == 0, pick(even, index), pick(odd, index))


def line_rows(ref, start, count):
    return ref[pl.ds(start, count, stride=SLICE), :]


def tile_split(tile):
    lane = lane_iota(SLICE)
    part = (lax.broadcasted_iota(jnp.int32, (SLICE, LANES), 0) >> 1) & 1
    even = pick(tile, (2 * lane) & (LANES - 1))
    odd = pick(tile, (2 * lane + 1) & (LANES - 1))
    low = lane < LANES // 2
    of_even = jnp.where(low, even, pltpu.roll(even, SLICE - 2, 0))
    of_odd = jnp.where(low, pltpu.roll(odd, 2, 0), odd)
    return jnp.where(part == 0, of_even, of_odd)


def split_tiles(source, target, count):
    for row in range(count):
        target[row * 8 : row * 8 + 8, :] = tile_split(source[row * 8 : row * 8 + 8, :])


def pivoted(rhs_ref, piv, cls, tx, ty, rows):
    x, y = line_xy(tx, ty)
    odd = xor(xor(x, y), cls)
    planes = []
    for a in range(3):
        base = (a * RHS + rows) * SLICE + x * 4 + y
        planes.append(
            split_z(line_rows(rhs_ref, base, ROWS), line_rows(rhs_ref, base + 2, ROWS), odd)
        )
    return [
        piv[0 * 3 + b] * planes[0] + piv[1 * 3 + b] * planes[1] + piv[2 * 3 + b] * planes[2]
        for b in range(3)
    ]


def class_rows(ref, cls, tx, ty, count):
    x, y = line_xy(tx, ty)
    odd = xor(xor(x, y), cls)
    return ref[pl.ds(x * 4 + odd * 2 + y, count, stride=SLICE), :]


def chunks(body):
    def step(i, carry):
        body(pl.multiple_of(i * ROWS, ROWS))
        return carry

    lax.fori_loop(0, RHS // ROWS, step, 0)


def lines():
    return [(tx, ty) for tx in range(2) for ty in range(2)]


def at_face(t, b, rows, count=ROWS):
    return pl.ds((t * 3 + b) * RHS + rows, count)


def from_sy(sya, syb, rows):
    return lambda tx, ty, a: (syb if ty else sya)[at_face(tx, a, rows), :]


def from_halos(halos, rows):
    rya, ryb, rxb, rxa = halos
    return (
        lambda tx, ty, a: (rxb if tx else rxa)[at_face(ty, a, rows), :],
        lambda tx, ty, a: (ryb if ty else rya)[at_face(tx, a, rows), :],
    )


def take(acc, coef, d, face, a, value):
    for b in range(3):
        row = face * 9 + a * 3 + b
        acc[b] = acc[b] - coef[d, row : row + 1, :] * value


def add_local(acc, coef, cls, tx, ty, get):
    x, y = line_xy(tx, ty)
    odd = xor(xor(x, y), cls)
    index = (lane_iota(ROWS) + (LANES - 1) + 2 * odd) & (LANES - 1)
    d = cls * 4 + tx * 2 + ty
    for a in range(3):
        center = get(tx, ty, a)
        take(acc, coef, d, FACE_LX, a, get(1 - tx, ty, a))
        take(acc, coef, d, FACE_LY, a, get(tx, 1 - ty, a))
        take(acc, coef, d, FACE_ZU, a, center)
        take(acc, coef, d, FACE_ZS, a, pick(center, index))
    return acc


def add_remote(acc, coef, cls, tx, ty, get_x, get_y):
    d = cls * 4 + tx * 2 + ty
    for a in range(3):
        take(acc, coef, d, FACE_RX, a, get_x(tx, ty, a))
        take(acc, coef, d, FACE_RY, a, get_y(tx, ty, a))
    return acc


def store_faces(faces, tx, ty, b, rows, value):
    sya, syb, sxb, sxa = faces
    (syb if ty else sya)[at_face(tx, b, rows), :] = value
    (sxb if tx else sxa)[at_face(ty, b, rows), :] = value


def first_kernel(
    rhs_hbm, piv_hbm, colors_hbm, q_ref, sya, syb, sxb, sxa,
    rhs_ref, piv_ref, colors_ref, tiles, color_tile, sems,
):
    steps = RHS // ROWS

    def rhs_copy(i, a):
        part = pl.ds((a * RHS + i * ROWS) * SLICE, ROWS * SLICE)
        return pltpu.make_async_copy(rhs_hbm.at[part], rhs_ref.at[part], sems.at[2 + i * 3 + a])

    piv_copy = pltpu.make_async_copy(piv_hbm, piv_ref, sems.at[0])
    color_copy = pltpu.make_async_copy(colors_hbm, colors_ref, sems.at[1])
    piv_copy.start()
    color_copy.start()
    for i in range(steps):
        for a in range(3):
            rhs_copy(i, a).start()
    piv_copy.wait()
    split_tiles(piv_ref, tiles, 9)
    color_copy.wait()
    color_tile[0:SLICE, :] = tile_split(colors_ref[...])

    def step(i, carry):
        for a in range(3):
            rhs_copy(i, a).wait()
        rows = pl.multiple_of(i * ROWS, ROWS)
        for tx, ty in lines():
            piv_rows = class_rows(tiles, 0, tx, ty, 9)
            piv = [piv_rows[e : e + 1] for e in range(9)]
            mask = class_rows(color_tile, 0, tx, ty, 1) == 0
            for b, value in enumerate(pivoted(rhs_ref, piv, 0, tx, ty, rows)):
                q_ref[tx * 2 + ty, b, pl.ds(rows, ROWS), :] = value
                store_faces((sya, syb, sxb, sxa), tx, ty, b, rows, jnp.where(mask, value, 0.0))
        return carry

    lax.fori_loop(0, steps, step, 0)


def second_kernel(
    rhs_ref, piv_ref, colors_ref, inc_ref, sya, syb, well_piv_ref,
    part_ref, fwd_ref, bwd_ref, cls_colors_ref, well_rows_ref, tiles, color_tile, raw, folded,
):
    well_rows_ref[...] = jnp.zeros(well_rows_ref.shape, jnp.float32)
    for a in range(3):
        well_rows_ref[0:2, a * 3 : a * 3 + 3] = well_piv_ref[a]
    split_tiles(piv_ref, tiles, 9)
    color_tile[0:SLICE, :] = tile_split(colors_ref[...])
    spot = lax.broadcasted_iota(jnp.int32, (SLICE, LANES), 0)
    lane = lane_iota(SLICE)
    x_low = (spot >> 2) == 0
    y_low = (spot & 1) == 0
    z_even = ((spot >> 1) & 1) == 0
    edge = (z_even & (lane == 0)) | (jnp.logical_not(z_even) & (lane == LANES - 1))

    slab, col = lax.axis_index("slab"), lax.axis_index("col")
    inside = [
        jnp.where(low, jnp.where(at == 0, 0.0, 1.0), jnp.where(at == last, 0.0, 1.0))
        for low, at, last in (
            (x_low, slab, lax.axis_size("slab") - 1),
            (y_low, col, lax.axis_size("col") - 1),
        )
    ]

    def source(face, entry):
        row = (face * 9 + entry) * 8
        return tile_split(inc_ref[row : row + 8, :])

    piv = [tiles[i * 8 : i * 8 + 8, :] for i in range(9)]
    for group, (first, second, low) in enumerate(((0, 1, x_low), (2, 3, y_low), (5, 4, z_even))):
        one = [None] * 9
        two = [None] * 9
        for entry in range(9):
            p, q = source(first, entry), source(second, entry)
            one[entry] = jnp.where(low, p, q)
            two[entry] = jnp.where(low, q, p)
            if group < 2:
                one[entry] = one[entry] * inside[group]
            else:
                two[entry] = jnp.where(edge, 0.0, two[entry])
        for which, block in ((0, one), (1, two)):
            face = group * 2 + which
            for a in range(3):
                for b in range(3):
                    row = (face * 9 + a * 3 + b) * 8
                    raw[row : row + 8, :] = block[a * 3 + b]
                    folded[row : row + 8, :] = (
                        block[a * 3] * piv[b]
                        + block[a * 3 + 1] * piv[3 + b]
                        + block[a * 3 + 2] * piv[6 + b]
                    )
    for cls in range(2):
        for tx, ty in lines():
            d = cls * 4 + tx * 2 + ty
            fwd_ref[d] = class_rows(folded, cls, tx, ty, 54)
            bwd_ref[d] = class_rows(raw, cls, tx, ty, 54)
            cls_colors_ref[d : d + 1, :] = class_rows(color_tile, cls, tx, ty, 1)
    for tx, ty in lines():
        piv_rows = class_rows(tiles, 1, tx, ty, 9)
        piv1 = [piv_rows[i : i + 1] for i in range(9)]

        def body(rows, tx=tx, ty=ty, piv1=piv1):
            acc = pivoted(rhs_ref, piv1, 1, tx, ty, rows)
            acc = add_local(acc, fwd_ref, 1, tx, ty, from_sy(sya, syb, rows))
            for b in range(3):
                part_ref[tx * 2 + ty, b, pl.ds(rows, ROWS), :] = acc[b]

        chunks(body)


def local_kernel(cls, base_ref, coef_ref, sya, syb, part_ref):
    for tx, ty in lines():
        n = tx * 2 + ty

        def body(rows, tx=tx, ty=ty, n=n):
            acc = [base_ref[n, b, pl.ds(rows, ROWS), :] for b in range(3)]
            acc = add_local(acc, coef_ref, cls, tx, ty, from_sy(sya, syb, rows))
            for b in range(3):
                part_ref[n, b, pl.ds(rows, ROWS), :] = acc[b]

        chunks(body)


def remote_kernel(cls, color, part_ref, coef_ref, colors_ref, rya, ryb, rxb, rxa, full_ref, *faces):
    for tx, ty in lines():
        n = tx * 2 + ty
        d = cls * 4 + n

        def body(rows, tx=tx, ty=ty, n=n, d=d):
            acc = [part_ref[n, b, pl.ds(rows, ROWS), :] for b in range(3)]
            acc = add_remote(acc, coef_ref, cls, tx, ty, *from_halos((rya, ryb, rxb, rxa), rows))
            mask = colors_ref[d : d + 1, :] == color
            for b in range(3):
                full_ref[n, b, pl.ds(rows, ROWS), :] = acc[b]
                store_faces(faces, tx, ty, b, rows, jnp.where(mask, acc[b], 0.0))

        chunks(body)


def perf_place(perf_cell):
    sp, cp = spots()
    x = perf_cell >> 9
    y = (perf_cell >> 8) & 1
    z = perf_cell & 255
    cls = (x + y + z) & 1
    tx = (x + 1 - sp) & 1
    ty = (y + 1 - cp) & 1
    return (cls * 4 + tx * 2 + ty) * LANES + (z >> 1)


def forward_one_kernel(
    part_ref, coef_ref, colors_ref, rya, ryb, rxb, rxa, perf_cell_ref, perf_well_ref, perf_in_ref,
    full_ref, sya, syb, sxb, sxa, table_ref,
):
    faces = (sya, syb, sxb, sxa)
    table_ref[...] = jnp.zeros((EXTRA, LANES), jnp.float32)
    table_ref[0:1, 0:PERFS] = perf_place(perf_cell_ref[...]).astype(jnp.float32)
    table_ref[1:2, 0:PERFS] = perf_well_ref[...].astype(jnp.float32)
    for a in range(3):
        table_ref[2 + a * 3 : 5 + a * 3, 0:PERFS] = perf_in_ref[a]
    remote_kernel(1, 1, part_ref, coef_ref, colors_ref, rya, ryb, rxb, rxa, full_ref, *faces)
    for target, start, step in ((sya, 4, 2), (syb, 5, 2), (sxb, 6, 1), (sxa, 4, 1)):
        target[SENT : SENT + EXTRA, :] = table_ref[...]
        if target.shape[0] > SENT + EXTRA:
            target[SENT + EXTRA :, :] = jnp.zeros((target.shape[0] - SENT - EXTRA, LANES), jnp.float32)
        for t in range(2):
            d = start + t * step
            row = SENT + 11 + t
            target[row : row + 1, :] = colors_ref[d : d + 1, :].astype(jnp.float32)


def forward_two_kernel(
    part_ref, coef_ref, colors_ref, rya, ryb, rxb, rxa, table_ref,
    full_ref, sya, syb, sxb, sxa, tables_ref,
):
    faces = (sya, syb, sxb, sxa)
    remote_kernel(0, 2, part_ref, coef_ref, colors_ref, rya, ryb, rxb, rxa, full_ref, *faces)
    tables_ref[0] = table_ref[...]
    for i, ref in enumerate((rya, ryb, rxb, rxa)):
        tables_ref[i + 1] = ref[SENT : SENT + EXTRA, :]


def hot(index, count, start=0, step=LANES):
    rows = lax.broadcasted_iota(jnp.int32, (count, index.shape[1]), 0)
    rows = start + (rows >> 7) * step + (rows & (LANES - 1))
    return jnp.where(rows == index, 1.0, 0.0).astype(jnp.bfloat16)


def halves(values):
    high = values.astype(jnp.bfloat16)
    return high, (values - high.astype(jnp.float32)).astype(jnp.bfloat16)


def dot_ones(parts, ones, dims):
    return sum(
        lax.dot_general(part, ones, (dims, ((), ())), preferred_element_type=jnp.float32)
        for part in parts
    )


def well_bits():
    slab = lax.axis_index("slab")
    return slab & 1, slab >> 3, (slab >> 1) & 3


def core_wells(shape, core):
    rows = lax.broadcasted_iota(jnp.int32, shape, 0)
    return (rows >> 3) * 16 + core * 8 + (rows & 7)


def own_row(j):
    return well_bits()[2] * 8 + lax.axis_index("col") * 2 + j


def planes_at_perfs(ref, cls, place):
    total = None
    for tx in range(2):
        planes = [ref[tx * 2 + ty].reshape(3 * RHS, LANES) for ty in range(2)]
        ones = hot(place, 2 * LANES, (cls * 4 + tx * 2) * LANES)
        term = dot_ones(halves(jnp.concatenate(planes, axis=1)), ones, ((1,), (0,)))
        total = term if total is None else total + term
    return total


def forward_three_local_kernel(
    base_ref, coef_ref, sya, syb, q_ref, u_ref, colors_ref, perf_cell_ref, part_ref, even_ref, at_ref
):
    local_kernel(1, base_ref, coef_ref, sya, syb, part_ref)
    for n in range(4):
        is_two = colors_ref[n : n + 1, :] == 2
        for b in range(3):
            even_ref[n, b] = jnp.where(is_two, u_ref[n, b], q_ref[n, b])
    at_ref[...] = planes_at_perfs(even_ref, 0, perf_place(perf_cell_ref[...]))


def forward_three_kernel(
    part_ref, t_ref, coef_ref, colors_ref, rya, ryb, rxb, rxa,
    perf_cell_ref, perf_well_ref, perf_out_ref, well_rhs_ref, at_even_ref,
    odd_ref, keep_ref, send_ref, at_ref,
):
    for tx, ty in lines():
        n = tx * 2 + ty
        d = 4 + n

        def body(rows, tx=tx, ty=ty, n=n, d=d):
            part = pl.ds(rows, ROWS)
            acc = [part_ref[n, b, part, :] for b in range(3)]
            acc = add_remote(acc, coef_ref, 1, tx, ty, *from_halos((rya, ryb, rxb, rxa), rows))
            is_one = colors_ref[d : d + 1, :] == 1
            for b in range(3):
                value = jnp.where(is_one, t_ref[n, b, part, :], acc[b])
                odd_ref[n, b, part, :] = value

        chunks(body)
    at_perfs = at_even_ref[...] + planes_at_perfs(odd_ref, 1, perf_place(perf_cell_ref[...]))
    for b in range(3):
        at_ref[b * RHS : (b + 1) * RHS, :] = sum(
            perf_out_ref[a, b : b + 1, :] * at_perfs[a * RHS : (a + 1) * RHS] for a in range(3)
        )
    core, _, _ = well_bits()
    device = lax.axis_index("slab") * lax.axis_size("col") + lax.axis_index("col")
    parts = halves(at_ref[...])
    count = keep_ref.shape[0]
    for ref, which in ((keep_ref, core), (send_ref, 1 - core)):
        wells = jnp.where(core_wells((count, PERFS), which) == perf_well_ref[...], 1.0, 0.0)
        total = sum(
            lax.dot_general(
                wells.astype(jnp.bfloat16), part, (((1,), (1,)), ((), ())),
                preferred_element_type=jnp.float32,
            )
            for part in parts
        )
        is_own = [core_wells((count, LANES), which) == device * 2 + j for j in range(2)]
        for b in range(3):
            own = sum(jnp.where(is_own[j], well_rhs_ref[b, j : j + 1, :], 0.0) for j in range(2))
            ref[:, b * LANES : (b + 1) * LANES] = own - total[:, b * LANES : (b + 1) * LANES]


def core_sum_kernel(keep_ref, got_ref, odd_ref, *outs):
    *outs, sya, syb = outs
    for tx, ty in lines():
        for e in range(3):
            (syb if ty else sya)[at_face(tx, e, 0, RHS), :] = odd_ref[tx * 2 + ty, e]
    for face in (sya, syb):
        face[SENT:, :] = jnp.zeros((EXTRA, LANES), jnp.float32)
    _, z_spot, _ = well_bits()
    count = outs[0].shape[0]
    for m, out in enumerate(outs):
        rows = pl.ds(pl.multiple_of((z_spot ^ m) * count, count), count)
        out[0:count, :] = keep_ref[rows, :] + got_ref[rows, :]
        if out.shape[0] > count:
            out[count:, :] = jnp.zeros((out.shape[0] - count, out.shape[1]), jnp.float32)


def sum_of(refs):
    a, b, c, d = (ref[0:BLOCK, :] for ref in refs)
    return (a + b) + (c + d)


def store_twice(value, out, far_out, lanes=slice(None)):
    out[:, lanes] = value
    far_out[0:BLOCK, lanes] = value


def z_sum_kernel(a, b, c, d, well_piv_ref, out_ref, far_ref):
    far_ref[BLOCK:, :] = jnp.zeros((SLICE, WIDE), jnp.float32)
    store_twice(sum_of((a, b, c, d)), out_ref, far_ref, slice(0, 3 * LANES))
    rows = lax.broadcasted_iota(jnp.int32, (BLOCK, LANES), 0)
    blocks = sum(jnp.where(rows == own_row(j), well_piv_ref[j : j + 1, :], 0.0) for j in range(2))
    store_twice(blocks, out_ref, far_ref, slice(3 * LANES, WIDE))


def y_sum_kernel(a, b, c, d, odd_ref, rya, ryb, out_ref, far_ref, sxb, sxa):
    far_ref[BLOCK:, :] = jnp.zeros((SLICE, WIDE), jnp.float32)
    store_twice(sum_of((a, b, c, d)), out_ref, far_ref)
    for tx, ty in lines():
        for e in range(3):
            (sxb if tx else sxa)[at_face(ty, e, 0, RHS), :] = odd_ref[tx * 2 + ty, e]


def stack_kernel(*refs):
    for i, ref in enumerate(refs[:4]):
        refs[-1][i * BLOCK : (i + 1) * BLOCK, :] = ref[0:BLOCK, :]


def solve_kernel(a, b, c, d, out_ref, far_ref, own_ref):
    total = sum_of((a, b, c, d))
    far_ref[BLOCK:, :] = jnp.zeros((SLICE, 3 * LANES), jnp.float32)
    rows = lax.broadcasted_iota(jnp.int32, (BLOCK, LANES), 0)
    for e in range(3):
        lanes = slice(e * LANES, (e + 1) * LANES)
        value = sum(
            total[:, 3 * LANES + i * 3 + e : 3 * LANES + i * 3 + e + 1]
            * total[:, i * LANES : (i + 1) * LANES]
            for i in range(3)
        )
        store_twice(value, out_ref, far_ref, lanes)
        for j in range(2):
            found = jnp.where(rows == own_row(j), value, 0.0)
            own_ref[e, j : j + 1, :] = jnp.sum(found, axis=0, keepdims=True)


def backward_two_kernel(
    wells_ref, other_ref, even_ref, odd_ref, colors_ref, coef_ref, rya, ryb, rxb, rxa, tables_ref,
    u_ref, x_odd_ref, sya, syb, sxb, sxa, fix_ref, x_even_ref, three_ref, hya, hyb, hxb, hxa,
):
    core, z_spot, _ = well_bits()

    def place_of_well(well):
        return (
            ((((well >> 3) & 1) ^ core) << 7)
            | ((((well >> 6) & 3) ^ z_spot) << 5)
            | (((well >> 4) & 3) << 3)
            | (well & 7)
        )

    wells = halves(jnp.concatenate([wells_ref[...].T, other_ref[...].T], axis=1))
    tables = [tables_ref[i] for i in range(5)]
    for first in (0, 2, 4):
        pair = tables[first : first + 2]
        well = jnp.concatenate([table[1:2] for table in pair], axis=1).astype(jnp.int32)
        at_perfs = dot_ones(wells, hot(place_of_well(well), 2 * LANES), ((1,), (0,)))
        for i, table in enumerate(pair):
            for b in range(3):
                fix = sum(
                    table[2 + a * 3 + b : 3 + a * 3 + b]
                    * at_perfs[a * RHS : (a + 1) * RHS, i * LANES : (i + 1) * LANES]
                    for a in range(3)
                )
                for part, value in enumerate(halves(fix)):
                    lanes = slice(part * LANES, (part + 1) * LANES)
                    fix_ref[first + i, b * RHS : (b + 1) * RHS, lanes] = value

    def spread(group, start, step):
        place = tables[group][0:1].astype(jnp.int32)
        ones = hot(place, 2 * LANES, start * LANES, step * LANES)
        return lax.dot_general(
            fix_ref[group], jnp.concatenate([ones, ones], axis=1),
            (((1,), (1,)), ((), ())), preferred_element_type=jnp.float32,
        )

    for cls, ref, out in ((1, odd_ref, x_odd_ref), (0, even_ref, x_even_ref)):
        for tx in range(2):
            fix = spread(0, cls * 4 + tx * 2, 1)
            for ty in range(2):
                n = tx * 2 + ty
                d = cls * 4 + n
                for b in range(3):
                    value = ref[n, b] - fix[b * RHS : (b + 1) * RHS, ty * LANES : (ty + 1) * LANES]
                    out[n, b] = value
                    if cls == 1:
                        three_ref[n, b] = jnp.where(colors_ref[d : d + 1, :] == 3, value, 0.0)
    for i, (halo, out, start, step) in enumerate(
        ((rya, hya, 4, 2), (ryb, hyb, 5, 2), (rxb, hxb, 6, 1), (rxa, hxa, 4, 1))
    ):
        fix = spread(i + 1, start, step)
        for t in range(2):
            mask = tables[i + 1][11 + t : 12 + t] == 3.0
            for b in range(3):
                value = halo[at_face(t, b, 0, RHS), :]
                value = value - fix[b * RHS : (b + 1) * RHS, t * LANES : (t + 1) * LANES]
                out[at_face(t, b, 0, RHS), :] = jnp.where(mask, value, 0.0)
    for tx, ty in lines():
        n = tx * 2 + ty

        def body(rows, tx=tx, ty=ty, n=n):
            acc = [x_even_ref[n, b, pl.ds(rows, ROWS), :] for b in range(3)]
            acc = add_local(
                acc, coef_ref, 0, tx, ty,
                lambda i, j, a: three_ref[i * 2 + j, a, pl.ds(rows, ROWS), :],
            )
            acc = add_remote(acc, coef_ref, 0, tx, ty, *from_halos((hya, hyb, hxb, hxa), rows))
            mask = colors_ref[n : n + 1, :] == 2
            for b in range(3):
                u_ref[n, b, pl.ds(rows, ROWS), :] = acc[b]
                store_faces((sya, syb, sxb, sxa), tx, ty, b, rows, jnp.where(mask, acc[b], 0.0))

        chunks(body)


def last_kernel(
    part_ref, u_ref, odd_three, odd_v, coef_ref, colors_ref, rya, ryb, rxb, rxa, out_hbm, out_ref, sems
):
    steps = RHS // ROWS

    def out_copy(i, b):
        part = pl.ds((b * RHS + i * ROWS) * SLICE, ROWS * SLICE)
        return pltpu.make_async_copy(out_ref.at[part], out_hbm.at[part], sems.at[i * 3 + b])

    def step(i, carry):
        rows = pl.multiple_of(i * ROWS, ROWS)
        part = pl.ds(rows, ROWS)
        for tx, ty in lines():
            n = tx * 2 + ty
            x, y = line_xy(tx, ty)
            flip = xor(x, y)
            acc = [part_ref[n, b, part, :] for b in range(3)]
            acc = add_remote(acc, coef_ref, 0, tx, ty, *from_halos((rya, ryb, rxb, rxa), rows))
            is_two = colors_ref[n : n + 1, :] == 2
            is_one = colors_ref[4 + n : 5 + n, :] == 1
            for b in range(3):
                even = jnp.where(is_two, u_ref[n, b, part, :], acc[b])
                odd = jnp.where(is_one, odd_v[n, b, part, :], odd_three[n, b, part, :])
                z_even = jnp.where(flip == 1, odd, even)
                z_odd = jnp.where(flip == 1, even, odd)
                for half in range(2):
                    start = (b * RHS + rows) * SLICE + x * 4 + half * 2 + y
                    out_ref[pl.ds(start, ROWS, stride=SLICE), :] = join_z(z_even, z_odd, half)
        for b in range(3):
            out_copy(i, b).start()
        return carry

    lax.fori_loop(0, steps, step, 0)
    for i in range(steps):
        for b in range(3):
            out_copy(i, b).wait()


def pairs(axis, second):
    count = lax.axis_size(axis)
    found = []
    for i in range(second, count, 2):
        found += [(i, (i + 1) % count), ((i + 1) % count, i)]
    return found


def swap(value, axis, mask):
    return lax.ppermute(value, axis, [(i, i ^ mask) for i in range(lax.axis_size(axis))])


def exchange(sya, syb, sxb, sxa):
    rya = lax.ppermute(sya, "col", pairs("col", 0))
    ryb = lax.ppermute(syb, "col", pairs("col", 1))
    rxb = lax.ppermute(sxb, "slab", pairs("slab", 1))
    rxa = lax.ppermute(sxa, "slab", pairs("slab", 0))
    return rya, ryb, rxb, rxa


def to_rows(array):
    lead = array.shape[:-3]
    split = array.reshape(lead + (2, 2, 2, LANES))
    return jnp.swapaxes(split, -3, -2).reshape(-1, LANES)


def from_rows(rows):
    split = rows.reshape(3, RHS, 2, 2, 2, LANES)
    return jnp.swapaxes(split, -3, -2).reshape(3, RHS, 2, 2, 2 * LANES)


def per_device(
    cell_rhs, well_rhs, cell_colors, incoming, pivot_inv,
    perf_cell, perf_well, perf_out, perf_in, well_pivot_inv,
):
    rhs = to_rows(cell_rhs)
    colors_in = to_rows(cell_colors)
    inc = to_rows(incoming)
    piv = to_rows(pivot_inv)
    place = perf_cell.reshape(1, PERFS)
    well = perf_well.reshape(1, PERFS)
    out_blocks = jnp.transpose(perf_out, (1, 2, 0))
    in_blocks = jnp.transpose(perf_in, (1, 2, 0))
    well_side = jnp.transpose(well_rhs, (1, 0, 2))
    tiles = pltpu.VMEM((17 * SLICE, LANES), jnp.float32)
    color_tile = pltpu.VMEM((9 * SLICE, LANES), jnp.int32)
    block_tiles = pltpu.VMEM((57 * SLICE, LANES), jnp.float32)
    piv_in = pltpu.VMEM((9 * SLICE, LANES), jnp.float32)
    color_in = pltpu.VMEM((SLICE, LANES), jnp.int32)
    whole = pltpu.VMEM((3 * RHS * SLICE, LANES), jnp.float32)
    steps = RHS // ROWS

    def local(cls, base, coef, s, name):
        def body(*refs):
            local_kernel(cls, *refs)

        return call(body, PLANES, (base, coef, *s[:2]), name=name)

    q_even, *s = call(
        first_kernel,
        [PLANES] + FACES,
        [pltpu.with_memory_space_constraint(v, pltpu.HBM) for v in (rhs, piv, colors_in)],
        [whole, piv_in, color_in, tiles, color_tile, pltpu.SemaphoreType.DMA((2 + 3 * steps,))],
        name="even_rhs",
        hbm=(0, 1, 2),
    )
    halo = exchange(*s)
    part, fwd, bwd, colors, well_piv = call(
        second_kernel,
        [PLANES, COEF, COEF, jax.ShapeDtypeStruct((8, LANES), jnp.int32), f32(8, LANES)],
        (rhs, piv, colors_in, inc, *s[:2], jnp.transpose(well_pivot_inv, (1, 0, 2))),
        [tiles, color_tile, block_tiles, block_tiles],
        name="blocks_and_local",
    )
    t_odd, *s, table = call(
        forward_one_kernel,
        [PLANES] + FACES_PLUS + [f32(EXTRA, LANES)],
        (part, fwd, colors, *halo, place, well, in_blocks),
        name="forward_one",
    )
    part = local(0, q_even, fwd, s, "forward_two_local")
    halo = exchange(*s)
    u_even, *s, tables = call(
        forward_two_kernel,
        [PLANES] + FACES + [f32(5, EXTRA, LANES)],
        (part, fwd, colors, *halo, table),
        name="forward_two",
    )
    part, even, at_even = call(
        forward_three_local_kernel,
        [PLANES, PLANES, f32(3 * RHS, PERFS)],
        (t_odd, fwd, *s[:2], q_even, u_even, colors, place),
        name="forward_three_local",
    )
    halo = exchange(*s)
    odd, keep, send = call(
        forward_three_kernel,
        [PLANES, f32(4 * BLOCK, 3 * LANES), f32(4 * BLOCK, 3 * LANES)],
        (part, t_odd, fwd, colors, *halo, place, well, out_blocks, well_side, at_even),
        [pltpu.VMEM((3 * RHS, PERFS), jnp.float32)],
        name="forward_three_wells",
    )
    narrow = [f32(BLOCK + (SLICE if m == 2 else 0), 3 * LANES) for m in range(4)]
    wide = [f32(BLOCK, WIDE), f32(BLOCK + SLICE, WIDE)]

    def swaps(near, far, axis, unit):
        return [swap(far if m == 2 else near, axis, unit * m) for m in (1, 2, 3)]

    *blocks, sya, syb = call(
        core_sum_kernel, narrow + [FACE_PLUS] * 2, (keep, swap(send, "slab", 1), odd), name="core_sum"
    )
    halo = [lax.ppermute(face, "col", pairs("col", i)) for i, face in enumerate((sya, syb))]
    moved = [swap(blocks[m], "slab", 8 * m) for m in (1, 2, 3)]
    mine, far = call(z_sum_kernel, wide, (blocks[0], *moved, well_piv), name="z_sum")
    mine, far, sxb, sxa = call(
        y_sum_kernel,
        wide + [FACE, FACE],
        (mine, *swaps(mine, far, "slab", 2), odd, *halo),
        name="y_sum",
        hbm=(5, 6),
    )
    halo.append(lax.ppermute(sxb, "slab", pairs("slab", 1)))
    halo.append(lax.ppermute(sxa, "slab", pairs("slab", 0)))
    mine, far, own_wells = call(
        solve_kernel,
        [narrow[0], narrow[2], f32(3, 2, RHS)],
        (mine, *swaps(mine, far, "col", 1)),
        name="solve_wells",
    )
    near = call(
        stack_kernel, f32(4 * BLOCK, 3 * LANES), (mine, *swaps(mine, far, "slab", 8)), name="stack"
    )
    far = swap(near, "slab", 1)
    u_even, x_odd, *s = call(
        backward_two_kernel,
        [PLANES, PLANES] + FACES,
        (near, far, even, odd, colors, bwd, *halo, tables),
        [pltpu.VMEM((5, 3 * RHS, 2 * LANES), jnp.bfloat16)]
        + [pltpu.VMEM(PLANES.shape, jnp.float32)] * 2
        + [pltpu.VMEM(FACE.shape, jnp.float32)] * 4,
        name="well_fix_backward_two",
    )
    part = local(1, x_odd, bwd, s, "backward_one_local")
    halo = exchange(*s)

    def backward_one(*refs):
        remote_kernel(1, 1, *refs)

    v_odd, *s = call(
        backward_one, [PLANES] + FACES, (part, bwd, colors, *halo), name="backward_one"
    )
    part = local(0, u_even, bwd, s, "backward_zero_local")
    halo = exchange(*s)
    rows = call(
        last_kernel,
        f32(3 * RHS * SLICE, LANES),
        (part, u_even, x_odd, v_odd, bwd, colors, *halo),
        [whole, pltpu.SemaphoreType.DMA((3 * steps,))],
        name="backward_zero",
        hbm_out=True,
    )
    return from_rows(rows), jnp.transpose(own_wells, (1, 0, 2))


def solution(mesh):
    placed = (
        P(None, None, "slab", "col", None),
        P(("slab", "col"), None, None),
        P("slab", "col", None),
        P(None, None, None, "slab", "col", None),
        P(None, None, "slab", "col", None),
        P(("slab", "col")),
        P(("slab", "col")),
        P(("slab", "col"), None, None),
        P(("slab", "col"), None, None),
        P(("slab", "col"), None, None),
    )
    return jax.shard_map(
        per_device,
        mesh=mesh,
        in_specs=placed,
        out_specs=(P(None, None, "slab", "col", None), P(("slab", "col"), None, None)),
        check_vma=False,
    )
```

```python
import jax
import jax.numpy as jnp
from jax import lax
from jax.experimental import pallas as pl
from jax.experimental.pallas import tpu as pltpu
from jax.sharding import PartitionSpec as P

RHS = 128
LANES = 128
ROWS = 64
SLICE = 8
FACE_RX, FACE_LX, FACE_RY, FACE_LY, FACE_ZU, FACE_ZS = range(6)
PERFS = 64
SENT = 6 * RHS
EXTRA = 16
WIDE = 4 * LANES
BLOCK = 32


def f32(*shape):
    return jax.ShapeDtypeStruct(shape, jnp.float32)


PLANES = f32(4, 3, RHS, LANES)
FACE = f32(SENT, LANES)
FACE_PLUS = f32(SENT + EXTRA, LANES)
PAST = (8, 16, 0, 0)
FACES = [f32(SENT + past, LANES) for past in PAST]
FACES_PLUS = [f32(SENT + EXTRA + past, LANES) for past in PAST]
COEF = f32(8, 54, LANES)


def call(body, outs, args, scratch=(), name=None, hbm=(), hbm_out=False):
    spaces = [pltpu.HBM if i in hbm else pltpu.VMEM for i in range(len(args))]
    out_space = pltpu.HBM if hbm_out else pltpu.VMEM
    return pl.pallas_call(
        body,
        out_shape=outs,
        in_specs=[pl.BlockSpec(memory_space=space) for space in spaces],
        out_specs=jax.tree.map(lambda _: pl.BlockSpec(memory_space=out_space), outs),
        scratch_shapes=list(scratch),
        compiler_params=pltpu.CompilerParams(vmem_limit_bytes=16 * 1024 * 1024),
        cost_estimate=pl.CostEstimate(flops=1_000_000, bytes_accessed=2_000_000, transcendentals=0),
        name=name,
    )(*args)


def spots():
    return lax.rem(lax.axis_index("slab"), 2), lax.rem(lax.axis_index("col"), 2)


def line_xy(tx, ty):
    sp, cp = spots()
    x = sp if tx else 1 - sp
    y = cp if ty else 1 - cp
    return x, y


def xor(a, b):
    return a + b - 2 * a * b


def lane_iota(rows):
    return lax.broadcasted_iota(jnp.int32, (rows, LANES), 1)


def pick(values, index):
    return jnp.take_along_axis(values, index, axis=1)


def split_z(low, high, odd):
    lane = lane_iota(low.shape[0])
    index = (2 * lane + odd) & (LANES - 1)
    return jnp.where(lane < LANES // 2, pick(low, index), pick(high, index))


def line_rows(ref, start, count):
    return ref[pl.ds(start, count, stride=SLICE), :]


def tile_split(tile):
    lane = lane_iota(SLICE)
    part = (lax.broadcasted_iota(jnp.int32, (SLICE, LANES), 0) >> 1) & 1
    even = pick(tile, (2 * lane) & (LANES - 1))
    odd = pick(tile, (2 * lane + 1) & (LANES - 1))
    low = lane < LANES // 2
    of_even = jnp.where(low, even, pltpu.roll(even, SLICE - 2, 0))
    of_odd = jnp.where(low, pltpu.roll(odd, 2, 0), odd)
    return jnp.where(part == 0, of_even, of_odd)


def split_tiles(source, target, count):
    for row in range(count):
        target[row * 8 : row * 8 + 8, :] = tile_split(source[row * 8 : row * 8 + 8, :])


def pivoted(rhs_ref, piv, cls, tx, ty, rows):
    x, y = line_xy(tx, ty)
    odd = xor(xor(x, y), cls)
    planes = []
    for a in range(3):
        base = (a * RHS + rows) * SLICE + x * 4 + y
        planes.append(
            split_z(line_rows(rhs_ref, base, ROWS), line_rows(rhs_ref, base + 2, ROWS), odd)
        )
    return [
        piv[0 * 3 + b] * planes[0] + piv[1 * 3 + b] * planes[1] + piv[2 * 3 + b] * planes[2]
        for b in range(3)
    ]


def class_rows(ref, cls, tx, ty, count):
    x, y = line_xy(tx, ty)
    odd = xor(xor(x, y), cls)
    return ref[pl.ds(x * 4 + odd * 2 + y, count, stride=SLICE), :]


def chunks(body):
    def step(i, carry):
        body(pl.multiple_of(i * ROWS, ROWS))
        return carry

    lax.fori_loop(0, RHS // ROWS, step, 0)


def lines():
    return [(tx, ty) for tx in range(2) for ty in range(2)]


def at_face(t, b, rows, count=ROWS):
    return pl.ds((t * 3 + b) * RHS + rows, count)


def from_sy(sya, syb, rows):
    return lambda tx, ty, a: (syb if ty else sya)[at_face(tx, a, rows), :]


def from_halos(halos, rows):
    rya, ryb, rxb, rxa = halos
    return (
        lambda tx, ty, a: (rxb if tx else rxa)[at_face(ty, a, rows), :],
        lambda tx, ty, a: (ryb if ty else rya)[at_face(tx, a, rows), :],
    )


def take(acc, coef, d, face, a, value):
    for b in range(3):
        row = face * 9 + a * 3 + b
        acc[b] = acc[b] - coef[d, row : row + 1, :] * value


def add_local(acc, coef, cls, tx, ty, get):
    x, y = line_xy(tx, ty)
    odd = xor(xor(x, y), cls)
    index = (lane_iota(ROWS) + (LANES - 1) + 2 * odd) & (LANES - 1)
    d = cls * 4 + tx * 2 + ty
    for a in range(3):
        center = get(tx, ty, a)
        take(acc, coef, d, FACE_LX, a, get(1 - tx, ty, a))
        take(acc, coef, d, FACE_LY, a, get(tx, 1 - ty, a))
        take(acc, coef, d, FACE_ZU, a, center)
        take(acc, coef, d, FACE_ZS, a, pick(center, index))
    return acc


def add_remote(acc, coef, cls, tx, ty, get_x, get_y):
    d = cls * 4 + tx * 2 + ty
    for a in range(3):
        take(acc, coef, d, FACE_RX, a, get_x(tx, ty, a))
        take(acc, coef, d, FACE_RY, a, get_y(tx, ty, a))
    return acc


def store_faces(faces, tx, ty, b, rows, value):
    sya, syb, sxb, sxa = faces
    (syb if ty else sya)[at_face(tx, b, rows), :] = value
    (sxb if tx else sxa)[at_face(ty, b, rows), :] = value


def first_kernel(
    rhs_hbm, piv_hbm, colors_hbm, q_ref, sya, syb, sxb, sxa,
    rhs_ref, piv_ref, colors_ref, tiles, color_tile, sems,
):
    steps = RHS // ROWS

    def rhs_copy(i, a):
        part = pl.ds((a * RHS + i * ROWS) * SLICE, ROWS * SLICE)
        return pltpu.make_async_copy(rhs_hbm.at[part], rhs_ref.at[part], sems.at[2 + i * 3 + a])

    piv_copy = pltpu.make_async_copy(piv_hbm, piv_ref, sems.at[0])
    color_copy = pltpu.make_async_copy(colors_hbm, colors_ref, sems.at[1])
    piv_copy.start()
    color_copy.start()
    for i in range(steps):
        for a in range(3):
            rhs_copy(i, a).start()
    piv_copy.wait()
    split_tiles(piv_ref, tiles, 9)
    color_copy.wait()
    color_tile[0:SLICE, :] = tile_split(colors_ref[...])

    def step(i, carry):
        for a in range(3):
            rhs_copy(i, a).wait()
        rows = pl.multiple_of(i * ROWS, ROWS)
        for tx, ty in lines():
            piv_rows = class_rows(tiles, 0, tx, ty, 9)
            piv = [piv_rows[e : e + 1] for e in range(9)]
            mask = class_rows(color_tile, 0, tx, ty, 1) == 0
            for b, value in enumerate(pivoted(rhs_ref, piv, 0, tx, ty, rows)):
                q_ref[tx * 2 + ty, b, pl.ds(rows, ROWS), :] = value
                store_faces((sya, syb, sxb, sxa), tx, ty, b, rows, jnp.where(mask, value, 0.0))
        return carry

    lax.fori_loop(0, steps, step, 0)


def second_kernel(
    rhs_ref, piv_ref, colors_ref, inc_ref, sya, syb, well_piv_ref,
    part_ref, fwd_ref, bwd_ref, cls_colors_ref, well_rows_ref, tiles, color_tile, raw, folded,
):
    well_rows_ref[...] = jnp.zeros(well_rows_ref.shape, jnp.float32)
    for a in range(3):
        well_rows_ref[0:2, a * 3 : a * 3 + 3] = well_piv_ref[a]
    split_tiles(piv_ref, tiles, 9)
    color_tile[0:SLICE, :] = tile_split(colors_ref[...])
    spot = lax.broadcasted_iota(jnp.int32, (SLICE, LANES), 0)
    lane = lane_iota(SLICE)
    x_low = (spot >> 2) == 0
    y_low = (spot & 1) == 0
    z_even = ((spot >> 1) & 1) == 0
    edge = (z_even & (lane == 0)) | (jnp.logical_not(z_even) & (lane == LANES - 1))

    slab, col = lax.axis_index("slab"), lax.axis_index("col")
    inside = [
        jnp.where(low, jnp.where(at == 0, 0.0, 1.0), jnp.where(at == last, 0.0, 1.0))
        for low, at, last in (
            (x_low, slab, lax.axis_size("slab") - 1),
            (y_low, col, lax.axis_size("col") - 1),
        )
    ]

    def source(face, entry):
        row = (face * 9 + entry) * 8
        return tile_split(inc_ref[row : row + 8, :])

    piv = [tiles[i * 8 : i * 8 + 8, :] for i in range(9)]
    for group, (first, second, low) in enumerate(((0, 1, x_low), (2, 3, y_low), (5, 4, z_even))):
        one = [None] * 9
        two = [None] * 9
        for entry in range(9):
            p, q = source(first, entry), source(second, entry)
            one[entry] = jnp.where(low, p, q)
            two[entry] = jnp.where(low, q, p)
            if group < 2:
                one[entry] = one[entry] * inside[group]
            else:
                two[entry] = jnp.where(edge, 0.0, two[entry])
        for which, block in ((0, one), (1, two)):
            face = group * 2 + which
            for a in range(3):
                for b in range(3):
                    row = (face * 9 + a * 3 + b) * 8
                    raw[row : row + 8, :] = block[a * 3 + b]
                    folded[row : row + 8, :] = (
                        block[a * 3] * piv[b]
                        + block[a * 3 + 1] * piv[3 + b]
                        + block[a * 3 + 2] * piv[6 + b]
                    )
    for cls in range(2):
        for tx, ty in lines():
            d = cls * 4 + tx * 2 + ty
            fwd_ref[d] = class_rows(folded, cls, tx, ty, 54)
            bwd_ref[d] = class_rows(raw, cls, tx, ty, 54)
            cls_colors_ref[d : d + 1, :] = class_rows(color_tile, cls, tx, ty, 1)
    for tx, ty in lines():
        piv_rows = class_rows(tiles, 1, tx, ty, 9)
        piv1 = [piv_rows[i : i + 1] for i in range(9)]

        def body(rows, tx=tx, ty=ty, piv1=piv1):
            acc = pivoted(rhs_ref, piv1, 1, tx, ty, rows)
            acc = add_local(acc, fwd_ref, 1, tx, ty, from_sy(sya, syb, rows))
            for b in range(3):
                part_ref[tx * 2 + ty, b, pl.ds(rows, ROWS), :] = acc[b]

        chunks(body)


def local_kernel(cls, base_ref, coef_ref, sya, syb, part_ref):
    for tx, ty in lines():
        n = tx * 2 + ty

        def body(rows, tx=tx, ty=ty, n=n):
            acc = [base_ref[n, b, pl.ds(rows, ROWS), :] for b in range(3)]
            acc = add_local(acc, coef_ref, cls, tx, ty, from_sy(sya, syb, rows))
            for b in range(3):
                part_ref[n, b, pl.ds(rows, ROWS), :] = acc[b]

        chunks(body)


def remote_kernel(cls, color, part_ref, coef_ref, colors_ref, rya, ryb, rxb, rxa, full_ref, *faces):
    for tx, ty in lines():
        n = tx * 2 + ty
        d = cls * 4 + n

        def body(rows, tx=tx, ty=ty, n=n, d=d):
            acc = [part_ref[n, b, pl.ds(rows, ROWS), :] for b in range(3)]
            acc = add_remote(acc, coef_ref, cls, tx, ty, *from_halos((rya, ryb, rxb, rxa), rows))
            mask = colors_ref[d : d + 1, :] == color
            for b in range(3):
                full_ref[n, b, pl.ds(rows, ROWS), :] = acc[b]
                store_faces(faces, tx, ty, b, rows, jnp.where(mask, acc[b], 0.0))

        chunks(body)


def perf_place(perf_cell):
    sp, cp = spots()
    x = perf_cell >> 9
    y = (perf_cell >> 8) & 1
    z = perf_cell & 255
    cls = (x + y + z) & 1
    tx = (x + 1 - sp) & 1
    ty = (y + 1 - cp) & 1
    return (cls * 4 + tx * 2 + ty) * LANES + (z >> 1)


def forward_one_kernel(
    part_ref, coef_ref, colors_ref, rya, ryb, rxb, rxa, perf_cell_ref, perf_well_ref, perf_in_ref,
    full_ref, sya, syb, sxb, sxa, table_ref,
):
    faces = (sya, syb, sxb, sxa)
    table_ref[...] = jnp.zeros((EXTRA, LANES), jnp.float32)
    table_ref[0:1, 0:PERFS] = perf_place(perf_cell_ref[...]).astype(jnp.float32)
    table_ref[1:2, 0:PERFS] = perf_well_ref[...].astype(jnp.float32)
    for a in range(3):
        table_ref[2 + a * 3 : 5 + a * 3, 0:PERFS] = perf_in_ref[a]
    remote_kernel(1, 1, part_ref, coef_ref, colors_ref, rya, ryb, rxb, rxa, full_ref, *faces)
    for target, start, step in ((sya, 4, 2), (syb, 5, 2), (sxb, 6, 1), (sxa, 4, 1)):
        target[SENT : SENT + EXTRA, :] = table_ref[...]
        if target.shape[0] > SENT + EXTRA:
            target[SENT + EXTRA :, :] = jnp.zeros((target.shape[0] - SENT - EXTRA, LANES), jnp.float32)
        for t in range(2):
            d = start + t * step
            row = SENT + 11 + t
            target[row : row + 1, :] = colors_ref[d : d + 1, :].astype(jnp.float32)


def forward_two_kernel(
    part_ref, coef_ref, colors_ref, rya, ryb, rxb, rxa, table_ref,
    full_ref, sya, syb, sxb, sxa, tables_ref,
):
    faces = (sya, syb, sxb, sxa)
    remote_kernel(0, 2, part_ref, coef_ref, colors_ref, rya, ryb, rxb, rxa, full_ref, *faces)
    tables_ref[0] = table_ref[...]
    for i, ref in enumerate((rya, ryb, rxb, rxa)):
        tables_ref[i + 1] = ref[SENT : SENT + EXTRA, :]


def hot(index, count, start=0, step=LANES):
    rows = lax.broadcasted_iota(jnp.int32, (count, index.shape[1]), 0)
    rows = start + (rows >> 7) * step + (rows & (LANES - 1))
    return jnp.where(rows == index, 1.0, 0.0).astype(jnp.bfloat16)


def halves(values):
    high = values.astype(jnp.bfloat16)
    return high, (values - high.astype(jnp.float32)).astype(jnp.bfloat16)


def dot_ones(parts, ones, dims):
    return sum(
        lax.dot_general(part, ones, (dims, ((), ())), preferred_element_type=jnp.float32)
        for part in parts
    )


def well_bits():
    slab = lax.axis_index("slab")
    return slab & 1, slab >> 3, (slab >> 1) & 3


def core_wells(shape, core):
    rows = lax.broadcasted_iota(jnp.int32, shape, 0)
    return (rows >> 3) * 16 + core * 8 + (rows & 7)


def own_row(j):
    return well_bits()[2] * 8 + lax.axis_index("col") * 2 + j


def planes_at_perfs(ref, cls, place):
    total = None
    for tx in range(2):
        planes = [ref[tx * 2 + ty].reshape(3 * RHS, LANES) for ty in range(2)]
        ones = hot(place, 2 * LANES, (cls * 4 + tx * 2) * LANES)
        term = dot_ones(halves(jnp.concatenate(planes, axis=1)), ones, ((1,), (0,)))
        total = term if total is None else total + term
    return total


def forward_three_local_kernel(
    base_ref, coef_ref, sya, syb, q_ref, u_ref, colors_ref, perf_cell_ref, part_ref, even_ref, at_ref
):
    local_kernel(1, base_ref, coef_ref, sya, syb, part_ref)
    for n in range(4):
        is_two = colors_ref[n : n + 1, :] == 2
        for b in range(3):
            even_ref[n, b] = jnp.where(is_two, u_ref[n, b], q_ref[n, b])
    at_ref[...] = planes_at_perfs(even_ref, 0, perf_place(perf_cell_ref[...]))


def forward_three_kernel(
    part_ref, t_ref, coef_ref, colors_ref, rya, ryb, rxb, rxa,
    perf_cell_ref, perf_well_ref, perf_out_ref, well_rhs_ref, at_even_ref,
    odd_ref, keep_ref, send_ref, at_ref,
):
    for tx, ty in lines():
        n = tx * 2 + ty
        d = 4 + n

        def body(rows, tx=tx, ty=ty, n=n, d=d):
            part = pl.ds(rows, ROWS)
            acc = [part_ref[n, b, part, :] for b in range(3)]
            acc = add_remote(acc, coef_ref, 1, tx, ty, *from_halos((rya, ryb, rxb, rxa), rows))
            is_one = colors_ref[d : d + 1, :] == 1
            for b in range(3):
                value = jnp.where(is_one, t_ref[n, b, part, :], acc[b])
                odd_ref[n, b, part, :] = value

        chunks(body)
    at_perfs = at_even_ref[...] + planes_at_perfs(odd_ref, 1, perf_place(perf_cell_ref[...]))
    for b in range(3):
        at_ref[b * RHS : (b + 1) * RHS, :] = sum(
            perf_out_ref[a, b : b + 1, :] * at_perfs[a * RHS : (a + 1) * RHS] for a in range(3)
        )
    core, _, _ = well_bits()
    device = lax.axis_index("slab") * lax.axis_size("col") + lax.axis_index("col")
    parts = halves(at_ref[...])
    count = keep_ref.shape[0]
    for ref, which in ((keep_ref, core), (send_ref, 1 - core)):
        wells = jnp.where(core_wells((count, PERFS), which) == perf_well_ref[...], 1.0, 0.0)
        total = sum(
            lax.dot_general(
                wells.astype(jnp.bfloat16), part, (((1,), (1,)), ((), ())),
                preferred_element_type=jnp.float32,
            )
            for part in parts
        )
        is_own = [core_wells((count, LANES), which) == device * 2 + j for j in range(2)]
        for b in range(3):
            own = sum(jnp.where(is_own[j], well_rhs_ref[b, j : j + 1, :], 0.0) for j in range(2))
            ref[:, b * LANES : (b + 1) * LANES] = own - total[:, b * LANES : (b + 1) * LANES]


def core_sum_kernel(keep_ref, got_ref, odd_ref, *outs):
    *outs, sya, syb = outs
    for tx, ty in lines():
        for e in range(3):
            (syb if ty else sya)[at_face(tx, e, 0, RHS), :] = odd_ref[tx * 2 + ty, e]
    for face in (sya, syb):
        face[SENT:, :] = jnp.zeros((EXTRA, LANES), jnp.float32)
    _, z_spot, _ = well_bits()
    count = outs[0].shape[0]
    for m, out in enumerate(outs):
        rows = pl.ds(pl.multiple_of((z_spot ^ m) * count, count), count)
        out[0:count, :] = keep_ref[rows, :] + got_ref[rows, :]
        if out.shape[0] > count:
            out[count:, :] = jnp.zeros((out.shape[0] - count, out.shape[1]), jnp.float32)


def sum_of(refs):
    a, b, c, d = (ref[0:BLOCK, :] for ref in refs)
    return (a + b) + (c + d)


def store_all(value, outs, lanes=slice(None)):
    for out in outs:
        out[0:BLOCK, lanes] = value
        if out.shape[0] > BLOCK:
            out[BLOCK:, lanes] = jnp.zeros((out.shape[0] - BLOCK, value.shape[1]), jnp.float32)


def z_sum_kernel(a, b, c, d, well_piv_ref, *outs):
    store_all(sum_of((a, b, c, d)), outs, slice(0, 3 * LANES))
    rows = lax.broadcasted_iota(jnp.int32, (BLOCK, LANES), 0)
    blocks = sum(jnp.where(rows == own_row(j), well_piv_ref[j : j + 1, :], 0.0) for j in range(2))
    store_all(blocks, outs, slice(3 * LANES, WIDE))


def y_sum_kernel(a, b, c, d, odd_ref, rya, ryb, out_ref, mid_ref, far_ref, sxb, sxa):
    store_all(sum_of((a, b, c, d)), (out_ref, mid_ref, far_ref))
    for tx, ty in lines():
        for e in range(3):
            (sxb if tx else sxa)[at_face(ty, e, 0, RHS), :] = odd_ref[tx * 2 + ty, e]


def stack_kernel(*refs):
    for i, ref in enumerate(refs[:4]):
        refs[-1][i * BLOCK : (i + 1) * BLOCK, :] = ref[0:BLOCK, :]


def solve_kernel(a, b, c, d, out_ref, mid_ref, far_ref, own_ref):
    total = sum_of((a, b, c, d))
    rows = lax.broadcasted_iota(jnp.int32, (BLOCK, LANES), 0)
    for e in range(3):
        lanes = slice(e * LANES, (e + 1) * LANES)
        value = sum(
            total[:, 3 * LANES + i * 3 + e : 3 * LANES + i * 3 + e + 1]
            * total[:, i * LANES : (i + 1) * LANES]
            for i in range(3)
        )
        store_all(value, (out_ref, mid_ref, far_ref), lanes)
        for j in range(2):
            found = jnp.where(rows == own_row(j), value, 0.0)
            own_ref[e, j : j + 1, :] = jnp.sum(found, axis=0, keepdims=True)


def backward_two_kernel(
    wells_ref, other_ref, even_ref, odd_ref, colors_ref, coef_ref, rya, ryb, rxb, rxa, tables_ref,
    u_ref, x_odd_ref, sya, syb, sxb, sxa, fix_ref, x_even_ref, three_ref, hya, hyb, hxb, hxa,
):
    core, z_spot, _ = well_bits()

    def place_of_well(well):
        return (
            ((((well >> 3) & 1) ^ core) << 7)
            | ((((well >> 6) & 3) ^ z_spot) << 5)
            | (((well >> 4) & 3) << 3)
            | (well & 7)
        )

    wells = halves(jnp.concatenate([wells_ref[...].T, other_ref[...].T], axis=1))
    tables = [tables_ref[i] for i in range(5)]
    for first in (0, 2, 4):
        pair = tables[first : first + 2]
        well = jnp.concatenate([table[1:2] for table in pair], axis=1).astype(jnp.int32)
        at_perfs = dot_ones(wells, hot(place_of_well(well), 2 * LANES), ((1,), (0,)))
        for i, table in enumerate(pair):
            for b in range(3):
                fix = sum(
                    table[2 + a * 3 + b : 3 + a * 3 + b]
                    * at_perfs[a * RHS : (a + 1) * RHS, i * LANES : (i + 1) * LANES]
                    for a in range(3)
                )
                for part, value in enumerate(halves(fix)):
                    lanes = slice(part * LANES, (part + 1) * LANES)
                    fix_ref[first + i, b * RHS : (b + 1) * RHS, lanes] = value

    def spread(group, start, step):
        place = tables[group][0:1].astype(jnp.int32)
        ones = hot(place, 2 * LANES, start * LANES, step * LANES)
        return lax.dot_general(
            fix_ref[group], jnp.concatenate([ones, ones], axis=1),
            (((1,), (1,)), ((), ())), preferred_element_type=jnp.float32,
        )

    for cls, ref, out in ((1, odd_ref, x_odd_ref), (0, even_ref, x_even_ref)):
        for tx in range(2):
            fix = spread(0, cls * 4 + tx * 2, 1)
            for ty in range(2):
                n = tx * 2 + ty
                d = cls * 4 + n
                for b in range(3):
                    value = ref[n, b] - fix[b * RHS : (b + 1) * RHS, ty * LANES : (ty + 1) * LANES]
                    out[n, b] = value
                    if cls == 1:
                        three_ref[n, b] = jnp.where(colors_ref[d : d + 1, :] == 3, value, 0.0)
    for i, (halo, out, start, step) in enumerate(
        ((rya, hya, 4, 2), (ryb, hyb, 5, 2), (rxb, hxb, 6, 1), (rxa, hxa, 4, 1))
    ):
        fix = spread(i + 1, start, step)
        for t in range(2):
            mask = tables[i + 1][11 + t : 12 + t] == 3.0
            for b in range(3):
                value = halo[at_face(t, b, 0, RHS), :]
                value = value - fix[b * RHS : (b + 1) * RHS, t * LANES : (t + 1) * LANES]
                out[at_face(t, b, 0, RHS), :] = jnp.where(mask, value, 0.0)
    for tx, ty in lines():
        n = tx * 2 + ty

        def body(rows, tx=tx, ty=ty, n=n):
            acc = [x_even_ref[n, b, pl.ds(rows, ROWS), :] for b in range(3)]
            acc = add_local(
                acc, coef_ref, 0, tx, ty,
                lambda i, j, a: three_ref[i * 2 + j, a, pl.ds(rows, ROWS), :],
            )
            acc = add_remote(acc, coef_ref, 0, tx, ty, *from_halos((hya, hyb, hxb, hxa), rows))
            mask = colors_ref[n : n + 1, :] == 2
            for b in range(3):
                u_ref[n, b, pl.ds(rows, ROWS), :] = acc[b]
                store_faces((sya, syb, sxb, sxa), tx, ty, b, rows, jnp.where(mask, acc[b], 0.0))

        chunks(body)


def backward_zero_local_kernel(
    base_ref, coef_ref, sya, syb, odd_three, odd_v, colors_ref, part_ref, ahead_ref
):
    local_kernel(0, base_ref, coef_ref, sya, syb, part_ref)
    lane = lane_iota(ROWS)

    def step(i, carry):
        rows = pl.multiple_of(i * ROWS, ROWS)
        part = pl.ds(rows, ROWS)
        for tx, ty in lines():
            n = tx * 2 + ty
            is_one = colors_ref[4 + n : 5 + n, :] == 1
            for b in range(3):
                odd = jnp.where(is_one, odd_v[n, b, part, :], odd_three[n, b, part, :])
                for half in range(2):
                    ahead_ref[n * 2 + half, b, part, :] = pick(odd, half * (LANES // 2) + (lane >> 1))
        return carry

    lax.fori_loop(0, RHS // ROWS, step, 0)


def last_kernel(
    part_ref, u_ref, ahead_ref, coef_ref, colors_ref, rya, ryb, rxb, rxa, out_hbm, out_ref, sems
):
    steps = RHS // ROWS

    def out_copy(i, b):
        part = pl.ds((b * RHS + i * ROWS) * SLICE, ROWS * SLICE)
        return pltpu.make_async_copy(out_ref.at[part], out_hbm.at[part], sems.at[i * 3 + b])

    def step(i, carry):
        rows = pl.multiple_of(i * ROWS, ROWS)
        part = pl.ds(rows, ROWS)
        for tx, ty in lines():
            n = tx * 2 + ty
            x, y = line_xy(tx, ty)
            even_odd = xor(x, y)
            lane = lane_iota(ROWS)
            is_even = (lane & 1) == even_odd
            acc = [part_ref[n, b, part, :] for b in range(3)]
            acc = add_remote(acc, coef_ref, 0, tx, ty, *from_halos((rya, ryb, rxb, rxa), rows))
            is_two = colors_ref[n : n + 1, :] == 2
            for b in range(3):
                even = jnp.where(is_two, u_ref[n, b, part, :], acc[b])
                for half in range(2):
                    start = (b * RHS + rows) * SLICE + x * 4 + half * 2 + y
                    out_ref[pl.ds(start, ROWS, stride=SLICE), :] = jnp.where(
                        is_even,
                        pick(even, half * (LANES // 2) + (lane >> 1)),
                        ahead_ref[n * 2 + half, b, part, :],
                    )
        for b in range(3):
            out_copy(i, b).start()
        return carry

    lax.fori_loop(0, steps, step, 0)
    for i in range(steps):
        for b in range(3):
            out_copy(i, b).wait()


def pairs(axis, second):
    count = lax.axis_size(axis)
    found = []
    for i in range(second, count, 2):
        found += [(i, (i + 1) % count), ((i + 1) % count, i)]
    return found


def swap(value, axis, mask):
    return lax.ppermute(value, axis, [(i, i ^ mask) for i in range(lax.axis_size(axis))])


def exchange(sya, syb, sxb, sxa):
    rya = lax.ppermute(sya, "col", pairs("col", 0))
    ryb = lax.ppermute(syb, "col", pairs("col", 1))
    rxb = lax.ppermute(sxb, "slab", pairs("slab", 1))
    rxa = lax.ppermute(sxa, "slab", pairs("slab", 0))
    return rya, ryb, rxb, rxa


def to_rows(array):
    lead = array.shape[:-3]
    split = array.reshape(lead + (2, 2, 2, LANES))
    return jnp.swapaxes(split, -3, -2).reshape(-1, LANES)


def from_rows(rows):
    split = rows.reshape(3, RHS, 2, 2, 2, LANES)
    return jnp.swapaxes(split, -3, -2).reshape(3, RHS, 2, 2, 2 * LANES)


def per_device(
    cell_rhs, well_rhs, cell_colors, incoming, pivot_inv,
    perf_cell, perf_well, perf_out, perf_in, well_pivot_inv,
):
    rhs = to_rows(cell_rhs)
    colors_in = to_rows(cell_colors)
    inc = to_rows(incoming)
    piv = to_rows(pivot_inv)
    place = perf_cell.reshape(1, PERFS)
    well = perf_well.reshape(1, PERFS)
    out_blocks = jnp.transpose(perf_out, (1, 2, 0))
    in_blocks = jnp.transpose(perf_in, (1, 2, 0))
    well_side = jnp.transpose(well_rhs, (1, 0, 2))
    tiles = pltpu.VMEM((17 * SLICE, LANES), jnp.float32)
    color_tile = pltpu.VMEM((9 * SLICE, LANES), jnp.int32)
    block_tiles = pltpu.VMEM((57 * SLICE, LANES), jnp.float32)
    piv_in = pltpu.VMEM((9 * SLICE, LANES), jnp.float32)
    color_in = pltpu.VMEM((SLICE, LANES), jnp.int32)
    whole = pltpu.VMEM((3 * RHS * SLICE, LANES), jnp.float32)
    steps = RHS // ROWS

    def local(cls, base, coef, s, name):
        def body(*refs):
            local_kernel(cls, *refs)

        return call(body, PLANES, (base, coef, *s[:2]), name=name)

    q_even, *s = call(
        first_kernel,
        [PLANES] + FACES,
        [pltpu.with_memory_space_constraint(v, pltpu.HBM) for v in (rhs, piv, colors_in)],
        [whole, piv_in, color_in, tiles, color_tile, pltpu.SemaphoreType.DMA((2 + 3 * steps,))],
        name="even_rhs",
        hbm=(0, 1, 2),
    )
    halo = exchange(*s)
    part, fwd, bwd, colors, well_piv = call(
        second_kernel,
        [PLANES, COEF, COEF, jax.ShapeDtypeStruct((8, LANES), jnp.int32), f32(8, LANES)],
        (rhs, piv, colors_in, inc, *s[:2], jnp.transpose(well_pivot_inv, (1, 0, 2))),
        [tiles, color_tile, block_tiles, block_tiles],
        name="blocks_and_local",
    )
    t_odd, *s, table = call(
        forward_one_kernel,
        [PLANES] + FACES_PLUS + [f32(EXTRA, LANES)],
        (part, fwd, colors, *halo, place, well, in_blocks),
        name="forward_one",
    )
    part = local(0, q_even, fwd, s, "forward_two_local")
    halo = exchange(*s)
    u_even, *s, tables = call(
        forward_two_kernel,
        [PLANES] + FACES + [f32(5, EXTRA, LANES)],
        (part, fwd, colors, *halo, table),
        name="forward_two",
    )
    part, even, at_even = call(
        forward_three_local_kernel,
        [PLANES, PLANES, f32(3 * RHS, PERFS)],
        (t_odd, fwd, *s[:2], q_even, u_even, colors, place),
        name="forward_three_local",
    )
    halo = exchange(*s)
    odd, keep, send = call(
        forward_three_kernel,
        [PLANES, f32(4 * BLOCK, 3 * LANES), f32(4 * BLOCK, 3 * LANES)],
        (part, t_odd, fwd, colors, *halo, place, well, out_blocks, well_side, at_even),
        [pltpu.VMEM((3 * RHS, PERFS), jnp.float32)],
        name="forward_three_wells",
    )
    past = (0, 0, 2 * SLICE, SLICE)
    narrow = [f32(BLOCK + more, 3 * LANES) for more in past]
    wide = [f32(BLOCK + more, WIDE) for more in sorted(set(past))]

    def swaps(values, axis, unit):
        near, mid, far = values
        return [swap(value, axis, unit * m) for m, value in ((1, near), (2, far), (3, mid))]

    *blocks, sya, syb = call(
        core_sum_kernel, [narrow[m] for m in (0, 3, 2, 0)] + [FACE_PLUS] * 2, (keep, swap(send, "slab", 1), odd), name="core_sum"
    )
    halo = [lax.ppermute(face, "col", pairs("col", i)) for i, face in enumerate((sya, syb))]
    moved = [swap(blocks[m], "slab", 8 * m) for m in (1, 2, 3)]
    mine = call(z_sum_kernel, wide, (blocks[0], *moved, well_piv), name="z_sum")
    *mine, sxb, sxa = call(
        y_sum_kernel,
        wide + [FACE, FACE],
        (mine[0], *swaps(mine, "slab", 2), odd, *halo),
        name="y_sum",
        hbm=(5, 6),
    )
    halo.append(lax.ppermute(sxb, "slab", pairs("slab", 1)))
    halo.append(lax.ppermute(sxa, "slab", pairs("slab", 0)))
    *mine, own_wells = call(
        solve_kernel,
        [narrow[0], narrow[3], narrow[2], f32(3, 2, RHS)],
        (mine[0], *swaps(mine, "col", 1)),
        name="solve_wells",
    )
    near = call(
        stack_kernel, f32(4 * BLOCK, 3 * LANES), (mine[0], *swaps(mine, "slab", 8)), name="stack"
    )
    far = swap(near, "slab", 1)
    u_even, x_odd, *s = call(
        backward_two_kernel,
        [PLANES, PLANES] + FACES,
        (near, far, even, odd, colors, bwd, *halo, tables),
        [pltpu.VMEM((5, 3 * RHS, 2 * LANES), jnp.bfloat16)]
        + [pltpu.VMEM(PLANES.shape, jnp.float32)] * 2
        + [pltpu.VMEM(FACE.shape, jnp.float32)] * 4,
        name="well_fix_backward_two",
    )
    part = local(1, x_odd, bwd, s, "backward_one_local")
    halo = exchange(*s)

    def backward_one(*refs):
        remote_kernel(1, 1, *refs)

    v_odd, *s = call(
        backward_one, [PLANES] + FACES, (part, bwd, colors, *halo), name="backward_one"
    )
    part, ahead = call(
        backward_zero_local_kernel,
        [PLANES, f32(8, 3, RHS, LANES)],
        (u_even, bwd, *s[:2], x_odd, v_odd, colors),
        name="backward_zero_local",
    )
    halo = exchange(*s)
    rows = call(
        last_kernel,
        f32(3 * RHS * SLICE, LANES),
        (part, u_even, ahead, bwd, colors, *halo),
        [whole, pltpu.SemaphoreType.DMA((3 * steps,))],
        name="backward_zero",
        hbm_out=True,
    )
    return from_rows(rows), jnp.transpose(own_wells, (1, 0, 2))


def solution(mesh):
    placed = (
        P(None, None, "slab", "col", None),
        P(("slab", "col"), None, None),
        P("slab", "col", None),
        P(None, None, None, "slab", "col", None),
        P(None, None, "slab", "col", None),
        P(("slab", "col")),
        P(("slab", "col")),
        P(("slab", "col"), None, None),
        P(("slab", "col"), None, None),
        P(("slab", "col"), None, None),
    )
    return jax.shard_map(
        per_device,
        mesh=mesh,
        in_specs=placed,
        out_specs=(P(None, None, "slab", "col", None), P(("slab", "col"), None, None)),
        check_vma=False,
    )
```
